256 devices in a mesh: blk: 16 (over x_lo, z), dp: 16 (over x_hi, y, core).
Axes of the slice: x: 4 (x_hi: 2, x_lo: 2; x = x_hi * 2 + x_lo), y: 4, z: 8, core: 2. Of those that a mesh axis runs over, the one named last changes fastest.
Arguments:
- user_emb: bfloat16 [65536, 256], P(('blk', 'dp')), may hold values from -6 to 6
- pos_feat: bfloat16 [65536, 256], P(('blk', 'dp')), may hold values from -6 to 6
- pos_id: int32 [65536], P(('blk', 'dp')), may hold values from 0 to 4095
- neg_feat: bfloat16 [131072, 256], P(('blk', 'dp')), may hold values from -6 to 6
- neg_id: int32 [131072], P(('blk', 'dp')), may hold values from 0 to 4095
- neg_bucket: int32 [131072], P(('blk', 'dp')), may hold values from 0 to 1023
- logq_table: float32 [1024], replicated, may hold values from -4 to 0
- w_in: bfloat16 [256, 2048], replicated, may hold values from -0.375 to 0.375
- w_out: bfloat16 [2048, 256], replicated, may hold values from -0.125 to 0.125
Outputs:
- user_grad: float32 [65536, 256], P(('blk', 'dp'))
- w_in_grad: float32 [256, 2048], replicated
- w_out_grad: float32 [2048, 256], replicated
The draws below stay inside these ranges and needn't reach their ends.
All inputs are finite; a program needn't handle non-finite values.
Results may differ from the reference program's by a relative error of at most 0.008.
Values may be sent and summed in bfloat16 or wider, within the bound.
No kernel may reach another device: no remote copies, remote signals or barrier semaphores. Data moves between devices by JAX's collectives and lax.ppermute only.
A program may use at most 128 MiB of HBM per device.

```python
import math
import jax
import jax.numpy as jnp
from jax import lax

E = 256
F = 256
H = 2048
BUCKETS = 1024
CATALOG = 4096
U_DEV = 256
N_DEV = 512
USERS = 65536
NEGS = 131072
N_BLK = 16
N_DP = 16


def skewed_ids(key, count):
    first = jax.random.randint(jax.random.fold_in(key, 1), (count,), 0, CATALOG)
    second = jax.random.randint(jax.random.fold_in(key, 2), (count,), 0, CATALOG)
    ids = (first * second // CATALOG).astype(jnp.int32)
    where = jax.random.randint(jax.random.fold_in(key, 3), (), 0, count)
    ids = ids.at[where].set(jnp.int32(CATALOG - 1))
    ids = ids.at[(where + 1) % count].set(jnp.int32(0))
    return ids


def draw_pos_id(key, part):
    key = jax.random.fold_in(key, 11)
    return skewed_ids(key, USERS)


def draw_neg_id(key, part):
    key = jax.random.fold_in(key, 12)
    return skewed_ids(key, NEGS)


def place_ends(array, key, least, largest):
    index_at = [jax.random.randint(jax.random.fold_in(key, axis), (), 0, length) for axis, length in enumerate(array.shape)]
    main_axis = array.shape.index(max(array.shape))
    next_to = index_at[:main_axis] + [(index_at[main_axis] + 1) % array.shape[main_axis]] + index_at[main_axis + 1:]
    return array.at[tuple(index_at)].set(least).at[tuple(next_to)].set(largest)


def levels(stream_key, shape, split, least, high):
    def one(position, blocks):
        steps = jax.random.uniform(jax.random.fold_in(jax.random.fold_in(stream_key, 6), position), (blocks,), jnp.float32, least / len(split), high / len(split))
        return jnp.repeat(jnp.exp(steps), shape[position] // blocks).reshape((-1,) + (1,) * (len(shape) - position - 1))

    gain = one(*split[0])
    for cut in split[1:]:
        gain = gain * one(*cut)
    return gain


def bell_draw(key, shape, deviation, bound, shards=(), dtype=jnp.bfloat16):
    gain = levels(key, shape, shards, -0.22, 0.18) if shards else 1.0
    result = jax.random.normal(key, shape, jnp.float32) * deviation * gain
    return jnp.minimum(jnp.maximum(result, -bound), bound).astype(dtype)


def setup_inputs(seed: int = 0) -> dict:
    splits = jax.random.split(jax.random.key(seed), 10)
    return {
        "user_emb": bell_draw(splits[0], (USERS, E), 1.0, 6.0, ((0, 256),)),
        "pos_feat": bell_draw(splits[1], (USERS, F), 1.0, 6.0, ((0, 256),)),
        "pos_id": draw_pos_id(jax.random.fold_in(splits[9], 71), 0),
        "neg_feat": bell_draw(splits[3], (NEGS, F), 1.0, 6.0, ((0, 256),)),
        "neg_id": draw_neg_id(jax.random.fold_in(splits[9], 71), 0),
        "neg_bucket": place_ends(jax.random.randint(splits[5], (NEGS,), 0, BUCKETS), jax.random.fold_in(splits[5], 1), 0, BUCKETS - 1).astype(jnp.int32),
        "logq_table": jnp.clip(jax.random.uniform(splits[6], (BUCKETS,), jnp.float32, -4.0, 0.0), -4.0, 0.0),
        "w_in": bell_draw(splits[7], (F, H), F ** -0.5, 0.375),
        "w_out": bell_draw(splits[8], (H, E), H ** -0.5, 0.125),
    }


score_gain = 2.0

def tower(feat, w_in, w_out):
    hidden = jnp.maximum(jnp.dot(feat, w_in, preferred_element_type=jnp.float32), 0.0).astype(jnp.bfloat16)
    emb = jnp.dot(hidden, w_out, preferred_element_type=jnp.float32).astype(jnp.bfloat16)
    return (hidden, emb)

def tower_grads(feat, hidden, emb_grad, w_out):
    back = jnp.dot(emb_grad, w_out.T, preferred_element_type=jnp.float32)
    back = jnp.where(hidden > 0, back, 0.0).astype(jnp.bfloat16)
    return (jnp.dot(feat.T, back, preferred_element_type=jnp.float32), jnp.dot(hidden.T, emb_grad, preferred_element_type=jnp.float32))

def regroup(values, per):
    shaped = values.reshape((N_BLK, N_DP, per) + values.shape[1:])
    shaped = jnp.swapaxes(shaped, 0, 1)
    return shaped.reshape((N_DP, N_BLK * per) + values.shape[1:])

def ungroup(values, per):
    shaped = values.reshape((N_DP, N_BLK, per) + values.shape[2:])
    shaped = jnp.swapaxes(shaped, 0, 1)
    return shaped.reshape((N_BLK * N_DP * per,) + values.shape[2:])

def group_step(items):
    users, pos_ids, pos_embs, neg_embs, neg_ids, neg_bias = items
    scale = score_gain / math.sqrt(E)
    scores = scale * jnp.dot(users, neg_embs.T, preferred_element_type=jnp.float32) - neg_bias[None, :]
    kept = jnp.where(neg_ids[None, :] != pos_ids[:, None], jnp.exp(scores), jnp.float32(0.0))
    pos_score = scale * jnp.einsum('ue,ue->u', users.astype(jnp.float32), pos_embs.astype(jnp.float32))
    pos_exp = jnp.exp(pos_score)
    total = pos_exp + lax.optimization_barrier(jnp.sum(kept, axis=1))
    prob = (kept / total[:, None]).astype(jnp.bfloat16)
    pos_prob = pos_exp / total
    user_grad = scale * jnp.dot(prob, neg_embs, preferred_element_type=jnp.float32) + scale * (pos_prob - 1.0)[:, None] * pos_embs.astype(jnp.float32)
    neg_grad = (scale * jnp.dot(prob.T, users, preferred_element_type=jnp.float32)).astype(jnp.bfloat16)
    pos_grad = (scale * (pos_prob - 1.0)[:, None] * users.astype(jnp.float32)).astype(jnp.bfloat16)
    return (user_grad, neg_grad, pos_grad)

def reference(user_emb, pos_feat, pos_id, neg_feat, neg_id, neg_bucket, logq_table, w_in, w_out):
    neg_hidden, neg_emb = tower(neg_feat, w_in, w_out)
    pos_hidden, pos_emb = tower(pos_feat, w_in, w_out)
    neg_bias = jnp.take(logq_table, neg_bucket)
    grouped = (regroup(user_emb, U_DEV), regroup(pos_id, U_DEV), regroup(pos_emb, U_DEV), regroup(neg_emb, N_DEV), regroup(neg_id, N_DEV), regroup(neg_bias, N_DEV))
    user_grad, neg_grad, pos_grad = lax.map(group_step, grouped)
    user_grad = ungroup(user_grad, U_DEV)
    neg_grad = ungroup(neg_grad, N_DEV)
    pos_grad = ungroup(pos_grad, U_DEV)
    neg_in, neg_out = tower_grads(neg_feat, neg_hidden, neg_grad, w_out)
    pos_in, pos_out = tower_grads(pos_feat, pos_hidden, pos_grad, w_out)
    return (user_grad, neg_in + pos_in, neg_out + pos_out)
```

```python
import jax
import jax.numpy as jnp
from jax import lax
from jax.experimental import pallas as pl
from jax.experimental.pallas import tpu as pltpu
from jax.sharding import Mesh, PartitionSpec as P

AXES = ("x_lo", "z", "x_hi", "y", "core")
SIZES = (2, 8, 2, 4, 2)
BF, F32, I32 = jnp.bfloat16, jnp.float32, jnp.int32
SCALE = 0.125
SMALL = 2.0**-64
E, H, U, N = 256, 2048, 256, 512
NN = 2 * N
ROWS = NN + U
TILE = 256
CHUNKS = H // TILE
NZ = 8
VMEM_LIMIT = 40 * 1024 * 1024

NT = (((1,), (1,)), ((), ()))


def params():
    return pltpu.CompilerParams(vmem_limit_bytes=VMEM_LIMIT)


def cost(flops, nbytes, trans=0):
    return pl.CostEstimate(flops=int(flops), bytes_accessed=int(nbytes), transcendentals=int(trans))


def whole(shape):
    return pl.BlockSpec(shape, lambda *_: (0,) * len(shape))


def mm(a, b):
    return jnp.dot(a, b, preferred_element_type=F32)


def tower_kernel(own_ref, far_ref, pos_ref, w_in_ref, w_out_ref, hid_ref, emb_ref, embt_ref, pemb_ref, featt_ref, feat, acc):
    j = pl.program_id(0)

    @pl.when(j == 0)
    def _():
        feat[0:N] = own_ref[...]
        feat[N:NN] = far_ref[0:N]
        feat[NN:ROWS] = pos_ref[...]
        acc[...] = jnp.zeros_like(acc)
        featt_ref[...] = feat[...].T

    for m in range(ROWS // TILE):
        rows = slice(m * TILE, (m + 1) * TILE)
        hid = jnp.maximum(mm(feat[rows], w_in_ref[...]), 0.0).astype(BF)
        hid_ref[0, rows] = hid
        acc[rows] += mm(hid, w_out_ref[...])

    @pl.when(j == CHUNKS - 1)
    def _():
        emb = acc[0:NN].astype(BF)
        emb_ref[...] = emb
        embt_ref[...] = emb.T
        pemb_ref[...] = acc[NN:ROWS].astype(BF)


def tower(own, far, pos, w_in, w_out):
    return pl.pallas_call(
        tower_kernel,
        grid=(CHUNKS,),
        in_specs=[
            whole((N, E)),
            whole(far.shape),
            whole((U, E)),
            pl.BlockSpec((E, TILE), lambda j: (0, j)),
            pl.BlockSpec((TILE, E), lambda j: (j, 0)),
        ],
        out_specs=[
            pl.BlockSpec((1, ROWS, TILE), lambda j: (j, 0, 0)),
            whole((NN, E)),
            whole((E, NN)),
            whole((U, E)),
            whole((E, ROWS)),
        ],
        out_shape=[
            jax.ShapeDtypeStruct((CHUNKS, ROWS, TILE), BF),
            jax.ShapeDtypeStruct((NN, E), BF),
            jax.ShapeDtypeStruct((E, NN), BF),
            jax.ShapeDtypeStruct((U, E), BF),
            jax.ShapeDtypeStruct((E, ROWS), BF),
        ],
        scratch_shapes=[pltpu.VMEM((ROWS, E), BF), pltpu.VMEM((ROWS, E), F32)],
        compiler_params=params(),
        cost_estimate=cost(4 * ROWS * E * H, 10e6),
        name="tower",
    )(own, far, pos, w_in, w_out)


def score_kernel(s_ref, emb_ref, nid_ref, bias_ref, pexp_ref, *rest):
    users = rest[:NZ]
    tloc_ref, tin_ref, kept_ref, idb, bb, kf, kb, sems = rest[NZ:]
    z = s_ref[0]
    idb[...] = jnp.broadcast_to(nid_ref[...], (NN, U))
    bb[...] = jnp.broadcast_to(bias_ref[...], (NN, U))
    copies = []
    for k in range(NZ):
        u = users[k][0:U]
        tail = users[k][U : U + 16].astype(F32)
        pid = tail[0:1] * 64.0 + tail[1:2]
        total = jnp.zeros((8, U), F32)
        for m in range(NN // TILE):
            rows = slice(m * TILE, (m + 1) * TILE)
            e = (emb_ref[rows].astype(F32) * SCALE).astype(BF)
            sc = lax.dot_general(e, u, NT, preferred_element_type=F32) - bb[rows]
            kept = jnp.where(idb[rows] != pid, jnp.exp(sc), 0.0)
            kf[rows] = kept
            total = total + jnp.sum(kept.reshape(TILE // 8, 8, U), axis=0)
        t = jnp.sum(total, axis=0, keepdims=True)
        shrink = jnp.where(t > 1.0, SMALL, 1.0)
        inv = jnp.where(t > 0.0, 1.0 / (t * shrink), 0.0)
        for m in range(NN // TILE):
            rows = slice(m * TILE, (m + 1) * TILE)
            kb[k, rows] = ((kf[rows] * shrink) * inv).astype(BF)
        row = pl.ds(jnp.bitwise_xor(z, k), 1)
        tloc_ref[row, :] = t
        tin_ref[row, :] = t + pexp_ref[...] if k == 0 else t
        copy = pltpu.make_async_copy(kb.at[k], kept_ref.at[k], sems.at[k])
        copy.start()
        copies.append(copy)
    for copy in copies:
        copy.wait()


def score(scalars, emb, nid, bias, pexp, users):
    vm = pl.BlockSpec(memory_space=pltpu.VMEM)
    return pl.pallas_call(
        score_kernel,
        in_specs=[pl.BlockSpec(memory_space=pltpu.SMEM)] + [vm] * (4 + NZ),
        out_specs=[vm, vm, pl.BlockSpec(memory_space=pl.ANY)],
        out_shape=[
            jax.ShapeDtypeStruct((NZ, U), F32),
            jax.ShapeDtypeStruct((NZ, U), F32),
            jax.ShapeDtypeStruct((NZ, NN, U), BF),
        ],
        scratch_shapes=[
            pltpu.VMEM((NN, U), F32),
            pltpu.VMEM((NN, U), F32),
            pltpu.VMEM((NN, U), F32),
            pltpu.VMEM((NZ, NN, U), BF),
            pltpu.SemaphoreType.DMA((NZ,)),
        ],
        compiler_params=params(),
        cost_estimate=cost(2 * NZ * U * NN * E, 6e6, NZ * U * NN),
        name="score",
    )(scalars, emb, nid, bias, pexp, *users)


def grad_kernel(s_ref, tot_ref, tloc_ref, pexp_ref, embt_ref, pemb_ref, kept_ref, *rest):
    users = rest[:NZ]
    ug_ref, g_ref, pterm_ref, kb, wu, ratio, rel, sems = rest[NZ:]
    z = s_ref[0]
    copies = []
    for k in range(NZ):
        copy = pltpu.make_async_copy(kept_ref.at[k], kb.at[:, pl.ds(k * U, U)], sems.at[k])
        copy.start()
        copies.append(copy)
    tot = tot_ref[...]
    shrink = jnp.where(tot > 1.0, SMALL, 1.0)
    ratio[...] = (tloc_ref[...] * shrink) * (1.0 / (tot * shrink))
    own = tot_ref[pl.ds(z, 1), :]
    shrink = jnp.where(own > 1.0, SMALL, 1.0)
    pprob = (pexp_ref[...] * shrink) * (1.0 / (own * shrink))
    rel[...] = jnp.zeros_like(rel)
    for k in range(NZ):
        rel[k : k + 1] = SCALE * ratio[pl.ds(jnp.bitwise_xor(z, k), 1), :]
    rel[NZ : NZ + 1] = SCALE * (pprob - 1.0)
    cols = rel[...].T
    for k in range(NZ):
        wu[k * U : (k + 1) * U] = (users[k][0:U].astype(F32) * cols[:, k : k + 1]).astype(BF)
    coef = cols[:, NZ : NZ + 1]
    g_ref[NN:ROWS] = (users[0][0:U].astype(F32) * coef).astype(BF)
    pterm_ref[...] = pemb_ref[...].astype(F32) * coef
    for k in range(NZ):
        copies[k].wait()
        ut = mm(embt_ref[...], kb[:, k * U : (k + 1) * U])
        ug_ref[jnp.bitwise_xor(z, k)] = (ut * rel[k : k + 1]).astype(BF)
    for m in range(NN // TILE):
        rows = slice(m * TILE, (m + 1) * TILE)
        g_ref[rows] = mm(kb[rows], wu[...]).astype(BF)


def grads(scalars, tot, tloc, pexp, embt, pemb, kept, users):
    vm = pl.BlockSpec(memory_space=pltpu.VMEM)
    return pl.pallas_call(
        grad_kernel,
        in_specs=[pl.BlockSpec(memory_space=pltpu.SMEM)] + [vm] * 5 + [pl.BlockSpec(memory_space=pl.ANY)] + [vm] * NZ,
        out_specs=[vm, vm, vm],
        out_shape=[
            jax.ShapeDtypeStruct((NZ, E, U), BF),
            jax.ShapeDtypeStruct((ROWS, E), BF),
            jax.ShapeDtypeStruct((U, E), F32),
        ],
        scratch_shapes=[
            pltpu.VMEM((NN, NZ * U), BF),
            pltpu.VMEM((NZ * U, E), BF),
            pltpu.VMEM((NZ, U), F32),
            pltpu.VMEM((128, U), F32),
            pltpu.SemaphoreType.DMA((NZ,)),
        ],
        compiler_params=params(),
        cost_estimate=cost(4 * NZ * U * NN * E, 8e6),
        name="grads",
    )(scalars, tot, tloc, pexp, embt, pemb, kept, *users)


def back_kernel(s_ref, g_ref, featt_ref, w_out_ref, hid_ref, mine_ref, theirs_ref, gt):
    @pl.when(pl.program_id(0) == 0)
    def _():
        gt[...] = g_ref[...].T

    first, second, core = s_ref[1], s_ref[2], s_ref[3]
    hid = hid_ref[0]
    back = lax.dot_general(g_ref[...], w_out_ref[...], NT, preferred_element_type=F32)
    back = jnp.where(hid > 0, back, 0.0).astype(BF)
    w_in = mm(featt_ref[...], back)
    w_out = mm(gt[...], hid).T
    mine = jnp.where(core == 0, w_in, w_out).astype(BF)
    theirs = jnp.where(core == 0, w_out, w_in).astype(BF)
    for half in range(2):
        rows = slice(half * 128, (half + 1) * 128)
        mine_ref[0, jnp.bitwise_xor(second & 1, half)] = mine[rows]
        theirs_ref[0, jnp.bitwise_xor(first & 1, half)] = theirs[rows]


def place(outer, inner):
    def index(j, s):
        return (jnp.bitwise_xor(j // 2, s[outer]), jnp.bitwise_xor(j % 2, s[inner] // 2), 0, 0)

    return pl.BlockSpec((1, 2, 128, TILE), index)


def backward(scalars, g, featt, w_out, hid):
    return pl.pallas_call(
        back_kernel,
        grid_spec=pltpu.PrefetchScalarGridSpec(
            num_scalar_prefetch=1,
            grid=(CHUNKS,),
            in_specs=[
                whole((ROWS, E)),
                whole((E, ROWS)),
                pl.BlockSpec((TILE, E), lambda j, s: (j, 0)),
                pl.BlockSpec((1, ROWS, TILE), lambda j, s: (j, 0, 0)),
            ],
            out_specs=[place(1, 2), place(2, 1)],
            scratch_shapes=[pltpu.VMEM((E, ROWS), BF)],
        ),
        out_shape=[jax.ShapeDtypeStruct((4, 4, 128, TILE), BF)] * 2,
        compiler_params=params(),
        cost_estimate=cost(6 * ROWS * E * H, 10e6),
        name="backward",
    )(scalars, g, featt, w_out, hid)


def finish_kernel(s_ref, mine_ref, other_ref, w_in_ref, w_out_ref):
    first, second, core = s_ref[1], s_ref[2], s_ref[3]
    for half in range(2):
        rows = slice(half * 128, (half + 1) * 128)
        mine = mine_ref[0, jnp.bitwise_xor(second & 1, half)].astype(F32)
        other = other_ref[0, jnp.bitwise_xor(first & 1, half)].astype(F32)
        w_in_ref[rows] = jnp.where(core == 0, mine, other)
        w_out_ref[rows] = jnp.where(core == 0, other, mine)


def finish(scalars, mine, other):
    return pl.pallas_call(
        finish_kernel,
        grid_spec=pltpu.PrefetchScalarGridSpec(
            num_scalar_prefetch=1,
            grid=(CHUNKS,),
            in_specs=[place(1, 2), place(2, 1)],
            out_specs=[
                pl.BlockSpec((E, TILE), lambda j, s: (0, j)),
                pl.BlockSpec((TILE, E), lambda j, s: (j, 0)),
            ],
        ),
        out_shape=[jax.ShapeDtypeStruct((E, H), F32), jax.ShapeDtypeStruct((H, E), F32)],
        compiler_params=params(),
        cost_estimate=cost(0, 6e6),
        name="finish",
    )(scalars, mine, other)


def swap(x, axis, k):
    return lax.ppermute(x, axis, [(i, i ^ k) for i in range(SIZES[AXES.index(axis)])])


def device(x_lo, z, x_hi, y, core):
    return (((x_lo * 8 + z) * 2 + x_hi) * 4 + y) * 2 + core


def plane_swap(x, k, x_core):
    pairs = []
    for z in range(8):
        for xx in range(4):
            for y in range(4):
                for core in range(2):
                    to_x, to_y = (xx ^ k, y) if core == x_core else (xx, y ^ k)
                    pairs.append(
                        (device(xx & 1, z, xx >> 1, y, core), device(to_x & 1, z, to_x >> 1, to_y, core))
                    )
    return lax.ppermute(x, AXES, pairs)


def add(*terms):
    return sum(t.astype(F32) for t in terms)


def all_reduce(mine, theirs):
    half = add(mine, swap(theirs, "core", 1)).astype(BF)
    quarter = add(half[0], *[plane_swap(half[k], k, 0) for k in (1, 2, 3)]).astype(BF)
    part = add(quarter[0], *[plane_swap(quarter[k], k, 1) for k in (1, 2, 3)])
    for k in (1, 2, 4):
        part = part + swap(part.astype(BF), "z", k).astype(F32)
    part = part.astype(BF)
    quarter = jnp.stack([part] + [plane_swap(part, k, 1) for k in (1, 2, 3)])
    half = jnp.stack([quarter] + [plane_swap(quarter, k, 0) for k in (1, 2, 3)])
    return half, swap(half, "core", 1)


def digits(ids, base):
    ids = ids.reshape(-1, 256)
    return [(ids // base).astype(BF), (ids % base).astype(BF)]


def on_device(user_emb, pos_feat, pos_id, neg_feat, neg_id, neg_bucket, logq_table, w_in, w_out):
    x_lo, z, x_hi, y, core = [lax.axis_index(a) for a in AXES]
    xx = x_hi * 2 + x_lo
    scalars = jnp.stack([z, jnp.where(core == 0, xx, y), jnp.where(core == 0, y, xx), core]).astype(I32)

    near = jnp.concatenate(
        [neg_feat] + digits(neg_id, 64) + digits(neg_bucket, 32) + [jnp.zeros((8, E), BF)], axis=0
    )
    far = swap(near, "x_lo", 1)
    mine = jnp.concatenate([user_emb] + digits(pos_id, 64) + [jnp.zeros((14, E), BF)], axis=0)
    users = [mine] + [swap(mine, "z", k) for k in range(1, NZ)]

    tail = far[N : N + 8].astype(F32)
    far_id = tail[0:2] * 64.0 + tail[2:4]
    far_bucket = (tail[4:6] * 32.0 + tail[6:8]).astype(I32)
    nid = jnp.concatenate([neg_id.astype(F32), far_id.reshape(-1)]).reshape(NN, 1)
    bucket = jnp.concatenate([neg_bucket, far_bucket.reshape(-1)])
    bias = jnp.take(logq_table, bucket).reshape(NN, 1)

    hid, emb, embt, pemb, featt = tower(neg_feat, far, pos_feat, w_in, w_out)
    pos_score = SCALE * jnp.sum(user_emb.astype(F32) * pemb.astype(F32), axis=1)
    pexp = jnp.exp(pos_score).reshape(1, U)

    tloc, tot, kept = score(scalars, emb, nid, bias, pexp, users)
    for k in (1, 2, 4):
        tot = tot + swap(tot, "z", k)
    ug, g, pterm = grads(scalars, tot, tloc, pexp, embt, pemb, kept, users)
    user_sum = lax.psum_scatter(ug, "z", scatter_dimension=0, tiled=False)
    mine_g, theirs_g = backward(scalars, g, featt, w_out, hid)
    half, other = all_reduce(mine_g, theirs_g)
    w_in_grad, w_out_grad = finish(scalars, half, other)
    user_grad = user_sum.astype(F32).T + pterm
    return user_grad, w_in_grad, w_out_grad


def solution(mesh):
    rows = P(AXES, None)
    ids = P(AXES)
    return jax.shard_map(
        on_device,
        mesh=Mesh(mesh.devices.reshape(SIZES), AXES),
        in_specs=(rows, rows, ids, rows, ids, ids, P(), P(), P()),
        out_specs=(rows, P(), P()),
        check_vma=False,
    )
```

```python
import jax
import jax.numpy as jnp
from jax import lax
from jax.experimental import pallas as pl
from jax.experimental.pallas import tpu as pltpu
from jax.sharding import Mesh, PartitionSpec as P

AXES = ("x_lo", "z", "x_hi", "y", "core")
SIZES = (2, 8, 2, 4, 2)
BF, F32, I32 = jnp.bfloat16, jnp.float32, jnp.int32
SCALE = 0.125
SMALL = 2.0**-64
E, H, U, N = 256, 2048, 256, 512
NN = 2 * N
ROWS = NN + U
TILE = 256
CHUNKS = H // TILE
NZ = 8
EARLY = 3
VMEM_LIMIT = 24 * 1024 * 1024

WIDE = 512
NT = (((1,), (1,)), ((), ()))
TN = (((0,), (0,)), ((), ()))


def params(limit=VMEM_LIMIT):
    return pltpu.CompilerParams(vmem_limit_bytes=limit)


def cost(flops, nbytes, trans=0):
    return pl.CostEstimate(flops=int(flops), bytes_accessed=int(nbytes), transcendentals=int(trans))


def whole(shape):
    return pl.BlockSpec(shape, lambda *_: (0,) * len(shape))


def mm(a, b):
    return jnp.dot(a, b, preferred_element_type=F32)


def pack_kernel(user_ref, pid_ref, feat_ref, nid_ref, bucket_ref, mine_ref, near_ref):
    row = lax.broadcasted_iota(I32, (16, E), 0)

    def tail(digits):
        out = jnp.zeros((16, E), F32)
        for i, digit in enumerate(digits):
            out = jnp.where(row == i, digit.astype(F32), out)
        return out.astype(BF)

    def digits(ids, bits):
        ids = [ids[:, i : i + 256] for i in range(0, ids.shape[1], 256)]
        return [i >> bits for i in ids] + [i & (2**bits - 1) for i in ids]

    mine_ref[0:U] = user_ref[...]
    mine_ref[U : U + 16] = tail(digits(pid_ref[...], 6))
    near_ref[0:N] = feat_ref[...]
    near_ref[N : N + 16] = tail(digits(nid_ref[...], 6) + digits(bucket_ref[...], 5))


def pack(user_emb, pos_id, neg_feat, neg_id, neg_bucket):
    vm = pl.BlockSpec(memory_space=pltpu.VMEM)
    return pl.pallas_call(
        pack_kernel,
        in_specs=[vm] * 5,
        out_specs=[vm] * 2,
        out_shape=[jax.ShapeDtypeStruct((U + 16, E), BF), jax.ShapeDtypeStruct((N + 16, E), BF)],
        compiler_params=params(60 * 1024 * 1024),
        cost_estimate=cost(0, 1e6),
        name="pack",
    )(user_emb, pos_id.reshape(1, U), neg_feat, neg_id.reshape(1, N), neg_bucket.reshape(1, N))


def tower_kernel(near_ref, far_ref, pos_ref, mine_ref, w_in_ref, w_out_ref, table_ref, early_ref, *outs):
    del early_ref
    hid_ref, emb_ref, pemb_ref, feat_ref, nid_ref, bias_ref, pexp_ref = outs
    sources = [(near_ref, 0), (near_ref, 256), (far_ref, 0), (far_ref, 256), (pos_ref, 0)]
    lane = lax.broadcasted_iota(I32, (TILE, 128), 1).astype(F32)
    for m, (ref, start) in enumerate(sources):
        rows = slice(m * TILE, (m + 1) * TILE)
        feat = ref[start : start + TILE]
        feat_ref[rows] = feat
        hid = jnp.maximum(mm(feat, w_in_ref[...]), 0.0).astype(BF)
        hid_ref[rows] = hid
        emb = mm(hid, w_out_ref[...]).astype(BF)
        if m < 4:
            emb_ref[rows] = emb
        else:
            pemb_ref[...] = emb
            prod = mine_ref[0:U].astype(F32) * emb.astype(F32)
            prod = (prod[:, 0:128] + prod[:, 128:256]).T
            pexp_ref[...] = jnp.exp(SCALE * jnp.sum(prod, axis=0, keepdims=True))
    for side, ref in enumerate((near_ref, far_ref)):
        tail = jnp.concatenate([ref[N : N + 16].astype(F32), jnp.zeros((112, E), F32)], axis=0).T
        for block in range(2):
            rows = slice((2 * side + block) * TILE, (2 * side + block + 1) * TILE)
            nid = tail[:, block : block + 1] * 64.0 + tail[:, block + 2 : block + 3]
            nid_ref[rows] = jnp.broadcast_to(nid, (TILE, 128))
            bucket = tail[:, block + 4 : block + 5] * 32.0 + tail[:, block + 6 : block + 7]
            found = jnp.zeros((TILE, 128), F32)
            for b in range(8):
                found = found + jnp.where(bucket == lane + 128.0 * b, table_ref[b : b + 1], 0.0)
            bias_ref[rows] = jnp.broadcast_to(jnp.sum(found, axis=1, keepdims=True), (TILE, 128))


def tower(near, far, pos, mine, w_in, w_out, table, early):
    vm = pl.BlockSpec(memory_space=pltpu.VMEM)
    return pl.pallas_call(
        tower_kernel,
        in_specs=[vm] * 7 + [pl.BlockSpec(memory_space=pl.ANY)],
        out_specs=[vm] * 7,
        out_shape=[
            jax.ShapeDtypeStruct((ROWS, H), BF),
            jax.ShapeDtypeStruct((NN, E), BF),
            jax.ShapeDtypeStruct((U, E), BF),
            jax.ShapeDtypeStruct((ROWS, E), BF),
            jax.ShapeDtypeStruct((NN, 128), F32),
            jax.ShapeDtypeStruct((NN, 128), F32),
            jax.ShapeDtypeStruct((1, U), F32),
        ],
        compiler_params=params(),
        cost_estimate=cost(4 * ROWS * E * H, 10e6),
        name="tower",
    )(near, far, pos, mine, w_in, w_out, table, early)


def twice(x):
    return jnp.concatenate([x, x], axis=1)


def score_kernel(s_ref, emb_ref, nid_ref, bias_ref, pexp_ref, *rest):
    users = rest[:NZ]
    tloc_ref, tin_ref, kept_ref, kf = rest[NZ:]
    z = s_ref[0]
    for k in range(NZ):
        u = (users[k][0:U].astype(F32) * SCALE).astype(BF)
        tail = users[k][U : U + 16].astype(F32)
        pid = tail[0:1] * 64.0 + tail[1:2]
        total = jnp.zeros((8, U), F32)
        for m in range(NN // TILE):
            rows = slice(m * TILE, (m + 1) * TILE)
            sc = lax.dot_general(emb_ref[rows], u, NT, preferred_element_type=F32) - twice(bias_ref[rows])
            kept = jnp.where(twice(nid_ref[rows]) != pid, jnp.exp(sc), 0.0)
            kf[rows] = kept
            total = total + jnp.sum(kept.reshape(TILE // 8, 8, U), axis=0)
        t = jnp.sum(total, axis=0, keepdims=True)
        shrink = jnp.where(t > 1.0, SMALL, 1.0)
        inv = jnp.where(t > 0.0, 1.0 / (t * shrink), 0.0)
        for m in range(NN // TILE):
            rows = slice(m * TILE, (m + 1) * TILE)
            kept_ref[rows, k * U : (k + 1) * U] = ((kf[rows] * shrink) * inv).astype(BF)
        row = pl.ds(jnp.bitwise_xor(z, k), 1)
        tloc_ref[row, :] = t
        tin_ref[row, :] = t + pexp_ref[...] if k == 0 else t


def score(scalars, emb, nid, bias, pexp, users):
    vm = pl.BlockSpec(memory_space=pltpu.VMEM)
    return pl.pallas_call(
        score_kernel,
        in_specs=[pl.BlockSpec(memory_space=pltpu.SMEM)] + [vm] * (4 + NZ),
        out_specs=[vm] * 3,
        out_shape=[
            jax.ShapeDtypeStruct((NZ, U), F32),
            jax.ShapeDtypeStruct((NZ, U), F32),
            jax.ShapeDtypeStruct((NN, NZ * U), BF),
        ],
        scratch_shapes=[pltpu.VMEM((NN, U), F32)],
        compiler_params=params(),
        cost_estimate=cost(2 * NZ * U * NN * E, 6e6, NZ * U * NN),
        name="score",
    )(scalars, emb, nid, bias, pexp, *users)


def grad_kernel(s_ref, tot_ref, tloc_ref, pexp_ref, emb_ref, pemb_ref, kept_ref, *rest):
    users = rest[:NZ]
    ug_ref, g_ref, pterm_ref, wu, ratio, rel = rest[NZ:]
    z = s_ref[0]
    tot = tot_ref[...]
    shrink = jnp.where(tot > 1.0, SMALL, 1.0)
    ratio[...] = (tloc_ref[...] * shrink) * (1.0 / (tot * shrink))
    own = tot_ref[pl.ds(z, 1), :]
    shrink = jnp.where(own > 1.0, SMALL, 1.0)
    pprob = (pexp_ref[...] * shrink) * (1.0 / (own * shrink))
    rel[...] = jnp.zeros_like(rel)
    for k in range(NZ):
        rel[k : k + 1] = SCALE * ratio[pl.ds(jnp.bitwise_xor(z, k), 1), :]
    rel[NZ : NZ + 1] = SCALE * (pprob - 1.0)
    cols = rel[...].T
    for k in range(NZ):
        wu[k * U : (k + 1) * U] = (users[k][0:U].astype(F32) * cols[:, k : k + 1]).astype(BF)
    coef = cols[:, NZ : NZ + 1]
    g_ref[NN:ROWS] = (users[0][0:U].astype(F32) * coef).astype(BF)
    pterm_ref[...] = pemb_ref[...].astype(F32) * coef
    for k in range(NZ):
        ug = lax.dot_general(kept_ref[:, k * U : (k + 1) * U], emb_ref[...], TN, preferred_element_type=F32)
        ug_ref[jnp.bitwise_xor(z, k)] = (ug * cols[:, k : k + 1]).astype(BF)
    for m in range(NN // TILE):
        rows = slice(m * TILE, (m + 1) * TILE)
        g_ref[rows] = mm(kept_ref[rows], wu[...]).astype(BF)


def grads(scalars, tot, tloc, pexp, emb, pemb, kept, users):
    vm = pl.BlockSpec(memory_space=pltpu.VMEM)
    return pl.pallas_call(
        grad_kernel,
        in_specs=[pl.BlockSpec(memory_space=pltpu.SMEM)] + [vm] * (6 + NZ),
        out_specs=[vm, vm, vm],
        out_shape=[
            jax.ShapeDtypeStruct((NZ, U, E), BF),
            jax.ShapeDtypeStruct((ROWS, E), BF),
            jax.ShapeDtypeStruct((U, E), F32),
        ],
        scratch_shapes=[
            pltpu.VMEM((NZ * U, E), BF),
            pltpu.VMEM((NZ, U), F32),
            pltpu.VMEM((128, U), F32),
        ],
        compiler_params=params(),
        cost_estimate=cost(4 * NZ * U * NN * E, 8e6),
        name="grads",
    )(scalars, tot, tloc, pexp, emb, pemb, kept, *users)


def back_kernel(s_ref, g_ref, feat_ref, w_out_ref, hid_ref, mine_ref, theirs_ref):
    first, second, core = s_ref[1], s_ref[2], s_ref[3]
    for c in range(H // WIDE):
        cols = slice(c * WIDE, (c + 1) * WIDE)
        hid = hid_ref[:, cols]
        back = lax.dot_general(g_ref[...], w_out_ref[cols], NT, preferred_element_type=F32)
        back = jnp.where(hid > 0, back, 0.0).astype(BF)
        w_in = lax.dot_general(feat_ref[...], back, TN, preferred_element_type=F32)
        w_out = lax.dot_general(hid, g_ref[...], TN, preferred_element_type=F32)
        to_mine, to_theirs = jnp.bitwise_xor(first, c), jnp.bitwise_xor(second, c)
        for t in range(WIDE // TILE):
            a, b = w_in[:, t * TILE : (t + 1) * TILE], w_out[t * TILE : (t + 1) * TILE]
            mine = jnp.where(core == 0, a, b).astype(BF)
            theirs = jnp.where(core == 0, b, a).astype(BF)
            for half in range(2):
                rows = slice(half * 128, (half + 1) * 128)
                mine_ref[to_mine, jnp.bitwise_xor(second, 2 * t + half)] = mine[rows]
                theirs_ref[to_theirs, jnp.bitwise_xor(first, 2 * t + half)] = theirs[rows]


def backward(scalars, g, feat, w_out, hid):
    vm = pl.BlockSpec(memory_space=pltpu.VMEM)
    return pl.pallas_call(
        back_kernel,
        in_specs=[pl.BlockSpec(memory_space=pltpu.SMEM)] + [vm] * 4,
        out_specs=[vm, vm],
        out_shape=[jax.ShapeDtypeStruct((4, 4, 128, TILE), BF)] * 2,
        compiler_params=params(),
        cost_estimate=cost(6 * ROWS * E * H, 10e6),
        name="backward",
    )(scalars, g, feat, w_out, hid)


def finish_kernel(s_ref, mine_ref, other_ref, w_in_ref, w_out_ref):
    first, second, core = s_ref[1], s_ref[2], s_ref[3]
    for t in range(2):
        for half in range(2):
            rows = slice(half * 128, (half + 1) * 128)
            mine = mine_ref[0, jnp.bitwise_xor(second, 2 * t + half)].astype(F32)
            other = other_ref[0, jnp.bitwise_xor(first, 2 * t + half)].astype(F32)
            w_in_ref[rows, t * TILE : (t + 1) * TILE] = jnp.where(core == 0, mine, other)
            start = t * TILE + half * 128
            w_out_ref[start : start + 128] = jnp.where(core == 0, other, mine)


def finish(scalars, mine, other):
    def place(outer):
        return pl.BlockSpec((1, 4, 128, TILE), lambda j, s: (jnp.bitwise_xor(j, s[outer]), 0, 0, 0))

    return pl.pallas_call(
        finish_kernel,
        grid_spec=pltpu.PrefetchScalarGridSpec(
            num_scalar_prefetch=1,
            grid=(4,),
            in_specs=[place(1), place(2)],
            out_specs=[
                pl.BlockSpec((E, 512), lambda j, s: (0, j)),
                pl.BlockSpec((512, E), lambda j, s: (j, 0)),
            ],
        ),
        out_shape=[jax.ShapeDtypeStruct((E, H), F32), jax.ShapeDtypeStruct((H, E), F32)],
        compiler_params=params(),
        cost_estimate=cost(0, 6e6),
        name="finish",
    )(scalars, mine, other)


def swap(x, axis, k):
    return lax.ppermute(x, axis, [(i, i ^ k) for i in range(SIZES[AXES.index(axis)])])


def device(x_lo, z, x_hi, y, core):
    return (((x_lo * 8 + z) * 2 + x_hi) * 4 + y) * 2 + core


def plane_swap(x, k, x_core):
    pairs = []
    for z in range(8):
        for xx in range(4):
            for y in range(4):
                for core in range(2):
                    to_x, to_y = (xx ^ k, y) if core == x_core else (xx, y ^ k)
                    pairs.append(
                        (device(xx & 1, z, xx >> 1, y, core), device(to_x & 1, z, to_x >> 1, to_y, core))
                    )
    return lax.ppermute(x, AXES, pairs)


def add(*terms):
    return sum(t.astype(F32) for t in terms)


def sum_over_z(x, rounds, dtype):
    for ks in rounds:
        sent = x.astype(dtype)
        terms = [t.astype(F32) for t in [sent] + [swap(sent, "z", k) for k in ks]]
        while len(terms) > 1:
            terms = [a + b for a, b in zip(terms[::2], terms[1::2])]
        x = terms[0]
    return x


def all_reduce(mine, theirs):
    half = add(mine, swap(theirs, "core", 1)).astype(BF)
    quarter = add(half[0], *[plane_swap(half[k], k, 0) for k in (1, 2, 3)]).astype(BF)
    part = add(quarter[0], *[plane_swap(quarter[k], k, 1) for k in (1, 2, 3)])
    part = sum_over_z(part, ((1,), (2, 4, 6)), BF).astype(BF)
    quarter = jnp.stack([part] + [plane_swap(part, k, 1) for k in (1, 2, 3)])
    half = jnp.stack([quarter] + [plane_swap(quarter, k, 0) for k in (1, 2, 3)])
    return half, swap(half, "core", 1)


def on_device(user_emb, pos_feat, pos_id, neg_feat, neg_id, neg_bucket, logq_table, w_in, w_out):
    x_lo, z, x_hi, y, core = [lax.axis_index(a) for a in AXES]
    xx = x_hi * 2 + x_lo
    scalars = jnp.stack([z, jnp.where(core == 0, xx, y), jnp.where(core == 0, y, xx), core]).astype(I32)

    mine, near = pack(user_emb, pos_id, neg_feat, neg_id, neg_bucket)
    far = swap(near, "x_lo", 1)
    users = [mine] + [swap(mine, "z", k) for k in range(1, NZ)]

    hid, emb, pemb, feat, nid, bias, pexp = tower(
        near, far, pos_feat, mine, w_in, w_out, logq_table.reshape(8, 128), users[EARLY]
    )
    tloc, tot, kept = score(scalars, emb, nid, bias, pexp, users)
    tot = sum_over_z(tot, ((1, 6, 7), (2,)), F32)
    ug, g, pterm = grads(scalars, tot, tloc, pexp, emb, pemb, kept, users)
    user_sum = lax.psum_scatter(ug, "z", scatter_dimension=0, tiled=False)
    mine_g, theirs_g = backward(scalars, g, feat, w_out, hid)
    half, other = all_reduce(mine_g, theirs_g)
    w_in_grad, w_out_grad = finish(scalars, half, other)
    user_grad = user_sum.astype(F32) + pterm
    return user_grad, w_in_grad, w_out_grad


def solution(mesh):
    rows = P(AXES, None)
    ids = P(AXES)
    return jax.shard_map(
        on_device,
        mesh=Mesh(mesh.devices.reshape(SIZES), AXES),
        in_specs=(rows, rows, ids, rows, ids, ids, P(), P(), P()),
        out_specs=(rows, P(), P()),
        check_vma=False,
    )
```

```python
import functools

import jax
import jax.numpy as jnp
from jax import lax
from jax.experimental import pallas as pl
from jax.experimental.pallas import tpu as pltpu
from jax.sharding import Mesh, PartitionSpec as P

AXES = ("x_lo", "z", "x_hi", "y", "core")
SIZES = (2, 8, 2, 4, 2)
BF, F32, I32 = jnp.bfloat16, jnp.float32, jnp.int32
SCALE = 0.125
SMALL = 2.0**-64
E, H, U, N = 256, 2048, 256, 512
NN = 2 * N
ROWS = NN + U
TILE = 256
CHUNKS = H // TILE
NZ = 8
OFFSETS = (0, -1, 1, -2, 2, -3, 3, 4)
FIRST = 5
VMEM_LIMIT = 24 * 1024 * 1024

WIDE = 512
NT = (((1,), (1,)), ((), ()))
TN = (((0,), (0,)), ((), ()))


def params(limit=VMEM_LIMIT):
    return pltpu.CompilerParams(vmem_limit_bytes=limit)


def cost(flops, nbytes, trans=0):
    return pl.CostEstimate(flops=int(flops), bytes_accessed=int(nbytes), transcendentals=int(trans))


def whole(shape):
    return pl.BlockSpec(shape, lambda *_: (0,) * len(shape))


def mm(a, b):
    return jnp.dot(a, b, preferred_element_type=F32)


def start(src, dst, sem):
    copy = pltpu.make_async_copy(src, dst, sem)
    copy.start()
    return copy


def pack_kernel(user_hbm, pid_hbm, feat_hbm, nid_hbm, bucket_hbm, mine_ref, near_ref, pid_ref, nid_ref, bucket_ref, sems):
    copies = [
        start(pid_hbm, pid_ref, sems.at[0]),
        start(nid_hbm, nid_ref, sems.at[1]),
        start(bucket_hbm, bucket_ref, sems.at[2]),
        start(user_hbm, mine_ref.at[0:U], sems.at[3]),
        start(feat_hbm, near_ref.at[0:N], sems.at[4]),
    ]
    row = lax.broadcasted_iota(I32, (16, E), 0)

    def tail(digits):
        out = jnp.zeros((16, E), F32)
        for i, digit in enumerate(digits):
            out = jnp.where(row == i, digit.astype(F32), out)
        return out.astype(BF)

    def digits(ids, bits):
        ids = [ids[:, i : i + 256] for i in range(0, ids.shape[1], 256)]
        return [i >> bits for i in ids] + [i & (2**bits - 1) for i in ids]

    for copy in copies[:3]:
        copy.wait()
    mine_ref[U : U + 16] = tail(digits(pid_ref[...], 6))
    near_ref[N : N + 16] = tail(digits(nid_ref[...], 6) + digits(bucket_ref[...], 5))
    for copy in copies[3:]:
        copy.wait()


def pack(user_emb, pos_id, neg_feat, neg_id, neg_bucket):
    vm = pl.BlockSpec(memory_space=pltpu.VMEM)
    return pl.pallas_call(
        pack_kernel,
        in_specs=[pl.BlockSpec(memory_space=pltpu.HBM)] * 5,
        out_specs=[vm] * 2,
        out_shape=[jax.ShapeDtypeStruct((U + 16, E), BF), jax.ShapeDtypeStruct((N + 16, E), BF)],
        scratch_shapes=[
            pltpu.VMEM((1, U), I32),
            pltpu.VMEM((1, N), I32),
            pltpu.VMEM((1, N), I32),
            pltpu.SemaphoreType.DMA((5,)),
        ],
        compiler_params=params(60 * 1024 * 1024),
        cost_estimate=cost(0, 1e6),
        name="pack",
    )(user_emb, pos_id.reshape(1, U), neg_feat, neg_id.reshape(1, N), neg_bucket.reshape(1, N))


def hidden(feat, w_in_ref):
    return jnp.maximum(mm(feat, w_in_ref[...]), 0.0).astype(BF)


def hidden_kernel(near_ref, pos_ref, w_in_ref, hid_ref):
    for m, feat in enumerate((near_ref[0:TILE], near_ref[TILE:N], pos_ref[...])):
        hid_ref[m * TILE : (m + 1) * TILE] = hidden(feat, w_in_ref)


def embed_kernel(hid_ref, w_out_ref, emb_ref, pemb_ref):
    for m, (ref, first) in enumerate([(emb_ref, 0), (emb_ref, TILE), (pemb_ref, 0)]):
        hid = hid_ref[m * TILE : (m + 1) * TILE]
        ref[first : first + TILE] = mm(hid, w_out_ref[...]).astype(BF)


def far_kernel(near_ref, far_ref, w_in_ref, w_out_ref, table_ref, hid_ref, emb_ref, nid_ref, bias_ref):
    lane = lax.broadcasted_iota(I32, (TILE, 128), 1).astype(F32)
    for side, ref in enumerate((near_ref, far_ref)):
        tail = jnp.concatenate([ref[N : N + 16].astype(F32), jnp.zeros((112, E), F32)], axis=0).T
        for block in range(2):
            rows = slice((2 * side + block) * TILE, (2 * side + block + 1) * TILE)
            nid = tail[:, block : block + 1] * 64.0 + tail[:, block + 2 : block + 3]
            nid_ref[rows] = jnp.broadcast_to(nid, (TILE, 128))
            bucket = tail[:, block + 4 : block + 5] * 32.0 + tail[:, block + 6 : block + 7]
            found = jnp.zeros((TILE, 128), F32)
            for b in range(8):
                found = found + jnp.where(bucket == lane + 128.0 * b, table_ref[b : b + 1], 0.0)
            bias_ref[rows] = jnp.broadcast_to(jnp.sum(found, axis=1, keepdims=True), (TILE, 128))
    for m in range(N // TILE):
        rows = slice(m * TILE, (m + 1) * TILE)
        hid = hidden(far_ref[rows], w_in_ref)
        hid_ref[rows] = hid
        emb_ref[rows] = mm(hid, w_out_ref[...]).astype(BF)


def in_vmem(kernel, name, flops, outs, *args):
    vm = pl.BlockSpec(memory_space=pltpu.VMEM)
    return pl.pallas_call(
        kernel,
        in_specs=[vm] * len(args),
        out_specs=[vm] * len(outs),
        out_shape=[jax.ShapeDtypeStruct(shape, dtype) for shape, dtype in outs],
        compiler_params=params(),
        cost_estimate=cost(flops, 4e6),
        name=name,
    )(*args)


def twice(x):
    return jnp.concatenate([x, x], axis=1)


def home(z, k):
    return (z + OFFSETS[k] + NZ) & (NZ - 1)


def score_kernel(ks, s_ref, near_emb, far_emb, nid_ref, bias_ref, pemb_ref, tloc_in, tin_in, *rest):
    users = rest[: len(ks)]
    tloc_ref, tin_ref, pexp_ref, kept_ref, kf = rest[len(ks) :]
    z = s_ref[0]
    tloc_ref[...] = tloc_in[...]
    tin_ref[...] = tin_in[...]
    if ks[0] == 0:
        prod = users[0][0:U].astype(F32) * pemb_ref[...].astype(F32)
        prod = (prod[:, 0:128] + prod[:, 128:256]).T
        pexp_ref[...] = jnp.exp(SCALE * jnp.sum(prod, axis=0, keepdims=True))
    else:
        pexp_ref[...] = jnp.zeros_like(pexp_ref)
    for i, k in enumerate(ks):
        u = (users[i][0:U].astype(F32) * SCALE).astype(BF)
        tail = users[i][U : U + 16].astype(F32)
        pid = tail[0:1] * 64.0 + tail[1:2]
        total = jnp.zeros((8, U), F32)
        for m in range(NN // TILE):
            rows = slice(m * TILE, (m + 1) * TILE)
            emb = near_emb[rows] if m < 2 else far_emb[(m - 2) * TILE : (m - 1) * TILE]
            sc = lax.dot_general(emb, u, NT, preferred_element_type=F32) - twice(bias_ref[rows])
            kept = jnp.where(twice(nid_ref[rows]) != pid, jnp.exp(sc), 0.0)
            kf[rows] = kept
            total = total + jnp.sum(kept.reshape(TILE // 8, 8, U), axis=0)
        t = jnp.sum(total, axis=0, keepdims=True)
        shrink = jnp.where(t > 1.0, SMALL, 1.0)
        inv = jnp.where(t > 0.0, 1.0 / (t * shrink), 0.0)
        for m in range(NN // TILE):
            rows = slice(m * TILE, (m + 1) * TILE)
            kept_ref[rows, i * U : (i + 1) * U] = ((kf[rows] * shrink) * inv).astype(BF)
        row = pl.ds(home(z, k), 1)
        tloc_ref[row, :] = t
        tin_ref[row, :] = t + pexp_ref[...] if k == 0 else t


def score(ks, scalars, near_emb, far_emb, nid, bias, pemb, tloc, tin, users):
    vm = pl.BlockSpec(memory_space=pltpu.VMEM)
    n = len(ks)
    return pl.pallas_call(
        functools.partial(score_kernel, ks),
        in_specs=[pl.BlockSpec(memory_space=pltpu.SMEM)] + [vm] * (7 + n),
        out_specs=[vm] * 4,
        out_shape=[
            jax.ShapeDtypeStruct((NZ, U), F32),
            jax.ShapeDtypeStruct((NZ, U), F32),
            jax.ShapeDtypeStruct((1, U), F32),
            jax.ShapeDtypeStruct((NN, n * U), BF),
        ],
        scratch_shapes=[pltpu.VMEM((NN, U), F32)],
        compiler_params=params(),
        cost_estimate=cost(2 * n * U * NN * E, 5e6, n * U * NN),
        name="score",
    )(scalars, near_emb, far_emb, nid, bias, pemb, tloc, tin, *[users[k] for k in ks])


def grad_kernel(s_ref, tot_ref, tloc_ref, pexp_ref, near_emb, far_emb, pemb_ref, kept_a, kept_b, *rest):
    users = rest[:NZ]
    ug_ref, g_ref, pterm_ref, wu, ratio, rel = rest[NZ:]
    z = s_ref[0]
    tot = tot_ref[...]
    shrink = jnp.where(tot > 1.0, SMALL, 1.0)
    ratio[...] = (tloc_ref[...] * shrink) * (1.0 / (tot * shrink))
    own = tot_ref[pl.ds(z, 1), :]
    shrink = jnp.where(own > 1.0, SMALL, 1.0)
    pprob = (pexp_ref[...] * shrink) * (1.0 / (own * shrink))
    rel[...] = jnp.zeros_like(rel)
    for k in range(NZ):
        rel[k : k + 1] = SCALE * ratio[pl.ds(home(z, k), 1), :]
    rel[NZ : NZ + 1] = SCALE * (pprob - 1.0)
    cols = rel[...].T
    for k in range(NZ):
        wu[k * U : (k + 1) * U] = (users[k][0:U].astype(F32) * cols[:, k : k + 1]).astype(BF)
    coef = cols[:, NZ : NZ + 1]
    g_ref[N : N + U] = (users[0][0:U].astype(F32) * coef).astype(BF)
    pterm_ref[...] = pemb_ref[...].astype(F32) * coef
    for k in range(NZ):
        kept, i = (kept_a, k) if k < FIRST else (kept_b, k - FIRST)
        cols_k = slice(i * U, (i + 1) * U)
        ug = lax.dot_general(kept[0:N, cols_k], near_emb[...], TN, preferred_element_type=F32)
        ug = ug + lax.dot_general(kept[N:NN, cols_k], far_emb[...], TN, preferred_element_type=F32)
        ug_ref[home(z, k)] = (ug * cols[:, k : k + 1]).astype(BF)
    for m in range(NN // TILE):
        rows = slice(m * TILE, (m + 1) * TILE)
        g = mm(kept_a[rows], wu[0 : FIRST * U]) + mm(kept_b[rows], wu[FIRST * U :])
        first = m * TILE if m < 2 else m * TILE + U
        g_ref[first : first + TILE] = g.astype(BF)


def grads(scalars, tot, tloc, pexp, near_emb, far_emb, pemb, kept_a, kept_b, users):
    vm = pl.BlockSpec(memory_space=pltpu.VMEM)
    return pl.pallas_call(
        grad_kernel,
        in_specs=[pl.BlockSpec(memory_space=pltpu.SMEM)] + [vm] * (8 + NZ),
        out_specs=[vm, vm, vm],
        out_shape=[
            jax.ShapeDtypeStruct((NZ, U, E), BF),
            jax.ShapeDtypeStruct((ROWS, E), BF),
            jax.ShapeDtypeStruct((U, E), F32),
        ],
        scratch_shapes=[
            pltpu.VMEM((NZ * U, E), BF),
            pltpu.VMEM((NZ, U), F32),
            pltpu.VMEM((128, U), F32),
        ],
        compiler_params=params(),
        cost_estimate=cost(4 * NZ * U * NN * E, 8e6),
        name="grads",
    )(scalars, tot, tloc, pexp, near_emb, far_emb, pemb, kept_a, kept_b, *users)


def back_kernel(s_ref, g_ref, near_ref, pos_ref, far_ref, w_out_ref, hid_ref, far_hid, mine_ref, theirs_ref, feat):
    first, second, core = s_ref[1], s_ref[2], s_ref[3]
    feat[0:N] = near_ref[0:N]
    feat[N : N + U] = pos_ref[...]
    feat[N + U : ROWS] = far_ref[0:N]
    for c in range(H // WIDE):
        cols = slice(c * WIDE, (c + 1) * WIDE)
        hid = jnp.concatenate([hid_ref[:, cols], far_hid[:, cols]], axis=0)
        back = lax.dot_general(g_ref[...], w_out_ref[cols], NT, preferred_element_type=F32)
        back = jnp.where(hid > 0, back, 0.0).astype(BF)
        w_in = lax.dot_general(feat[...], back, TN, preferred_element_type=F32)
        w_out = lax.dot_general(hid, g_ref[...], TN, preferred_element_type=F32)
        to_mine, to_theirs = jnp.bitwise_xor(first, c), jnp.bitwise_xor(second, c)
        for t in range(WIDE // TILE):
            a, b = w_in[:, t * TILE : (t + 1) * TILE], w_out[t * TILE : (t + 1) * TILE]
            mine = jnp.where(core == 0, a, b).astype(BF)
            theirs = jnp.where(core == 0, b, a).astype(BF)
            for half in range(2):
                rows = slice(half * 128, (half + 1) * 128)
                mine_ref[to_mine, jnp.bitwise_xor(second, 2 * t + half)] = mine[rows]
                theirs_ref[to_theirs, jnp.bitwise_xor(first, 2 * t + half)] = theirs[rows]


def backward(scalars, g, near, pos, far, w_out, hid, far_hid):
    vm = pl.BlockSpec(memory_space=pltpu.VMEM)
    return pl.pallas_call(
        back_kernel,
        in_specs=[pl.BlockSpec(memory_space=pltpu.SMEM)] + [vm] * 7,
        out_specs=[vm, vm],
        out_shape=[jax.ShapeDtypeStruct((4, 4, 128, TILE), BF)] * 2,
        scratch_shapes=[pltpu.VMEM((ROWS, E), BF)],
        compiler_params=params(),
        cost_estimate=cost(6 * ROWS * E * H, 10e6),
        name="backward",
    )(scalars, g, near, pos, far, w_out, hid, far_hid)


def finish_kernel(s_ref, mine_ref, other_ref, w_in_ref, w_out_ref):
    first, second, core = s_ref[1], s_ref[2], s_ref[3]
    for t in range(2):
        for half in range(2):
            rows = slice(half * 128, (half + 1) * 128)
            mine = mine_ref[0, jnp.bitwise_xor(second, 2 * t + half)].astype(F32)
            other = other_ref[0, jnp.bitwise_xor(first, 2 * t + half)].astype(F32)
            w_in_ref[rows, t * TILE : (t + 1) * TILE] = jnp.where(core == 0, mine, other)
            start = t * TILE + half * 128
            w_out_ref[start : start + 128] = jnp.where(core == 0, other, mine)


def finish(scalars, mine, other):
    def place(outer):
        return pl.BlockSpec((1, 4, 128, TILE), lambda j, s: (jnp.bitwise_xor(j, s[outer]), 0, 0, 0))

    return pl.pallas_call(
        finish_kernel,
        grid_spec=pltpu.PrefetchScalarGridSpec(
            num_scalar_prefetch=1,
            grid=(4,),
            in_specs=[place(1), place(2)],
            out_specs=[
                pl.BlockSpec((E, 512), lambda j, s: (0, j)),
                pl.BlockSpec((512, E), lambda j, s: (j, 0)),
            ],
        ),
        out_shape=[jax.ShapeDtypeStruct((E, H), F32), jax.ShapeDtypeStruct((H, E), F32)],
        compiler_params=params(),
        cost_estimate=cost(0, 6e6),
        name="finish",
    )(scalars, mine, other)


def swap(x, axis, k):
    return lax.ppermute(x, axis, [(i, i ^ k) for i in range(SIZES[AXES.index(axis)])])


def after(x, *needed):
    return lax.optimization_barrier((x, *needed))[0]


def shift(x, by):
    return lax.ppermute(x, "z", [(i, (i + by) % NZ) for i in range(NZ)])


def device(x_lo, z, x_hi, y, core):
    return (((x_lo * 8 + z) * 2 + x_hi) * 4 + y) * 2 + core


def plane_swap(x, k, x_core):
    pairs = []
    for z in range(8):
        for xx in range(4):
            for y in range(4):
                for core in range(2):
                    to_x, to_y = (xx ^ k, y) if core == x_core else (xx, y ^ k)
                    pairs.append(
                        (device(xx & 1, z, xx >> 1, y, core), device(to_x & 1, z, to_x >> 1, to_y, core))
                    )
    return lax.ppermute(x, AXES, pairs)


def add(*terms):
    return sum(t.astype(F32) for t in terms)


def sum_over_z(x, rounds, dtype):
    for ks in rounds:
        sent = x.astype(dtype)
        terms = [t.astype(F32) for t in [sent] + [swap(sent, "z", k) for k in ks]]
        while len(terms) > 1:
            terms = [a + b for a, b in zip(terms[::2], terms[1::2])]
        x = terms[0]
    return x


def all_reduce(mine, theirs):
    half = add(mine, swap(theirs, "core", 1)).astype(BF)
    quarter = add(half[0], *[plane_swap(half[k], k, 0) for k in (1, 2, 3)]).astype(BF)
    part = add(quarter[0], *[plane_swap(quarter[k], k, 1) for k in (1, 2, 3)])
    part = sum_over_z(part, ((1,), (2, 4, 6)), BF).astype(BF)
    quarter = jnp.stack([part] + [plane_swap(part, k, 1) for k in (1, 2, 3)])
    half = jnp.stack([quarter] + [plane_swap(quarter, k, 0) for k in (1, 2, 3)])
    return half, swap(half, "core", 1)


def on_device(user_emb, pos_feat, pos_id, neg_feat, neg_id, neg_bucket, logq_table, w_in, w_out):
    x_lo, z, x_hi, y, core = [lax.axis_index(a) for a in AXES]
    xx = x_hi * 2 + x_lo
    scalars = jnp.stack([z, jnp.where(core == 0, xx, y), jnp.where(core == 0, y, xx), core]).astype(I32)

    mine, near = pack(user_emb, pos_id, neg_feat, neg_id, neg_bucket)
    up, down = shift(mine, 1), shift(mine, -1)
    far = swap(near, "x_lo", 1)
    users = [mine, up, down]
    (hid,) = in_vmem(hidden_kernel, "hidden", 2 * (N + U) * E * H, [((N + U, H), BF)], near, pos_feat, w_in)
    up, down = shift(after(up, hid), 1), shift(after(down, hid), -1)
    users += [up, down]
    near_emb, pemb = in_vmem(
        embed_kernel, "embed", 2 * (N + U) * E * H, [((N, E), BF), ((U, E), BF)], hid, w_out
    )
    up, down = shift(after(up, near_emb), 1), shift(after(down, near_emb), -1)
    users += [up, down]
    far_hid, far_emb, nid, bias = in_vmem(
        far_kernel,
        "far",
        4 * N * E * H,
        [((N, H), BF), ((N, E), BF), ((NN, 128), F32), ((NN, 128), F32)],
        near,
        far,
        w_in,
        w_out,
        logq_table.reshape(8, 128),
    )
    users += [shift(after(up, far_emb), 1)]
    none = jnp.zeros((NZ, U), F32)
    ks = tuple(range(NZ))
    tloc, tot, pexp, kept_a = score(ks[:FIRST], scalars, near_emb, far_emb, nid, bias, pemb, none, none, users)
    tloc, tot, _, kept_b = score(ks[FIRST:], scalars, near_emb, far_emb, nid, bias, pemb, tloc, tot, users)
    tot = sum_over_z(tot, ((1, 6, 7), (2,)), F32)
    ug, g, pterm = grads(scalars, tot, tloc, pexp, near_emb, far_emb, pemb, kept_a, kept_b, users)
    user_sum = lax.psum_scatter(ug, "z", scatter_dimension=0, tiled=False)
    mine_g, theirs_g = backward(scalars, g, near, pos_feat, far, w_out, hid, far_hid)
    half, other = all_reduce(mine_g, theirs_g)
    w_in_grad, w_out_grad = finish(scalars, half, other)
    user_grad = user_sum.astype(F32) + pterm
    return user_grad, w_in_grad, w_out_grad


def solution(mesh):
    rows = P(AXES, None)
    ids = P(AXES)
    return jax.shard_map(
        on_device,
        mesh=Mesh(mesh.devices.reshape(SIZES), AXES),
        in_specs=(rows, rows, ids, rows, ids, ids, P(), P(), P()),
        out_specs=(rows, P(), P()),
        check_vma=False,
    )
```

```python
import functools

import jax
import jax.numpy as jnp
from jax import lax
from jax.experimental import pallas as pl
from jax.experimental.pallas import tpu as pltpu
from jax.sharding import Mesh, PartitionSpec as P

AXES = ("x_lo", "z", "x_hi", "y", "core")
SIZES = (2, 8, 2, 4, 2)
BF, F32, I32 = jnp.bfloat16, jnp.float32, jnp.int32
SCALE = 0.125
SMALL = 2.0**-64
E, H, U, N = 256, 2048, 256, 512
NN = 2 * N
ROWS = NN + U
TILE = 256
CHUNKS = H // TILE
NZ = 8
OFFSETS = (0, -1, 1, -2, 2, -3, 3, 4)
FIRST = 5
VMEM_LIMIT = 24 * 1024 * 1024

WIDE = 512
NT = (((1,), (1,)), ((), ()))
TN = (((0,), (0,)), ((), ()))


def params(limit=VMEM_LIMIT):
    return pltpu.CompilerParams(vmem_limit_bytes=limit)


def cost(flops, nbytes, trans=0):
    return pl.CostEstimate(flops=int(flops), bytes_accessed=int(nbytes), transcendentals=int(trans))


def whole(shape):
    return pl.BlockSpec(shape, lambda *_: (0,) * len(shape))


def mm(a, b):
    return jnp.dot(a, b, preferred_element_type=F32)


def start(src, dst, sem):
    copy = pltpu.make_async_copy(src, dst, sem)
    copy.start()
    return copy


def pack_kernel(s_ref, user_hbm, pid_hbm, feat_hbm, nid_hbm, bucket_hbm, mine_ref, near_ref, pid_ref, nid_ref, bucket_ref, sems):
    del s_ref
    copies = [
        start(pid_hbm, pid_ref, sems.at[0]),
        start(nid_hbm, nid_ref, sems.at[1]),
        start(bucket_hbm, bucket_ref, sems.at[2]),
        start(user_hbm, mine_ref.at[0:U], sems.at[3]),
        start(feat_hbm, near_ref.at[0:N], sems.at[4]),
    ]
    row = lax.broadcasted_iota(I32, (16, E), 0)

    def tail(digits):
        out = jnp.zeros((16, E), F32)
        for i, digit in enumerate(digits):
            out = jnp.where(row == i, digit.astype(F32), out)
        return out.astype(BF)

    def digits(ids, bits):
        ids = [ids[:, i : i + 256] for i in range(0, ids.shape[1], 256)]
        return [i >> bits for i in ids] + [i & (2**bits - 1) for i in ids]

    for copy in copies[:3]:
        copy.wait()
    mine_ref[U : U + 16] = tail(digits(pid_ref[...], 6))
    near_ref[N : N + 16] = tail(digits(nid_ref[...], 6) + digits(bucket_ref[...], 5))
    for copy in copies[3:]:
        copy.wait()


def pack(scalars, user_emb, pos_id, neg_feat, neg_id, neg_bucket):
    vm = pl.BlockSpec(memory_space=pltpu.VMEM)
    return pl.pallas_call(
        pack_kernel,
        in_specs=[pl.BlockSpec(memory_space=pltpu.SMEM)] + [pl.BlockSpec(memory_space=pltpu.HBM)] * 5,
        out_specs=[vm] * 2,
        out_shape=[jax.ShapeDtypeStruct((U + 16, E), BF), jax.ShapeDtypeStruct((N + 16, E), BF)],
        scratch_shapes=[
            pltpu.VMEM((1, U), I32),
            pltpu.VMEM((1, N), I32),
            pltpu.VMEM((1, N), I32),
            pltpu.SemaphoreType.DMA((5,)),
        ],
        compiler_params=params(60 * 1024 * 1024),
        cost_estimate=cost(0, 1e6),
        name="pack",
    )(scalars, user_emb, pos_id.reshape(1, U), neg_feat, neg_id.reshape(1, N), neg_bucket.reshape(1, N))


def hidden(feat, w_in_ref):
    return jnp.maximum(mm(feat, w_in_ref[...]), 0.0).astype(BF)


def hidden_kernel(near_ref, pos_ref, w_in_ref, hid_ref, feat_ref, tail_ref, w_in_out):
    for m, feat in enumerate((near_ref[0:TILE], near_ref[TILE:N], pos_ref[...])):
        rows = slice(m * TILE, (m + 1) * TILE)
        feat_ref[rows] = feat
        hid_ref[rows] = hidden(feat, w_in_ref)
    tail_ref[...] = near_ref[N : N + 16]
    w_in_out[...] = w_in_ref[...]


def embed_kernel(hid_ref, w_out_ref, emb_ref, pemb_ref, w_out_out):
    w_out_out[...] = w_out_ref[...]
    for m, (ref, first) in enumerate([(emb_ref, 0), (emb_ref, TILE), (pemb_ref, 0)]):
        hid = hid_ref[m * TILE : (m + 1) * TILE]
        ref[first : first + TILE] = mm(hid, w_out_ref[...]).astype(BF)


def far_kernel(near_tail, far_ref, w_in_ref, w_out_ref, table_ref, hid_ref, emb_ref, nid_ref, bias_ref):
    lane = lax.broadcasted_iota(I32, (TILE, 128), 1).astype(F32)
    for side, tail in enumerate((near_tail[...], far_ref[N : N + 16])):
        tail = jnp.concatenate([tail.astype(F32), jnp.zeros((112, E), F32)], axis=0).T
        for block in range(2):
            rows = slice((2 * side + block) * TILE, (2 * side + block + 1) * TILE)
            nid = tail[:, block : block + 1] * 64.0 + tail[:, block + 2 : block + 3]
            nid_ref[rows] = jnp.broadcast_to(nid, (TILE, 128))
            bucket = tail[:, block + 4 : block + 5] * 32.0 + tail[:, block + 6 : block + 7]
            found = jnp.zeros((TILE, 128), F32)
            for b in range(8):
                found = found + jnp.where(bucket == lane + 128.0 * b, table_ref[b : b + 1], 0.0)
            bias_ref[rows] = jnp.broadcast_to(jnp.sum(found, axis=1, keepdims=True), (TILE, 128))
    for m in range(N // TILE):
        rows = slice(m * TILE, (m + 1) * TILE)
        hid = hidden(far_ref[rows], w_in_ref)
        hid_ref[rows] = hid
        emb_ref[rows] = mm(hid, w_out_ref[...]).astype(BF)


def in_vmem(kernel, name, flops, outs, *args):
    vm = pl.BlockSpec(memory_space=pltpu.VMEM)
    return pl.pallas_call(
        kernel,
        in_specs=[vm] * len(args),
        out_specs=[vm] * len(outs),
        out_shape=[jax.ShapeDtypeStruct(shape, dtype) for shape, dtype in outs],
        compiler_params=params(14 * 1024 * 1024),
        cost_estimate=cost(flops, 4e6),
        name=name,
    )(*args)


def twice(x):
    return jnp.concatenate([x, x], axis=1)


def home(z, k):
    return (z + OFFSETS[k] + NZ) & (NZ - 1)


def score_kernel(ks, s_ref, near_emb, far_emb, nid_ref, bias_ref, pemb_ref, tloc_in, tin_in, *rest):
    users = rest[: len(ks)]
    tloc_ref, tin_ref, pexp_ref, kept_ref, kf = rest[len(ks) :]
    z = s_ref[0]
    tloc_ref[...] = tloc_in[...]
    tin_ref[...] = tin_in[...]
    if ks[0] == 0:
        prod = users[0][0:U].astype(F32) * pemb_ref[...].astype(F32)
        prod = (prod[:, 0:128] + prod[:, 128:256]).T
        pexp_ref[...] = jnp.exp(SCALE * jnp.sum(prod, axis=0, keepdims=True))
    else:
        pexp_ref[...] = jnp.zeros_like(pexp_ref)
    for i, k in enumerate(ks):
        u = (users[i][0:U].astype(F32) * SCALE).astype(BF)
        tail = users[i][U : U + 16].astype(F32)
        pid = tail[0:1] * 64.0 + tail[1:2]
        total = jnp.zeros((8, U), F32)
        for m in range(NN // TILE):
            rows = slice(m * TILE, (m + 1) * TILE)
            emb = near_emb[rows] if m < 2 else far_emb[(m - 2) * TILE : (m - 1) * TILE]
            sc = lax.dot_general(emb, u, NT, preferred_element_type=F32) - twice(bias_ref[rows])
            kept = jnp.where(twice(nid_ref[rows]) != pid, jnp.exp(sc), 0.0)
            kf[rows] = kept
            total = total + jnp.sum(kept.reshape(TILE // 8, 8, U), axis=0)
        t = jnp.sum(total, axis=0, keepdims=True)
        shrink = jnp.where(t > 1.0, SMALL, 1.0)
        inv = jnp.where(t > 0.0, 1.0 / (t * shrink), 0.0)
        for m in range(NN // TILE):
            rows = slice(m * TILE, (m + 1) * TILE)
            kept_ref[rows, i * U : (i + 1) * U] = ((kf[rows] * shrink) * inv).astype(BF)
        row = pl.ds(home(z, k), 1)
        tloc_ref[row, :] = t
        tin_ref[row, :] = t + pexp_ref[...] if k == 0 else t


def score(ks, scalars, near_emb, far_emb, nid, bias, pemb, tloc, tin, users):
    vm = pl.BlockSpec(memory_space=pltpu.VMEM)
    n = len(ks)
    return pl.pallas_call(
        functools.partial(score_kernel, ks),
        in_specs=[pl.BlockSpec(memory_space=pltpu.SMEM)] + [vm] * (7 + n),
        out_specs=[vm] * 4,
        out_shape=[
            jax.ShapeDtypeStruct((NZ, U), F32),
            jax.ShapeDtypeStruct((NZ, U), F32),
            jax.ShapeDtypeStruct((1, U), F32),
            jax.ShapeDtypeStruct((NN, n * U), BF),
        ],
        scratch_shapes=[pltpu.VMEM((NN, U), F32)],
        compiler_params=params(14 * 1024 * 1024),
        cost_estimate=cost(2 * n * U * NN * E, 5e6, n * U * NN),
        name="score",
    )(scalars, near_emb, far_emb, nid, bias, pemb, tloc, tin, *[users[k] for k in ks])


def grad_kernel(s_ref, tot_ref, tloc_ref, pexp_ref, near_emb, far_emb, pemb_ref, kept_a, kept_b, *rest):
    users = rest[:NZ]
    keep_ref, send_ref, g_ref, pterm_ref, wu, ratio, rel = rest[NZ:]
    z = s_ref[0]
    tot = tot_ref[...]
    shrink = jnp.where(tot > 1.0, SMALL, 1.0)
    ratio[...] = (tloc_ref[...] * shrink) * (1.0 / (tot * shrink))
    own = tot_ref[pl.ds(z, 1), :]
    shrink = jnp.where(own > 1.0, SMALL, 1.0)
    pprob = (pexp_ref[...] * shrink) * (1.0 / (own * shrink))
    rel[...] = jnp.zeros_like(rel)
    for k in range(NZ):
        rel[k : k + 1] = SCALE * ratio[pl.ds(home(z, k), 1), :]
    rel[NZ : NZ + 1] = SCALE * (pprob - 1.0)
    cols = rel[...].T
    for k in range(NZ):
        wu[k * U : (k + 1) * U] = (users[k][0:U].astype(F32) * cols[:, k : k + 1]).astype(BF)
    coef = cols[:, NZ : NZ + 1]
    g_ref[N : N + U] = (users[0][0:U].astype(F32) * coef).astype(BF)
    pterm_ref[...] = pemb_ref[...].astype(F32) * coef
    for k in range(NZ):
        kept, i = (kept_a, k) if k < FIRST else (kept_b, k - FIRST)
        cols_k = slice(i * U, (i + 1) * U)
        ug = lax.dot_general(kept[0:N, cols_k], near_emb[...], TN, preferred_element_type=F32)
        ug = ug + lax.dot_general(kept[N:NN, cols_k], far_emb[...], TN, preferred_element_type=F32)
        apart = jnp.bitwise_xor(home(z, k), z)
        place = (apart & 2) + (apart >> 2)
        (send_ref if OFFSETS[k] % 2 else keep_ref)[place] = (ug * cols[:, k : k + 1]).astype(BF)
    for m in range(NN // TILE):
        rows = slice(m * TILE, (m + 1) * TILE)
        g = mm(kept_a[rows], wu[0 : FIRST * U]) + mm(kept_b[rows], wu[FIRST * U :])
        first = m * TILE if m < 2 else m * TILE + U
        g_ref[first : first + TILE] = g.astype(BF)


def grads(scalars, tot, tloc, pexp, near_emb, far_emb, pemb, kept_a, kept_b, users):
    vm = pl.BlockSpec(memory_space=pltpu.VMEM)
    return pl.pallas_call(
        grad_kernel,
        in_specs=[pl.BlockSpec(memory_space=pltpu.SMEM)] + [vm] * (8 + NZ),
        out_specs=[vm] * 4,
        out_shape=[
            jax.ShapeDtypeStruct((NZ // 2, U, E), BF),
            jax.ShapeDtypeStruct((NZ // 2, U, E), BF),
            jax.ShapeDtypeStruct((ROWS, E), BF),
            jax.ShapeDtypeStruct((U, E), F32),
        ],
        scratch_shapes=[
            pltpu.VMEM((NZ * U, E), BF),
            pltpu.VMEM((NZ, U), F32),
            pltpu.VMEM((128, U), F32),
        ],
        compiler_params=params(),
        cost_estimate=cost(4 * NZ * U * NN * E, 8e6),
        name="grads",
    )(scalars, tot, tloc, pexp, near_emb, far_emb, pemb, kept_a, kept_b, *users)


def back_kernel(s_ref, g_ref, feat_ref, far_ref, w_out_ref, hid_ref, far_hid, mine_ref, theirs_ref, feat):
    first, second, core = s_ref[1], s_ref[2], s_ref[3]
    feat[0 : N + U] = feat_ref[...]
    feat[N + U : ROWS] = far_ref[0:N]
    for c in range(H // WIDE):
        cols = slice(c * WIDE, (c + 1) * WIDE)
        hid = jnp.concatenate([hid_ref[:, cols], far_hid[:, cols]], axis=0)
        back = lax.dot_general(g_ref[...], w_out_ref[cols], NT, preferred_element_type=F32)
        back = jnp.where(hid > 0, back, 0.0).astype(BF)
        w_in = lax.dot_general(feat[...], back, TN, preferred_element_type=F32)
        w_out = lax.dot_general(hid, g_ref[...], TN, preferred_element_type=F32)
        to_mine, to_theirs = jnp.bitwise_xor(first, c), jnp.bitwise_xor(second, c)
        for t in range(WIDE // TILE):
            a, b = w_in[:, t * TILE : (t + 1) * TILE], w_out[t * TILE : (t + 1) * TILE]
            mine = jnp.where(core == 0, a, b).astype(BF)
            theirs = jnp.where(core == 0, b, a).astype(BF)
            for half in range(2):
                rows = slice(half * 128, (half + 1) * 128)
                mine_ref[to_mine, jnp.bitwise_xor(second, 2 * t + half)] = mine[rows]
                theirs_ref[to_theirs, jnp.bitwise_xor(first, 2 * t + half)] = theirs[rows]


def backward(scalars, g, feat, far, w_out, hid, far_hid):
    vm = pl.BlockSpec(memory_space=pltpu.VMEM)
    return pl.pallas_call(
        back_kernel,
        in_specs=[pl.BlockSpec(memory_space=pltpu.SMEM)] + [vm] * 6,
        out_specs=[vm, vm],
        out_shape=[jax.ShapeDtypeStruct((4, 4, 128, TILE), BF)] * 2,
        scratch_shapes=[pltpu.VMEM((ROWS, E), BF)],
        compiler_params=params(),
        cost_estimate=cost(6 * ROWS * E * H, 10e6),
        name="backward",
    )(scalars, g, feat, far, w_out, hid, far_hid)


def finish_kernel(s_ref, mine_ref, other_ref, w_in_ref, w_out_ref):
    first, second, core = s_ref[1], s_ref[2], s_ref[3]
    for t in range(2):
        for half in range(2):
            rows = slice(half * 128, (half + 1) * 128)
            mine = mine_ref[0, jnp.bitwise_xor(second, 2 * t + half)].astype(F32)
            other = other_ref[0, jnp.bitwise_xor(first, 2 * t + half)].astype(F32)
            w_in_ref[rows, t * TILE : (t + 1) * TILE] = jnp.where(core == 0, mine, other)
            start = t * TILE + half * 128
            w_out_ref[start : start + 128] = jnp.where(core == 0, other, mine)


def finish(scalars, mine, other):
    def place(outer):
        return pl.BlockSpec((1, 4, 128, TILE), lambda j, s: (jnp.bitwise_xor(j, s[outer]), 0, 0, 0))

    return pl.pallas_call(
        finish_kernel,
        grid_spec=pltpu.PrefetchScalarGridSpec(
            num_scalar_prefetch=1,
            grid=(4,),
            in_specs=[place(1), place(2)],
            out_specs=[
                pl.BlockSpec((E, 512), lambda j, s: (0, j)),
                pl.BlockSpec((512, E), lambda j, s: (j, 0)),
            ],
        ),
        out_shape=[jax.ShapeDtypeStruct((E, H), F32), jax.ShapeDtypeStruct((H, E), F32)],
        compiler_params=params(),
        cost_estimate=cost(0, 6e6),
        name="finish",
    )(scalars, mine, other)


def swap(x, axis, k):
    return lax.ppermute(x, axis, [(i, i ^ k) for i in range(SIZES[AXES.index(axis)])])


def after(x, *needed):
    return lax.optimization_barrier((x, *needed))[0]


def shift(x, by):
    return lax.ppermute(x, "z", [(i, (i + by) % NZ) for i in range(NZ)])


def device(x_lo, z, x_hi, y, core):
    return (((x_lo * 8 + z) * 2 + x_hi) * 4 + y) * 2 + core


def plane_swap(x, k, x_core):
    pairs = []
    for z in range(8):
        for xx in range(4):
            for y in range(4):
                for core in range(2):
                    to_x, to_y = (xx ^ k, y) if core == x_core else (xx, y ^ k)
                    pairs.append(
                        (device(xx & 1, z, xx >> 1, y, core), device(to_x & 1, z, to_x >> 1, to_y, core))
                    )
    return lax.ppermute(x, AXES, pairs)


def add(*terms):
    return sum(t.astype(F32) for t in terms)


def sum_over_z(x, rounds, dtype):
    for ks in rounds:
        sent = x.astype(dtype)
        terms = [t.astype(F32) for t in [sent] + [swap(sent, "z", k) for k in ks]]
        while len(terms) > 1:
            terms = [a + b for a, b in zip(terms[::2], terms[1::2])]
        x = terms[0]
    return x


def halve(keep, send, k):
    total = add(keep, swap(send, "z", k)).astype(BF)
    half = total.shape[0] // 2
    return (total[:half], total[half:]) if half else total[0]


def all_reduce(mine, theirs, keep, send):
    half = add(mine, swap(theirs, "core", 1)).astype(BF)
    quarter = add(half[0], *[plane_swap(half[k], k, 0) for k in (1, 2, 3)]).astype(BF)
    keep, send = halve(keep, send, 1)
    quarter, keep, send = lax.optimization_barrier((quarter, keep, send))
    part = add(quarter[0], *[plane_swap(quarter[k], k, 1) for k in (1, 2, 3)])
    keep, send = halve(keep, send, 2)
    part, keep, send = lax.optimization_barrier((part, keep, send))
    part = sum_over_z(part, ((1,), (2, 4, 6)), BF).astype(BF)
    part, keep, send = lax.optimization_barrier((part, keep, send))
    quarter = jnp.stack([part] + [plane_swap(part, k, 1) for k in (1, 2, 3)])
    user = halve(keep, send, 4)
    quarter, user = lax.optimization_barrier((quarter, user))
    half = jnp.stack([quarter] + [plane_swap(quarter, k, 0) for k in (1, 2, 3)])
    return half, swap(half, "core", 1), user


def on_device(user_emb, pos_feat, pos_id, neg_feat, neg_id, neg_bucket, logq_table, w_in, w_out):
    x_lo, z, x_hi, y, core = [lax.axis_index(a) for a in AXES]
    xx = x_hi * 2 + x_lo
    scalars = jnp.stack([z, jnp.where(core == 0, xx, y), jnp.where(core == 0, y, xx), core]).astype(I32)

    mine, near = pack(scalars, user_emb, pos_id, neg_feat, neg_id, neg_bucket)
    up, down = shift(mine, 1), shift(mine, -1)
    far = swap(near, "x_lo", 1)
    users = [mine, up, down]
    hid, feat, tail, w_in = in_vmem(
        hidden_kernel,
        "hidden",
        2 * (N + U) * E * H,
        [((N + U, H), BF), ((N + U, E), BF), ((16, E), BF), ((E, H), BF)],
        near,
        pos_feat,
        w_in,
    )
    up, down = shift(after(up, hid), 1), shift(after(down, hid), -1)
    users += [up, down]
    near_emb, pemb, w_out = in_vmem(
        embed_kernel, "embed", 2 * (N + U) * E * H, [((N, E), BF), ((U, E), BF), ((H, E), BF)], hid, w_out
    )
    up, down = shift(after(up, near_emb), 1), shift(after(down, near_emb), -1)
    users += [up, down]
    far_hid, far_emb, nid, bias = in_vmem(
        far_kernel,
        "far",
        4 * N * E * H,
        [((N, H), BF), ((N, E), BF), ((NN, 128), F32), ((NN, 128), F32)],
        tail,
        far,
        w_in,
        w_out,
        logq_table.reshape(8, 128),
    )
    users += [shift(after(up, far_emb), 1)]
    none = jnp.zeros((NZ, U), F32)
    ks = tuple(range(NZ))
    tloc, tot, pexp, kept_a = score(ks[:FIRST], scalars, near_emb, far_emb, nid, bias, pemb, none, none, users)
    tloc, tot, _, kept_b = score(ks[FIRST:], scalars, near_emb, far_emb, nid, bias, pemb, tloc, tot, users)
    tot = sum_over_z(tot, ((1, 6, 7), (2,)), F32)
    keep, send, g, pterm = grads(
        scalars, tot, tloc, pexp, near_emb, far_emb, pemb, kept_a, kept_b, users
    )
    mine_g, theirs_g = backward(scalars, g, feat, far, w_out, hid, far_hid)
    half, other, user = all_reduce(mine_g, theirs_g, keep, send)
    w_in_grad, w_out_grad = finish(scalars, half, other)
    return user.astype(F32) + pterm, w_in_grad, w_out_grad


def solution(mesh):
    rows = P(AXES, None)
    ids = P(AXES)
    return jax.shard_map(
        on_device,
        mesh=Mesh(mesh.devices.reshape(SIZES), AXES),
        in_specs=(rows, rows, ids, rows, ids, ids, P(), P(), P()),
        out_specs=(rows, P(), P()),
        check_vma=False,
    )
```

```python
import functools

import jax
import jax.numpy as jnp
from jax import lax
from jax.experimental import pallas as pl
from jax.experimental.pallas import tpu as pltpu
from jax.sharding import Mesh, PartitionSpec as P

AXES = ("x_lo", "z", "x_hi", "y", "core")
SIZES = (2, 8, 2, 4, 2)
BF, F32, I32 = jnp.bfloat16, jnp.float32, jnp.int32
SCALE = 0.125
SMALL = 2.0**-64
E, H, U, N = 256, 2048, 256, 512
NN = 2 * N
ROWS = NN + U
TILE = 256
CHUNKS = H // TILE
NZ = 8
OFFSETS = (0, -1, 1, -2, 2, -3, 3, 4)
FIRST = 5
VMEM_LIMIT = 24 * 1024 * 1024

WIDE = 512
NT = (((1,), (1,)), ((), ()))
TN = (((0,), (0,)), ((), ()))


def params(limit=VMEM_LIMIT):
    return pltpu.CompilerParams(vmem_limit_bytes=limit)


def cost(flops, nbytes, trans=0):
    return pl.CostEstimate(flops=int(flops), bytes_accessed=int(nbytes), transcendentals=int(trans))


def whole(shape):
    return pl.BlockSpec(shape, lambda *_: (0,) * len(shape))


def mm(a, b):
    return jnp.dot(a, b, preferred_element_type=F32)


def start(src, dst, sem):
    copy = pltpu.make_async_copy(src, dst, sem)
    copy.start()
    return copy


def pack_kernel(user_hbm, pid_hbm, feat_hbm, nid_hbm, bucket_hbm, mine_ref, near_ref, pid_ref, nid_ref, bucket_ref, sems):
    copies = [
        start(pid_hbm, pid_ref, sems.at[0]),
        start(nid_hbm, nid_ref, sems.at[1]),
        start(bucket_hbm, bucket_ref, sems.at[2]),
        start(user_hbm, mine_ref.at[0:U], sems.at[3]),
        start(feat_hbm, near_ref.at[0:N], sems.at[4]),
    ]
    row = lax.broadcasted_iota(I32, (16, E), 0)

    def tail(digits):
        out = jnp.zeros((16, E), F32)
        for i, digit in enumerate(digits):
            out = jnp.where(row == i, digit.astype(F32), out)
        return out.astype(BF)

    def digits(ids, bits):
        ids = [ids[:, i : i + 256] for i in range(0, ids.shape[1], 256)]
        return [i >> bits for i in ids] + [i & (2**bits - 1) for i in ids]

    for copy in copies[:3]:
        copy.wait()
    mine_ref[U : U + 16] = tail(digits(pid_ref[...], 6))
    near_ref[N : N + 16] = tail(digits(nid_ref[...], 6) + digits(bucket_ref[...], 5))
    for copy in copies[3:]:
        copy.wait()


def pack(user_emb, pos_id, neg_feat, neg_id, neg_bucket):
    vm = pl.BlockSpec(memory_space=pltpu.VMEM)
    return pl.pallas_call(
        pack_kernel,
        in_specs=[pl.BlockSpec(memory_space=pltpu.HBM)] * 5,
        out_specs=[vm] * 2,
        out_shape=[jax.ShapeDtypeStruct((U + 16, E), BF), jax.ShapeDtypeStruct((N + 16, E), BF)],
        scratch_shapes=[
            pltpu.VMEM((1, U), I32),
            pltpu.VMEM((1, N), I32),
            pltpu.VMEM((1, N), I32),
            pltpu.SemaphoreType.DMA((5,)),
        ],
        compiler_params=params(60 * 1024 * 1024),
        cost_estimate=cost(0, 1e6),
        name="pack",
    )(user_emb, pos_id.reshape(1, U), neg_feat, neg_id.reshape(1, N), neg_bucket.reshape(1, N))


def hidden(feat, w_in_ref):
    return jnp.maximum(mm(feat, w_in_ref[...]), 0.0).astype(BF)


def hidden_kernel(near_ref, pos_ref, w_in_ref, hid_ref, feat_ref, tail_ref, w_in_out):
    for m, feat in enumerate((near_ref[0:TILE], near_ref[TILE:N], pos_ref[...])):
        rows = slice(m * TILE, (m + 1) * TILE)
        feat_ref[rows] = feat
        hid_ref[rows] = hidden(feat, w_in_ref)
    tail_ref[...] = near_ref[N : N + 16]
    w_in_out[...] = w_in_ref[...]


def embed_kernel(hid_ref, w_out_ref, emb_ref, pemb_ref, w_out_out):
    w_out_out[...] = w_out_ref[...]
    for m, (ref, first) in enumerate([(emb_ref, 0), (emb_ref, TILE), (pemb_ref, 0)]):
        hid = hid_ref[m * TILE : (m + 1) * TILE]
        ref[first : first + TILE] = mm(hid, w_out_ref[...]).astype(BF)


def far_kernel(near_tail, far_ref, w_in_ref, w_out_ref, table_ref, hid_ref, emb_ref, nid_ref, bias_ref):
    lane = lax.broadcasted_iota(I32, (TILE, 128), 1).astype(F32)
    for side, tail in enumerate((near_tail[...], far_ref[N : N + 16])):
        tail = jnp.concatenate([tail.astype(F32), jnp.zeros((112, E), F32)], axis=0).T
        for block in range(2):
            rows = slice((2 * side + block) * TILE, (2 * side + block + 1) * TILE)
            nid = tail[:, block : block + 1] * 64.0 + tail[:, block + 2 : block + 3]
            nid_ref[rows] = jnp.broadcast_to(nid, (TILE, 128))
            bucket = tail[:, block + 4 : block + 5] * 32.0 + tail[:, block + 6 : block + 7]
            found = jnp.zeros((TILE, 128), F32)
            for b in range(8):
                found = found + jnp.where(bucket == lane + 128.0 * b, table_ref[b : b + 1], 0.0)
            bias_ref[rows] = jnp.broadcast_to(jnp.sum(found, axis=1, keepdims=True), (TILE, 128))
    for m in range(N // TILE):
        rows = slice(m * TILE, (m + 1) * TILE)
        hid = hidden(far_ref[rows], w_in_ref)
        hid_ref[rows] = hid
        emb_ref[rows] = mm(hid, w_out_ref[...]).astype(BF)


def in_vmem(kernel, name, flops, outs, *args):
    vm = pl.BlockSpec(memory_space=pltpu.VMEM)
    return pl.pallas_call(
        kernel,
        in_specs=[vm] * len(args),
        out_specs=[vm] * len(outs),
        out_shape=[jax.ShapeDtypeStruct(shape, dtype) for shape, dtype in outs],
        compiler_params=params(14 * 1024 * 1024),
        cost_estimate=cost(flops, 4e6),
        name=name,
    )(*args)


def twice(x):
    return jnp.concatenate([x, x], axis=1)


def home(z, k):
    return (z + OFFSETS[k] + NZ) & (NZ - 1)


def score_kernel(ks, near_emb, far_emb, nid_ref, bias_ref, pemb_ref, tloc_in, tin_in, *rest):
    users = rest[: len(ks)]
    tloc_ref, tin_ref, pexp_ref, kept_ref, kf = rest[len(ks) :]
    z = lax.axis_index("z")
    tloc_ref[...] = tloc_in[...]
    tin_ref[...] = tin_in[...]
    if ks[0] == 0:
        prod = users[0][0:U].astype(F32) * pemb_ref[...].astype(F32)
        prod = (prod[:, 0:128] + prod[:, 128:256]).T
        pexp_ref[...] = jnp.exp(SCALE * jnp.sum(prod, axis=0, keepdims=True))
    else:
        pexp_ref[...] = jnp.zeros_like(pexp_ref)
    for i, k in enumerate(ks):
        u = (users[i][0:U].astype(F32) * SCALE).astype(BF)
        tail = users[i][U : U + 16].astype(F32)
        pid = tail[0:1] * 64.0 + tail[1:2]
        total = jnp.zeros((8, U), F32)
        for m in range(NN // TILE):
            rows = slice(m * TILE, (m + 1) * TILE)
            emb = near_emb[rows] if m < 2 else far_emb[(m - 2) * TILE : (m - 1) * TILE]
            sc = lax.dot_general(emb, u, NT, preferred_element_type=F32) - twice(bias_ref[rows])
            kept = jnp.where(twice(nid_ref[rows]) != pid, jnp.exp(sc), 0.0)
            kf[rows] = kept
            total = total + jnp.sum(kept.reshape(TILE // 8, 8, U), axis=0)
        t = jnp.sum(total, axis=0, keepdims=True)
        shrink = jnp.where(t > 1.0, SMALL, 1.0)
        inv = jnp.where(t > 0.0, 1.0 / (t * shrink), 0.0)
        for m in range(NN // TILE):
            rows = slice(m * TILE, (m + 1) * TILE)
            kept_ref[rows, i * U : (i + 1) * U] = ((kf[rows] * shrink) * inv).astype(BF)
        row = pl.ds(home(z, k), 1)
        tloc_ref[row, :] = t
        tin_ref[row, :] = t + pexp_ref[...] if k == 0 else t


def score(ks, near_emb, far_emb, nid, bias, pemb, tloc, tin, users):
    vm = pl.BlockSpec(memory_space=pltpu.VMEM)
    n = len(ks)
    return pl.pallas_call(
        functools.partial(score_kernel, ks),
        in_specs=[vm] * (7 + n),
        out_specs=[vm] * 4,
        out_shape=[
            jax.ShapeDtypeStruct((NZ, U), F32),
            jax.ShapeDtypeStruct((NZ, U), F32),
            jax.ShapeDtypeStruct((1, U), F32),
            jax.ShapeDtypeStruct((NN, n * U), BF),
        ],
        scratch_shapes=[pltpu.VMEM((NN, U), F32)],
        compiler_params=params(14 * 1024 * 1024),
        cost_estimate=cost(2 * n * U * NN * E, 5e6, n * U * NN),
        name="score",
    )(near_emb, far_emb, nid, bias, pemb, tloc, tin, *[users[k] for k in ks])


def grad_kernel(tot_ref, tloc_ref, pexp_ref, near_emb, far_emb, pemb_ref, kept_a, kept_b, *rest):
    users = rest[:NZ]
    keep_ref, send_ref, g_ref, pterm_ref, wu, ratio, rel = rest[NZ:]
    z = lax.axis_index("z")
    tot = tot_ref[...]
    shrink = jnp.where(tot > 1.0, SMALL, 1.0)
    ratio[...] = (tloc_ref[...] * shrink) * (1.0 / (tot * shrink))
    own = tot_ref[pl.ds(z, 1), :]
    shrink = jnp.where(own > 1.0, SMALL, 1.0)
    pprob = (pexp_ref[...] * shrink) * (1.0 / (own * shrink))
    rel[...] = jnp.zeros_like(rel)
    for k in range(NZ):
        rel[k : k + 1] = SCALE * ratio[pl.ds(home(z, k), 1), :]
    rel[NZ : NZ + 1] = SCALE * (pprob - 1.0)
    cols = rel[...].T
    for k in range(NZ):
        wu[k * U : (k + 1) * U] = (users[k][0:U].astype(F32) * cols[:, k : k + 1]).astype(BF)
    coef = cols[:, NZ : NZ + 1]
    g_ref[N : N + U] = (users[0][0:U].astype(F32) * coef).astype(BF)
    pterm_ref[...] = pemb_ref[...].astype(F32) * coef
    for k in range(NZ):
        kept, i = (kept_a, k) if k < FIRST else (kept_b, k - FIRST)
        cols_k = slice(i * U, (i + 1) * U)
        ug = lax.dot_general(kept[0:N, cols_k], near_emb[...], TN, preferred_element_type=F32)
        ug = ug + lax.dot_general(kept[N:NN, cols_k], far_emb[...], TN, preferred_element_type=F32)
        apart = jnp.bitwise_xor(home(z, k), z)
        place = (apart & 2) + (apart >> 2)
        (send_ref if OFFSETS[k] % 2 else keep_ref)[place] = (ug * cols[:, k : k + 1]).astype(BF)
    for m in range(NN // TILE):
        rows = slice(m * TILE, (m + 1) * TILE)
        g = mm(kept_a[rows], wu[0 : FIRST * U]) + mm(kept_b[rows], wu[FIRST * U :])
        first = m * TILE if m < 2 else m * TILE + U
        g_ref[first : first + TILE] = g.astype(BF)


def grads(tot, tloc, pexp, near_emb, far_emb, pemb, kept_a, kept_b, users):
    vm = pl.BlockSpec(memory_space=pltpu.VMEM)
    return pl.pallas_call(
        grad_kernel,
        in_specs=[vm] * (8 + NZ),
        out_specs=[vm] * 4,
        out_shape=[
            jax.ShapeDtypeStruct((NZ // 2, U, E), BF),
            jax.ShapeDtypeStruct((NZ // 2, U, E), BF),
            jax.ShapeDtypeStruct((ROWS, E), BF),
            jax.ShapeDtypeStruct((U, E), F32),
        ],
        scratch_shapes=[
            pltpu.VMEM((NZ * U, E), BF),
            pltpu.VMEM((NZ, U), F32),
            pltpu.VMEM((128, U), F32),
        ],
        compiler_params=params(),
        cost_estimate=cost(4 * NZ * U * NN * E, 8e6),
        name="grads",
    )(tot, tloc, pexp, near_emb, far_emb, pemb, kept_a, kept_b, *users)


def order():
    core = lax.axis_index("core")
    xx, y = lax.axis_index("x_hi") * 2 + lax.axis_index("x_lo"), lax.axis_index("y")
    return core, jnp.where(core == 0, xx, y), jnp.where(core == 0, y, xx)


def back_kernel(mine, g_ref, feat_ref, far_ref, w_out_ref, hid_ref, far_hid, out_ref):
    core, first, second = order()
    if not mine:
        core, first, second = 1 - core, second, first
    for c in range(2):
        cols = pl.ds(pl.multiple_of(core * (H // 2) + c * WIDE, WIDE), WIDE)
        w_in = w_out = 0.0
        for rows, feat, hid in ((slice(0, N + U), feat_ref, hid_ref), (slice(N + U, ROWS), far_ref, far_hid)):
            hid = hid[:, cols]
            g = g_ref[rows]
            back = lax.dot_general(g, w_out_ref[cols], NT, preferred_element_type=F32)
            back = jnp.where(hid > 0, back, 0.0).astype(BF)
            w_in += lax.dot_general(feat[0 : g.shape[0]], back, TN, preferred_element_type=F32)
            w_out += lax.dot_general(hid, g, TN, preferred_element_type=F32)
        w_in, w_out = w_in.astype(BF), w_out.astype(BF)
        for t in range(2):
            for half in range(2):
                inner = jnp.bitwise_xor(second, 2 * t + half)
                rows = slice(half * 128, (half + 1) * 128)
                out_ref[jnp.bitwise_xor(first, c), inner] = w_in[rows, t * TILE : (t + 1) * TILE]
                rows = slice(t * TILE + half * 128, t * TILE + (half + 1) * 128)
                out_ref[jnp.bitwise_xor(first, 2 + c), inner] = w_out[rows]


def backward(mine, *args):
    return in_vmem(
        functools.partial(back_kernel, mine), "backward", 3 * ROWS * E * H, [((4, 4, 128, TILE), BF)], *args
    )[0]


def finish_kernel(mine, x_ref, *rest):
    w_in_hbm, w_out_hbm, a, b, sems = rest[-5:]
    core, first, second = order()
    if not mine:
        core, first, second = 1 - core, second, first
    copies = []
    for c in range(2):
        for t in range(2):
            for half in range(2):
                inner = jnp.bitwise_xor(second, 2 * t + half)
                start_t = c * WIDE + t * TILE
                cols = slice(start_t, start_t + TILE)
                a[half * 128 : (half + 1) * 128, cols] = x_ref[jnp.bitwise_xor(first, c), inner].astype(F32)
                rows = slice(start_t + half * 128, start_t + (half + 1) * 128)
                b[rows] = x_ref[jnp.bitwise_xor(first, 2 + c), inner].astype(F32)
        here = pl.ds(c * WIDE, WIDE)
        there = pl.ds(pl.multiple_of(core * (H // 2) + c * WIDE, WIDE), WIDE)
        copies.append(start(a.at[:, here], w_in_hbm.at[:, there], sems.at[2 * c]))
        copies.append(start(b.at[here], w_out_hbm.at[there], sems.at[2 * c + 1]))
    for copy in copies:
        copy.wait()


def finish(mine, x, *outs):
    vm, hbm = pl.BlockSpec(memory_space=pltpu.VMEM), pl.BlockSpec(memory_space=pl.ANY)
    return pl.pallas_call(
        functools.partial(finish_kernel, mine),
        in_specs=[vm] + [hbm] * len(outs),
        out_specs=[hbm, hbm],
        out_shape=[jax.ShapeDtypeStruct((E, H), F32), jax.ShapeDtypeStruct((H, E), F32)],
        scratch_shapes=[
            pltpu.VMEM((E, H // 2), F32),
            pltpu.VMEM((H // 2, E), F32),
            pltpu.SemaphoreType.DMA((4,)),
        ],
        input_output_aliases={1: 0, 2: 1} if outs else {},
        compiler_params=params(14 * 1024 * 1024),
        cost_estimate=cost(0, 3e6),
        name="finish",
    )(x, *outs)


def swap(x, axis, k):
    return lax.ppermute(x, axis, [(i, i ^ k) for i in range(SIZES[AXES.index(axis)])])


def after(x, *needed):
    return lax.optimization_barrier((x, *needed))[0]


def shift(x, by):
    return lax.ppermute(x, "z", [(i, (i + by) % NZ) for i in range(NZ)])


def device(x_lo, z, x_hi, y, core):
    return (((x_lo * 8 + z) * 2 + x_hi) * 4 + y) * 2 + core


def plane_swap(x, k, x_core):
    pairs = []
    for z in range(8):
        for xx in range(4):
            for y in range(4):
                for core in range(2):
                    to_x, to_y = (xx ^ k, y) if core == x_core else (xx, y ^ k)
                    pairs.append(
                        (device(xx & 1, z, xx >> 1, y, core), device(to_x & 1, z, to_x >> 1, to_y, core))
                    )
    return lax.ppermute(x, AXES, pairs)


def add(*terms):
    return sum(t.astype(F32) for t in terms)


def sum_over_z(x, rounds, dtype):
    for ks in rounds:
        sent = x.astype(dtype)
        terms = [t.astype(F32) for t in [sent] + [swap(sent, "z", k) for k in ks]]
        while len(terms) > 1:
            terms = [a + b for a, b in zip(terms[::2], terms[1::2])]
        x = terms[0]
    return x


def all_reduce(mine, theirs, keep, send):
    half = add(mine, swap(theirs, "core", 1)).astype(BF)
    quarter = add(half[0], *[plane_swap(half[k], k, 0) for k in (1, 2, 3)]).astype(BF)
    keep = add(keep, swap(send, "z", 1)).astype(BF)
    quarter, keep = lax.optimization_barrier((quarter, keep))
    part = add(quarter[0], *[plane_swap(quarter[k], k, 1) for k in (1, 2, 3)])
    part = sum_over_z(part, ((1,), (2, 4, 6)), BF).astype(BF)
    part, keep = lax.optimization_barrier((part, keep))
    quarter = jnp.stack([part] + [plane_swap(part, k, 1) for k in (1, 2, 3)])
    user = add(keep[0], *[swap(keep[i], "z", k) for i, k in ((1, 4), (2, 2), (3, 6))])
    others = [plane_swap(quarter, k, 0) for k in (1, 2, 3)]
    others, user = lax.optimization_barrier((others, user))
    half = jnp.stack([quarter] + others)
    return half, swap(half, "core", 1), user


def on_device(user_emb, pos_feat, pos_id, neg_feat, neg_id, neg_bucket, logq_table, w_in, w_out):
    mine, near = pack(user_emb, pos_id, neg_feat, neg_id, neg_bucket)
    up, down = shift(mine, 1), shift(mine, -1)
    far = swap(near, "x_lo", 1)
    users = [mine, up, down]
    hid, feat, tail, w_in = in_vmem(
        hidden_kernel,
        "hidden",
        2 * (N + U) * E * H,
        [((N + U, H), BF), ((N + U, E), BF), ((16, E), BF), ((E, H), BF)],
        near,
        pos_feat,
        w_in,
    )
    up, down = shift(after(up, hid), 1), shift(after(down, hid), -1)
    users += [up, down]
    near_emb, pemb, w_out = in_vmem(
        embed_kernel, "embed", 2 * (N + U) * E * H, [((N, E), BF), ((U, E), BF), ((H, E), BF)], hid, w_out
    )
    up, down = shift(after(up, near_emb), 1), shift(after(down, near_emb), -1)
    users += [up, down]
    far_hid, far_emb, nid, bias = in_vmem(
        far_kernel,
        "far",
        4 * N * E * H,
        [((N, H), BF), ((N, E), BF), ((NN, 128), F32), ((NN, 128), F32)],
        tail,
        far,
        w_in,
        w_out,
        logq_table.reshape(8, 128),
    )
    users += [shift(after(up, far_emb), 1)]
    none = jnp.zeros((NZ, U), F32)
    ks = tuple(range(NZ))
    tloc, tot, pexp, kept_a = score(ks[:FIRST], near_emb, far_emb, nid, bias, pemb, none, none, users)
    tloc, tot, _, kept_b = score(ks[FIRST:], near_emb, far_emb, nid, bias, pemb, tloc, tot, users)
    tot = sum_over_z(tot, ((1, 6, 7), (2,)), F32)
    keep, send, g, pterm = grads(tot, tloc, pexp, near_emb, far_emb, pemb, kept_a, kept_b, users)
    args = (g, feat, far, w_out, hid, far_hid)
    theirs_g = backward(False, *args)
    half, other, user = all_reduce(backward(True, *args), theirs_g, keep, send)
    w_in_grad, w_out_grad = finish(False, other, *finish(True, half))
    return user + pterm, w_in_grad, w_out_grad


def solution(mesh):
    rows = P(AXES, None)
    ids = P(AXES)
    return jax.shard_map(
        on_device,
        mesh=Mesh(mesh.devices.reshape(SIZES), AXES),
        in_specs=(rows, rows, ids, rows, ids, ids, P(), P(), P()),
        out_specs=(rows, P(), P()),
        check_vma=False,
    )
```

```python
import functools

import jax
import jax.numpy as jnp
from jax import lax
from jax.experimental import pallas as pl
from jax.experimental.pallas import tpu as pltpu
from jax.sharding import Mesh, PartitionSpec as P

AXES = ("x_lo", "z", "x_hi", "y", "core")
SIZES = (2, 8, 2, 4, 2)
BF, F32, I32 = jnp.bfloat16, jnp.float32, jnp.int32
SCALE = 0.125
SMALL = 2.0**-64
E, H, U, N = 256, 2048, 256, 512
NN = 2 * N
ROWS = NN + U
TILE = 256
CHUNKS = H // TILE
NZ = 8
OFFSETS = (0, -1, 1, -2, 2, -3, 3, 4)
FIRST = 5
VMEM_LIMIT = 24 * 1024 * 1024

WIDE = 512
NT = (((1,), (1,)), ((), ()))
TN = (((0,), (0,)), ((), ()))


def params(limit=VMEM_LIMIT):
    return pltpu.CompilerParams(vmem_limit_bytes=limit)


def cost(flops, nbytes, trans=0):
    return pl.CostEstimate(flops=int(flops), bytes_accessed=int(nbytes), transcendentals=int(trans))


def whole(shape):
    return pl.BlockSpec(shape, lambda *_: (0,) * len(shape))


def mm(a, b):
    return jnp.dot(a, b, preferred_element_type=F32)


def start(src, dst, sem):
    copy = pltpu.make_async_copy(src, dst, sem)
    copy.start()
    return copy


def pack_kernel(user_hbm, pid_hbm, feat_hbm, nid_hbm, bucket_hbm, mine_ref, near_ref, pid_ref, nid_ref, bucket_ref, sems):
    copies = [
        start(pid_hbm, pid_ref, sems.at[0]),
        start(nid_hbm, nid_ref, sems.at[1]),
        start(bucket_hbm, bucket_ref, sems.at[2]),
        start(user_hbm, mine_ref.at[0:U], sems.at[3]),
        start(feat_hbm, near_ref.at[0:N], sems.at[4]),
    ]
    row = lax.broadcasted_iota(I32, (16, E), 0)

    def tail(digits):
        out = jnp.zeros((16, E), F32)
        for i, digit in enumerate(digits):
            out = jnp.where(row == i, digit.astype(F32), out)
        return out.astype(BF)

    def digits(ids, bits):
        ids = [ids[:, i : i + 256] for i in range(0, ids.shape[1], 256)]
        return [i >> bits for i in ids] + [i & (2**bits - 1) for i in ids]

    for copy in copies[:3]:
        copy.wait()
    mine_ref[U : U + 16] = tail(digits(pid_ref[...], 6))
    near_ref[N : N + 16] = tail(digits(nid_ref[...], 6) + digits(bucket_ref[...], 5))
    for copy in copies[3:]:
        copy.wait()


def pack(user_emb, pos_id, neg_feat, neg_id, neg_bucket):
    vm = pl.BlockSpec(memory_space=pltpu.VMEM)
    return pl.pallas_call(
        pack_kernel,
        in_specs=[pl.BlockSpec(memory_space=pltpu.HBM)] * 5,
        out_specs=[vm] * 2,
        out_shape=[jax.ShapeDtypeStruct((U + 16, E), BF), jax.ShapeDtypeStruct((N + 16, E), BF)],
        scratch_shapes=[
            pltpu.VMEM((1, U), I32),
            pltpu.VMEM((1, N), I32),
            pltpu.VMEM((1, N), I32),
            pltpu.SemaphoreType.DMA((5,)),
        ],
        compiler_params=params(60 * 1024 * 1024),
        cost_estimate=cost(0, 1e6),
        name="pack",
    )(user_emb, pos_id.reshape(1, U), neg_feat, neg_id.reshape(1, N), neg_bucket.reshape(1, N))


def hidden(feat, w_in_ref):
    return jnp.maximum(mm(feat, w_in_ref[...]), 0.0).astype(BF)


def hidden_kernel(near_ref, pos_ref, w_in_ref, hid_ref, feat_ref, tail_ref, w_in_out):
    for m, feat in enumerate((near_ref[0:TILE], near_ref[TILE:N], pos_ref[...])):
        rows = slice(m * TILE, (m + 1) * TILE)
        feat_ref[rows] = feat
        hid_ref[rows] = hidden(feat, w_in_ref)
    tail_ref[...] = near_ref[N : N + 16]
    w_in_out[...] = w_in_ref[...]


def embed_kernel(hid_ref, w_out_ref, emb_ref, pemb_ref, w_out_out):
    w_out_out[...] = w_out_ref[...]
    for m, (ref, first) in enumerate([(emb_ref, 0), (emb_ref, TILE), (pemb_ref, 0)]):
        hid = hid_ref[m * TILE : (m + 1) * TILE]
        ref[first : first + TILE] = mm(hid, w_out_ref[...]).astype(BF)


def far_kernel(near_tail, far_ref, w_in_ref, w_out_ref, table_ref, hid_ref, emb_ref, nid_ref, bias_ref):
    lane = lax.broadcasted_iota(I32, (TILE, 128), 1).astype(F32)
    for side, tail in enumerate((near_tail[...], far_ref[N : N + 16])):
        tail = jnp.concatenate([tail.astype(F32), jnp.zeros((112, E), F32)], axis=0).T
        for block in range(2):
            rows = slice((2 * side + block) * TILE, (2 * side + block + 1) * TILE)
            nid = tail[:, block : block + 1] * 64.0 + tail[:, block + 2 : block + 3]
            nid_ref[rows] = jnp.broadcast_to(nid, (TILE, 128))
            bucket = tail[:, block + 4 : block + 5] * 32.0 + tail[:, block + 6 : block + 7]
            found = jnp.zeros((TILE, 128), F32)
            for b in range(8):
                found = found + jnp.where(bucket == lane + 128.0 * b, table_ref[b : b + 1], 0.0)
            bias_ref[rows] = jnp.broadcast_to(jnp.sum(found, axis=1, keepdims=True), (TILE, 128))
    for m in range(N // TILE):
        rows = slice(m * TILE, (m + 1) * TILE)
        hid = hidden(far_ref[rows], w_in_ref)
        hid_ref[rows] = hid
        emb_ref[rows] = mm(hid, w_out_ref[...]).astype(BF)


def in_vmem(kernel, name, flops, outs, *args):
    vm = pl.BlockSpec(memory_space=pltpu.VMEM)
    return pl.pallas_call(
        kernel,
        in_specs=[vm] * len(args),
        out_specs=[vm] * len(outs),
        out_shape=[jax.ShapeDtypeStruct(shape, dtype) for shape, dtype in outs],
        compiler_params=params(14 * 1024 * 1024),
        cost_estimate=cost(flops, 4e6),
        name=name,
    )(*args)


def twice(x):
    return jnp.concatenate([x, x], axis=1)


def home(z, k):
    return (z + OFFSETS[k] + NZ) & (NZ - 1)


def score_kernel(ks, near_emb, far_emb, nid_ref, bias_ref, pemb_ref, tloc_in, tin_in, *rest):
    users = rest[: len(ks)]
    tloc_ref, tin_ref, pexp_ref, kept_ref, kf = rest[len(ks) :]
    z = lax.axis_index("z")
    tloc_ref[...] = tloc_in[...]
    tin_ref[...] = tin_in[...]
    if ks[0] == 0:
        prod = users[0][0:U].astype(F32) * pemb_ref[...].astype(F32)
        prod = (prod[:, 0:128] + prod[:, 128:256]).T
        pexp_ref[...] = jnp.exp(SCALE * jnp.sum(prod, axis=0, keepdims=True))
    else:
        pexp_ref[...] = jnp.zeros_like(pexp_ref)
    for i, k in enumerate(ks):
        u = (users[i][0:U].astype(F32) * SCALE).astype(BF)
        tail = users[i][U : U + 16].astype(F32)
        pid = tail[0:1] * 64.0 + tail[1:2]
        total = jnp.zeros((8, U), F32)
        for m in range(NN // TILE):
            rows = slice(m * TILE, (m + 1) * TILE)
            emb = near_emb[rows] if m < 2 else far_emb[(m - 2) * TILE : (m - 1) * TILE]
            sc = lax.dot_general(emb, u, NT, preferred_element_type=F32) - twice(bias_ref[rows])
            kept = jnp.where(twice(nid_ref[rows]) != pid, jnp.exp(sc), 0.0)
            kf[rows] = kept
            total = total + jnp.sum(kept.reshape(TILE // 8, 8, U), axis=0)
        t = jnp.sum(total, axis=0, keepdims=True)
        shrink = jnp.where(t > 1.0, SMALL, 1.0)
        inv = jnp.where(t > 0.0, 1.0 / (t * shrink), 0.0)
        for m in range(NN // TILE):
            rows = slice(m * TILE, (m + 1) * TILE)
            kept_ref[rows, i * U : (i + 1) * U] = ((kf[rows] * shrink) * inv).astype(BF)
        row = pl.ds(home(z, k), 1)
        tloc_ref[row, :] = t
        tin_ref[row, :] = t + pexp_ref[...] if k == 0 else t


def score(ks, near_emb, far_emb, nid, bias, pemb, tloc, tin, users):
    vm = pl.BlockSpec(memory_space=pltpu.VMEM)
    n = len(ks)
    return pl.pallas_call(
        functools.partial(score_kernel, ks),
        in_specs=[vm] * (7 + n),
        out_specs=[vm] * 4,
        out_shape=[
            jax.ShapeDtypeStruct((NZ, U), F32),
            jax.ShapeDtypeStruct((NZ, U), F32),
            jax.ShapeDtypeStruct((1, U), F32),
            jax.ShapeDtypeStruct((NN, n * U), BF),
        ],
        scratch_shapes=[pltpu.VMEM((NN, U), F32)],
        compiler_params=params(14 * 1024 * 1024),
        cost_estimate=cost(2 * n * U * NN * E, 5e6, n * U * NN),
        name="score",
    )(near_emb, far_emb, nid, bias, pemb, tloc, tin, *[users[k] for k in ks])


def grad_kernel(tot_ref, tloc_ref, pexp_ref, near_emb, far_emb, pemb_ref, kept_a, kept_b, *rest):
    users = rest[:NZ]
    keep_ref, send_ref, g_ref, pterm_ref, wu, ratio, rel = rest[NZ:]
    z = lax.axis_index("z")
    tot = tot_ref[...]
    shrink = jnp.where(tot > 1.0, SMALL, 1.0)
    ratio[...] = (tloc_ref[...] * shrink) * (1.0 / (tot * shrink))
    own = tot_ref[pl.ds(z, 1), :]
    shrink = jnp.where(own > 1.0, SMALL, 1.0)
    pprob = (pexp_ref[...] * shrink) * (1.0 / (own * shrink))
    rel[...] = jnp.zeros_like(rel)
    for k in range(NZ):
        rel[k : k + 1] = SCALE * ratio[pl.ds(home(z, k), 1), :]
    rel[NZ : NZ + 1] = SCALE * (pprob - 1.0)
    cols = rel[...].T
    for k in range(NZ):
        wu[k * U : (k + 1) * U] = (users[k][0:U].astype(F32) * cols[:, k : k + 1]).astype(BF)
    coef = cols[:, NZ : NZ + 1]
    g_ref[N : N + U] = (users[0][0:U].astype(F32) * coef).astype(BF)
    pterm_ref[...] = pemb_ref[...].astype(F32) * coef
    for k in range(NZ):
        kept, i = (kept_a, k) if k < FIRST else (kept_b, k - FIRST)
        cols_k = slice(i * U, (i + 1) * U)
        ug = lax.dot_general(kept[0:N, cols_k], near_emb[...], TN, preferred_element_type=F32)
        ug = ug + lax.dot_general(kept[N:NN, cols_k], far_emb[...], TN, preferred_element_type=F32)
        apart = jnp.bitwise_xor(home(z, k), z)
        place = (apart & 2) + (apart >> 2)
        (send_ref if OFFSETS[k] % 2 else keep_ref)[place] = (ug * cols[:, k : k + 1]).astype(BF)
    for m in range(NN // TILE):
        rows = slice(m * TILE, (m + 1) * TILE)
        g = mm(kept_a[rows], wu[0 : FIRST * U]) + mm(kept_b[rows], wu[FIRST * U :])
        first = m * TILE if m < 2 else m * TILE + U
        g_ref[first : first + TILE] = g.astype(BF)


def grads(tot, tloc, pexp, near_emb, far_emb, pemb, kept_a, kept_b, users):
    vm = pl.BlockSpec(memory_space=pltpu.VMEM)
    return pl.pallas_call(
        grad_kernel,
        in_specs=[vm] * (8 + NZ),
        out_specs=[vm] * 4,
        out_shape=[
            jax.ShapeDtypeStruct((NZ // 2, U, E), BF),
            jax.ShapeDtypeStruct((NZ // 2, U, E), BF),
            jax.ShapeDtypeStruct((ROWS, E), BF),
            jax.ShapeDtypeStruct((U, E), F32),
        ],
        scratch_shapes=[
            pltpu.VMEM((NZ * U, E), BF),
            pltpu.VMEM((NZ, U), F32),
            pltpu.VMEM((128, U), F32),
        ],
        compiler_params=params(),
        cost_estimate=cost(4 * NZ * U * NN * E, 8e6),
        name="grads",
    )(tot, tloc, pexp, near_emb, far_emb, pemb, kept_a, kept_b, *users)


def order():
    core = lax.axis_index("core")
    xx, y = lax.axis_index("x_hi") * 2 + lax.axis_index("x_lo"), lax.axis_index("y")
    return core, jnp.where(core == 0, xx, y), jnp.where(core == 0, y, xx)


def back_kernel(mine, g_ref, feat_ref, far_ref, w_out_ref, hid_ref, far_hid, out_ref):
    core, first, second = order()
    if not mine:
        core, first, second = 1 - core, second, first
    for c in range(2):
        cols = pl.ds(pl.multiple_of(core * (H // 2) + c * WIDE, WIDE), WIDE)
        w_in = w_out = 0.0
        for rows, feat, hid in ((slice(0, N + U), feat_ref, hid_ref), (slice(N + U, ROWS), far_ref, far_hid)):
            hid = hid[:, cols]
            g = g_ref[rows]
            back = lax.dot_general(g, w_out_ref[cols], NT, preferred_element_type=F32)
            back = jnp.where(hid > 0, back, 0.0).astype(BF)
            w_in += lax.dot_general(feat[0 : g.shape[0]], back, TN, preferred_element_type=F32)
            w_out += lax.dot_general(hid, g, TN, preferred_element_type=F32)
        w_in, w_out = w_in.astype(BF), w_out.astype(BF)
        for t in range(2):
            for half in range(2):
                inner = jnp.bitwise_xor(second, 2 * t + half)
                rows = slice(half * 128, (half + 1) * 128)
                out_ref[jnp.bitwise_xor(first, c), inner] = w_in[rows, t * TILE : (t + 1) * TILE]
                rows = slice(t * TILE + half * 128, t * TILE + (half + 1) * 128)
                out_ref[jnp.bitwise_xor(first, 2 + c), inner] = w_out[rows]


def backward(mine, *args):
    return in_vmem(
        functools.partial(back_kernel, mine), "backward", 3 * ROWS * E * H, [((4, 4, 128, TILE), BF)], *args
    )[0]


def finish_kernel(mine, x_ref, *rest):
    w_in_hbm, w_out_hbm, a, b, sems = rest[-5:]
    core, first, second = order()
    if not mine:
        core, first, second = 1 - core, second, first
    copies = []
    for c in range(2):
        for t in range(2):
            for half in range(2):
                inner = jnp.bitwise_xor(second, 2 * t + half)
                start_t = c * WIDE + t * TILE
                cols = slice(start_t, start_t + TILE)
                a[half * 128 : (half + 1) * 128, cols] = x_ref[jnp.bitwise_xor(first, c), inner].astype(F32)
                rows = slice(start_t + half * 128, start_t + (half + 1) * 128)
                b[rows] = x_ref[jnp.bitwise_xor(first, 2 + c), inner].astype(F32)
        here = pl.ds(c * WIDE, WIDE)
        there = pl.ds(pl.multiple_of(core * (H // 2) + c * WIDE, WIDE), WIDE)
        copies.append(start(a.at[:, here], w_in_hbm.at[:, there], sems.at[2 * c]))
        copies.append(start(b.at[here], w_out_hbm.at[there], sems.at[2 * c + 1]))
    for copy in copies:
        copy.wait()


def finish(mine, x, *outs):
    vm, hbm = pl.BlockSpec(memory_space=pltpu.VMEM), pl.BlockSpec(memory_space=pl.ANY)
    return pl.pallas_call(
        functools.partial(finish_kernel, mine),
        in_specs=[vm] + [hbm] * len(outs),
        out_specs=[hbm, hbm],
        out_shape=[jax.ShapeDtypeStruct((E, H), F32), jax.ShapeDtypeStruct((H, E), F32)],
        scratch_shapes=[
            pltpu.VMEM((E, H // 2), F32),
            pltpu.VMEM((H // 2, E), F32),
            pltpu.SemaphoreType.DMA((4,)),
        ],
        input_output_aliases={1: 0, 2: 1} if outs else {},
        compiler_params=params(14 * 1024 * 1024),
        cost_estimate=cost(0, 3e6),
        name="finish",
    )(x, *outs)


def swap(x, axis, k):
    return lax.ppermute(x, axis, [(i, i ^ k) for i in range(SIZES[AXES.index(axis)])])


def after(x, *needed):
    return lax.optimization_barrier((x, *needed))[0]


def shift(x, by):
    return lax.ppermute(x, "z", [(i, (i + by) % NZ) for i in range(NZ)])


def to_core(x, core):
    return lax.ppermute(x, "core", [(1 - core, core)])


def swap_on_core_1(x, k):
    places = [(x_lo, z, x_hi, y) for x_lo in range(2) for z in range(NZ) for x_hi in range(2) for y in range(4)]
    pairs = [(device(a, z, b, y, 1), device(a, z ^ k, b, y, 1)) for a, z, b, y in places]
    return lax.ppermute(x, AXES, pairs)


def device(x_lo, z, x_hi, y, core):
    return (((x_lo * 8 + z) * 2 + x_hi) * 4 + y) * 2 + core


def plane_swap(x, k, x_core):
    pairs = []
    for z in range(8):
        for xx in range(4):
            for y in range(4):
                for core in range(2):
                    to_x, to_y = (xx ^ k, y) if core == x_core else (xx, y ^ k)
                    pairs.append(
                        (device(xx & 1, z, xx >> 1, y, core), device(to_x & 1, z, to_x >> 1, to_y, core))
                    )
    return lax.ppermute(x, AXES, pairs)


def add(*terms):
    return sum(t.astype(F32) for t in terms)


def sum_over_z(x, rounds, dtype):
    for ks in rounds:
        sent = x.astype(dtype)
        terms = [t.astype(F32) for t in [sent] + [swap(sent, "z", k) for k in ks]]
        while len(terms) > 1:
            terms = [a + b for a, b in zip(terms[::2], terms[1::2])]
        x = terms[0]
    return x


def all_reduce(mine, theirs, keep, send):
    keep_0, send_0 = to_core(keep, 1), to_core(send, 1)
    half = add(mine, swap(theirs, "core", 1)).astype(BF)
    half, keep_0, send_0 = lax.optimization_barrier((half, keep_0, send_0))
    quarter = add(half[0], *[plane_swap(half[k], k, 0) for k in (1, 2, 3)]).astype(BF)
    keep = add(keep, swap_on_core_1(send, 1)).astype(BF)
    keep_0 = add(keep_0, swap_on_core_1(send_0, 1)).astype(BF)
    quarter, keep, keep_0 = lax.optimization_barrier((quarter, keep, keep_0))
    part = add(quarter[0], *[plane_swap(quarter[k], k, 1) for k in (1, 2, 3)])
    part = sum_over_z(part, ((1,), (2, 4, 6)), BF).astype(BF)
    part, keep, keep_0 = lax.optimization_barrier((part, keep, keep_0))
    quarter = jnp.stack([part] + [plane_swap(part, k, 1) for k in (1, 2, 3)])
    both = [jnp.stack([keep[i], keep_0[i]]) for i in range(4)]
    both = add(both[0], *[swap_on_core_1(both[i], k) for i, k in ((1, 4), (2, 2), (3, 6))])
    others = [plane_swap(quarter, k, 0) for k in (1, 2, 3)]
    others, both = lax.optimization_barrier((others, both))
    half = jnp.stack([quarter] + others)
    user = jnp.where(lax.axis_index("core") == 1, both[0], to_core(both[1].astype(BF), 0).astype(F32))
    return half, swap(half, "core", 1), user


def on_device(user_emb, pos_feat, pos_id, neg_feat, neg_id, neg_bucket, logq_table, w_in, w_out):
    mine, near = pack(user_emb, pos_id, neg_feat, neg_id, neg_bucket)
    up, down = shift(mine, 1), shift(mine, -1)
    far = swap(near, "x_lo", 1)
    users = [mine, up, down]
    hid, feat, tail, w_in = in_vmem(
        hidden_kernel,
        "hidden",
        2 * (N + U) * E * H,
        [((N + U, H), BF), ((N + U, E), BF), ((16, E), BF), ((E, H), BF)],
        near,
        pos_feat,
        w_in,
    )
    up, down = shift(after(up, hid), 1), shift(after(down, hid), -1)
    users += [up, down]
    near_emb, pemb, w_out = in_vmem(
        embed_kernel, "embed", 2 * (N + U) * E * H, [((N, E), BF), ((U, E), BF), ((H, E), BF)], hid, w_out
    )
    up, down = shift(after(up, near_emb), 1), shift(after(down, near_emb), -1)
    users += [up, down]
    far_hid, far_emb, nid, bias = in_vmem(
        far_kernel,
        "far",
        4 * N * E * H,
        [((N, H), BF), ((N, E), BF), ((NN, 128), F32), ((NN, 128), F32)],
        tail,
        far,
        w_in,
        w_out,
        logq_table.reshape(8, 128),
    )
    users += [shift(after(up, far_emb), 1)]
    none = jnp.zeros((NZ, U), F32)
    ks = tuple(range(NZ))
    tloc, tot, pexp, kept_a = score(ks[:FIRST], near_emb, far_emb, nid, bias, pemb, none, none, users)
    tloc, tot, _, kept_b = score(ks[FIRST:], near_emb, far_emb, nid, bias, pemb, tloc, tot, users)
    tot = sum_over_z(tot, ((1, 6, 7), (2,)), F32)
    keep, send, g, pterm = grads(tot, tloc, pexp, near_emb, far_emb, pemb, kept_a, kept_b, users)
    args = (g, feat, far, w_out, hid, far_hid)
    theirs_g = backward(False, *args)
    half, other, user = all_reduce(backward(True, *args), theirs_g, keep, send)
    w_in_grad, w_out_grad = finish(False, other, *finish(True, half))
    return user + pterm, w_in_grad, w_out_grad


def solution(mesh):
    rows = P(AXES, None)
    ids = P(AXES)
    return jax.shard_map(
        on_device,
        mesh=Mesh(mesh.devices.reshape(SIZES), AXES),
        in_specs=(rows, rows, ids, rows, ids, ids, P(), P(), P()),
        out_specs=(rows, P(), P()),
        check_vma=False,
    )
```

```python
import functools

import jax
import jax.numpy as jnp
from jax import lax
from jax.experimental import pallas as pl
from jax.experimental.pallas import tpu as pltpu
from jax.sharding import Mesh, PartitionSpec as P

AXES = ("x_lo", "z", "x_hi", "y", "core")
SIZES = (2, 8, 2, 4, 2)
BF, F32, I32 = jnp.bfloat16, jnp.float32, jnp.int32
SCALE = 0.125
SMALL = 2.0**-64
E, H, U, N = 256, 2048, 256, 512
NN = 2 * N
ROWS = NN + U
TILE = 256
CHUNKS = H // TILE
NZ = 8
OFFSETS = (0, -1, 1, -2, 2, -3, 3, 4)
FIRST = 7
VMEM_LIMIT = 24 * 1024 * 1024

WIDE = 512
NT = (((1,), (1,)), ((), ()))
TN = (((0,), (0,)), ((), ()))


def params(limit=VMEM_LIMIT):
    return pltpu.CompilerParams(vmem_limit_bytes=limit)


def cost(flops, nbytes, trans=0):
    return pl.CostEstimate(flops=int(flops), bytes_accessed=int(nbytes), transcendentals=int(trans))


def whole(shape):
    return pl.BlockSpec(shape, lambda *_: (0,) * len(shape))


def mm(a, b):
    return jnp.dot(a, b, preferred_element_type=F32)


def start(src, dst, sem):
    copy = pltpu.make_async_copy(src, dst, sem)
    copy.start()
    return copy


def pack_kernel(user_hbm, pid_hbm, feat_hbm, nid_hbm, bucket_hbm, mine_ref, near_ref, pid_ref, nid_ref, bucket_ref, sems):
    copies = [
        start(pid_hbm, pid_ref, sems.at[0]),
        start(nid_hbm, nid_ref, sems.at[1]),
        start(bucket_hbm, bucket_ref, sems.at[2]),
        start(user_hbm, mine_ref.at[0:U], sems.at[3]),
        start(feat_hbm, near_ref.at[0:N], sems.at[4]),
    ]
    row = lax.broadcasted_iota(I32, (16, E), 0)

    def tail(digits):
        out = jnp.zeros((16, E), F32)
        for i, digit in enumerate(digits):
            out = jnp.where(row == i, digit.astype(F32), out)
        return out.astype(BF)

    def digits(ids, bits):
        ids = [ids[:, i : i + 256] for i in range(0, ids.shape[1], 256)]
        return [i >> bits for i in ids] + [i & (2**bits - 1) for i in ids]

    for copy in copies[:3]:
        copy.wait()
    mine_ref[U : U + 16] = tail(digits(pid_ref[...], 6))
    near_ref[N : N + 16] = tail(digits(nid_ref[...], 6) + digits(bucket_ref[...], 5))
    for copy in copies[3:]:
        copy.wait()


def pack(user_emb, pos_id, neg_feat, neg_id, neg_bucket):
    vm = pl.BlockSpec(memory_space=pltpu.VMEM)
    return pl.pallas_call(
        pack_kernel,
        in_specs=[pl.BlockSpec(memory_space=pltpu.HBM)] * 5,
        out_specs=[vm] * 2,
        out_shape=[jax.ShapeDtypeStruct((U + 16, E), BF), jax.ShapeDtypeStruct((N + 16, E), BF)],
        scratch_shapes=[
            pltpu.VMEM((1, U), I32),
            pltpu.VMEM((1, N), I32),
            pltpu.VMEM((1, N), I32),
            pltpu.SemaphoreType.DMA((5,)),
        ],
        compiler_params=params(60 * 1024 * 1024),
        cost_estimate=cost(1e10, 1e6),
        name="pack",
    )(user_emb, pos_id.reshape(1, U), neg_feat, neg_id.reshape(1, N), neg_bucket.reshape(1, N))


def hidden(feat, w_in_ref):
    return jnp.maximum(mm(feat, w_in_ref[...]), 0.0).astype(BF)


def hidden_kernel(near_ref, pos_ref, w_in_ref, hid_ref, feat_ref, w_in_out):
    for m, feat in enumerate((near_ref[0:TILE], near_ref[TILE:N], pos_ref[...])):
        rows = slice(m * TILE, (m + 1) * TILE)
        feat_ref[rows] = feat
        hid_ref[rows] = hidden(feat, w_in_ref)
    w_in_out[...] = w_in_ref[...]


def embed_kernel(hid_ref, w_out_ref, emb_ref, pemb_ref, w_out_out):
    w_out_out[...] = w_out_ref[...]
    for m, (ref, first) in enumerate([(emb_ref, 0), (emb_ref, TILE), (pemb_ref, 0)]):
        hid = hid_ref[m * TILE : (m + 1) * TILE]
        ref[first : first + TILE] = mm(hid, w_out_ref[...]).astype(BF)


def far_kernel(near_ref, far_ref, w_in_ref, w_out_ref, table_ref, hid_ref, emb_ref, nid_ref, bias_ref):
    lane = lax.broadcasted_iota(I32, (TILE, 128), 1).astype(F32)
    for side, tail in enumerate((near_ref[N : N + 16], far_ref[N : N + 16])):
        tail = jnp.concatenate([tail.astype(F32), jnp.zeros((112, E), F32)], axis=0).T
        for block in range(2):
            rows = slice((2 * side + block) * TILE, (2 * side + block + 1) * TILE)
            nid = tail[:, block : block + 1] * 64.0 + tail[:, block + 2 : block + 3]
            nid_ref[rows] = jnp.broadcast_to(nid, (TILE, 128))
            bucket = tail[:, block + 4 : block + 5] * 32.0 + tail[:, block + 6 : block + 7]
            found = jnp.zeros((TILE, 128), F32)
            for b in range(8):
                found = found + jnp.where(bucket == lane + 128.0 * b, table_ref[b : b + 1], 0.0)
            bias_ref[rows] = jnp.broadcast_to(jnp.sum(found, axis=1, keepdims=True), (TILE, 128))
    for m in range(N // TILE):
        rows = slice(m * TILE, (m + 1) * TILE)
        hid = hidden(far_ref[rows], w_in_ref)
        hid_ref[rows] = hid
        emb_ref[rows] = mm(hid, w_out_ref[...]).astype(BF)


def in_vmem(kernel, name, flops, outs, *args):
    vm = pl.BlockSpec(memory_space=pltpu.VMEM)
    return pl.pallas_call(
        kernel,
        in_specs=[vm] * len(args),
        out_specs=[vm] * len(outs),
        out_shape=[jax.ShapeDtypeStruct(shape, dtype) for shape, dtype in outs],
        compiler_params=params(14 * 1024 * 1024),
        cost_estimate=cost(flops, 4e6),
        name=name,
    )(*args)


def twice(x):
    return jnp.concatenate([x, x], axis=1)


def home(z, k):
    return (z + OFFSETS[k] + NZ) & (NZ - 1)


def score_kernel(ks, near_emb, far_emb, nid_ref, bias_ref, pemb_ref, tloc_in, tin_in, *rest):
    users = rest[: len(ks)]
    tloc_ref, tin_ref, pexp_ref, kept_ref, kf = rest[len(ks) :]
    z = lax.axis_index("z")
    tloc_ref[...] = tloc_in[...]
    tin_ref[...] = tin_in[...]
    if ks[0] == 0:
        prod = users[0][0:U].astype(F32) * pemb_ref[...].astype(F32)
        prod = (prod[:, 0:128] + prod[:, 128:256]).T
        pexp_ref[...] = jnp.exp(SCALE * jnp.sum(prod, axis=0, keepdims=True))
    else:
        pexp_ref[...] = jnp.zeros_like(pexp_ref)
    for i, k in enumerate(ks):
        u = (users[i][0:U].astype(F32) * SCALE).astype(BF)
        tail = users[i][U : U + 16].astype(F32)
        pid = tail[0:1] * 64.0 + tail[1:2]
        total = jnp.zeros((8, U), F32)
        for m in range(NN // TILE):
            rows = slice(m * TILE, (m + 1) * TILE)
            emb = near_emb[rows] if m < 2 else far_emb[(m - 2) * TILE : (m - 1) * TILE]
            sc = lax.dot_general(emb, u, NT, preferred_element_type=F32) - twice(bias_ref[rows])
            kept = jnp.where(twice(nid_ref[rows]) != pid, jnp.exp(sc), 0.0)
            kf[rows] = kept
            total = total + jnp.sum(kept.reshape(TILE // 8, 8, U), axis=0)
        t = jnp.sum(total, axis=0, keepdims=True)
        shrink = jnp.where(t > 1.0, SMALL, 1.0)
        inv = jnp.where(t > 0.0, 1.0 / (t * shrink), 0.0)
        for m in range(NN // TILE):
            rows = slice(m * TILE, (m + 1) * TILE)
            kept_ref[rows, i * U : (i + 1) * U] = ((kf[rows] * shrink) * inv).astype(BF)
        row = pl.ds(home(z, k), 1)
        tloc_ref[row, :] = t
        tin_ref[row, :] = t + pexp_ref[...] if k == 0 else t


def score(ks, near_emb, far_emb, nid, bias, pemb, tloc, tin, users):
    vm = pl.BlockSpec(memory_space=pltpu.VMEM)
    n = len(ks)
    return pl.pallas_call(
        functools.partial(score_kernel, ks),
        in_specs=[vm] * (7 + n),
        out_specs=[vm] * 4,
        out_shape=[
            jax.ShapeDtypeStruct((NZ, U), F32),
            jax.ShapeDtypeStruct((NZ, U), F32),
            jax.ShapeDtypeStruct((1, U), F32),
            jax.ShapeDtypeStruct((NN, n * U), BF),
        ],
        scratch_shapes=[pltpu.VMEM((NN, U), F32)],
        compiler_params=params(14 * 1024 * 1024),
        cost_estimate=cost(2 * n * U * NN * E, 5e6, n * U * NN),
        name="score",
    )(near_emb, far_emb, nid, bias, pemb, tloc, tin, *[users[k] for k in ks])


def grad_kernel(tot_ref, tloc_ref, pexp_ref, near_emb, far_emb, pemb_ref, kept_a, kept_b, *rest):
    users = rest[:NZ]
    keep_ref, send_ref, g_ref, pterm_ref, wu, ratio, rel = rest[NZ:]
    z = lax.axis_index("z")
    tot = tot_ref[...]
    shrink = jnp.where(tot > 1.0, SMALL, 1.0)
    ratio[...] = (tloc_ref[...] * shrink) * (1.0 / (tot * shrink))
    own = tot_ref[pl.ds(z, 1), :]
    shrink = jnp.where(own > 1.0, SMALL, 1.0)
    pprob = (pexp_ref[...] * shrink) * (1.0 / (own * shrink))
    rel[...] = jnp.zeros_like(rel)
    for k in range(NZ):
        rel[k : k + 1] = SCALE * ratio[pl.ds(home(z, k), 1), :]
    rel[NZ : NZ + 1] = SCALE * (pprob - 1.0)
    cols = rel[...].T
    for k in range(NZ):
        wu[k * U : (k + 1) * U] = (users[k][0:U].astype(F32) * cols[:, k : k + 1]).astype(BF)
    coef = cols[:, NZ : NZ + 1]
    g_ref[N : N + U] = (users[0][0:U].astype(F32) * coef).astype(BF)
    pterm_ref[...] = pemb_ref[...].astype(F32) * coef
    for k in range(NZ):
        kept, i = (kept_a, k) if k < FIRST else (kept_b, k - FIRST)
        cols_k = slice(i * U, (i + 1) * U)
        ug = lax.dot_general(kept[0:N, cols_k], near_emb[...], TN, preferred_element_type=F32)
        ug = ug + lax.dot_general(kept[N:NN, cols_k], far_emb[...], TN, preferred_element_type=F32)
        apart = jnp.bitwise_xor(home(z, k), z)
        place = (apart & 2) + (apart >> 2)
        (send_ref if OFFSETS[k] % 2 else keep_ref)[place] = (ug * cols[:, k : k + 1]).astype(BF)
    for m in range(NN // TILE):
        rows = slice(m * TILE, (m + 1) * TILE)
        g = mm(kept_a[rows], wu[0 : FIRST * U]) + mm(kept_b[rows], wu[FIRST * U :])
        first = m * TILE if m < 2 else m * TILE + U
        g_ref[first : first + TILE] = g.astype(BF)


def grads(tot, tloc, pexp, near_emb, far_emb, pemb, kept_a, kept_b, users):
    vm = pl.BlockSpec(memory_space=pltpu.VMEM)
    return pl.pallas_call(
        grad_kernel,
        in_specs=[vm] * (8 + NZ),
        out_specs=[vm] * 4,
        out_shape=[
            jax.ShapeDtypeStruct((NZ // 2, U, E), BF),
            jax.ShapeDtypeStruct((NZ // 2, U, E), BF),
            jax.ShapeDtypeStruct((ROWS, E), BF),
            jax.ShapeDtypeStruct((U, E), F32),
        ],
        scratch_shapes=[
            pltpu.VMEM((NZ * U, E), BF),
            pltpu.VMEM((NZ, U), F32),
            pltpu.VMEM((128, U), F32),
        ],
        compiler_params=params(),
        cost_estimate=cost(4 * NZ * U * NN * E, 8e6),
        name="grads",
    )(tot, tloc, pexp, near_emb, far_emb, pemb, kept_a, kept_b, *users)


def order():
    core = lax.axis_index("core")
    xx, y = lax.axis_index("x_hi") * 2 + lax.axis_index("x_lo"), lax.axis_index("y")
    return core, jnp.where(core == 0, xx, y), jnp.where(core == 0, y, xx)


def back_kernel(mine, g_ref, feat_ref, far_ref, w_out_ref, hid_ref, far_hid, out_ref):
    core, first, second = order()
    if not mine:
        core, first, second = 1 - core, second, first
    for c in range(2):
        cols = pl.ds(pl.multiple_of(core * (H // 2) + c * WIDE, WIDE), WIDE)
        w_in = w_out = 0.0
        for rows, feat, hid in ((slice(0, N + U), feat_ref, hid_ref), (slice(N + U, ROWS), far_ref, far_hid)):
            hid = hid[:, cols]
            g = g_ref[rows]
            back = lax.dot_general(g, w_out_ref[cols], NT, preferred_element_type=F32)
            back = jnp.where(hid > 0, back, 0.0).astype(BF)
            w_in += lax.dot_general(feat[0 : g.shape[0]], back, TN, preferred_element_type=F32)
            w_out += lax.dot_general(hid, g, TN, preferred_element_type=F32)
        w_in, w_out = w_in.astype(BF), w_out.astype(BF)
        for t in range(2):
            for half in range(2):
                inner = jnp.bitwise_xor(second, 2 * t + half)
                rows = slice(half * 128, (half + 1) * 128)
                out_ref[jnp.bitwise_xor(first, c), inner] = w_in[rows, t * TILE : (t + 1) * TILE]
                rows = slice(t * TILE + half * 128, t * TILE + (half + 1) * 128)
                out_ref[jnp.bitwise_xor(first, 2 + c), inner] = w_out[rows]


def backward(mine, *args):
    return in_vmem(
        functools.partial(back_kernel, mine), "backward", 3 * ROWS * E * H, [((4, 4, 128, TILE), BF)], *args
    )[0]


def finish_kernel(mine, x_ref, *rest):
    w_in_hbm, w_out_hbm, a, b, sems = rest[-5:]
    core, first, second = order()
    if not mine:
        core, first, second = 1 - core, second, first
    copies = []
    for c in range(2):
        for t in range(2):
            for half in range(2):
                inner = jnp.bitwise_xor(second, 2 * t + half)
                start_t = c * WIDE + t * TILE
                cols = slice(start_t, start_t + TILE)
                a[half * 128 : (half + 1) * 128, cols] = x_ref[jnp.bitwise_xor(first, c), inner].astype(F32)
                rows = slice(start_t + half * 128, start_t + (half + 1) * 128)
                b[rows] = x_ref[jnp.bitwise_xor(first, 2 + c), inner].astype(F32)
        here = pl.ds(c * WIDE, WIDE)
        there = pl.ds(pl.multiple_of(core * (H // 2) + c * WIDE, WIDE), WIDE)
        copies.append(start(a.at[:, here], w_in_hbm.at[:, there], sems.at[2 * c]))
        copies.append(start(b.at[here], w_out_hbm.at[there], sems.at[2 * c + 1]))
    for copy in copies:
        copy.wait()


def finish(mine, x, *outs):
    vm, hbm = pl.BlockSpec(memory_space=pltpu.VMEM), pl.BlockSpec(memory_space=pl.ANY)
    return pl.pallas_call(
        functools.partial(finish_kernel, mine),
        in_specs=[vm] + [hbm] * len(outs),
        out_specs=[hbm, hbm],
        out_shape=[jax.ShapeDtypeStruct((E, H), F32), jax.ShapeDtypeStruct((H, E), F32)],
        scratch_shapes=[
            pltpu.VMEM((E, H // 2), F32),
            pltpu.VMEM((H // 2, E), F32),
            pltpu.SemaphoreType.DMA((4,)),
        ],
        input_output_aliases={1: 0, 2: 1} if outs else {},
        compiler_params=params(14 * 1024 * 1024),
        cost_estimate=cost(0, 3e6),
        name="finish",
    )(x, *outs)


def swap(x, axis, k):
    return lax.ppermute(x, axis, [(i, i ^ k) for i in range(SIZES[AXES.index(axis)])])


def after(x, *needed):
    return lax.optimization_barrier((x, *needed))[0]


def shift(x, by):
    return lax.ppermute(x, "z", [(i, (i + by) % NZ) for i in range(NZ)])


def device(x_lo, z, x_hi, y, core):
    return (((x_lo * 8 + z) * 2 + x_hi) * 4 + y) * 2 + core


def plane_swap(x, k, x_core):
    pairs = []
    for z in range(8):
        for xx in range(4):
            for y in range(4):
                for core in range(2):
                    to_x, to_y = (xx ^ k, y) if core == x_core else (xx, y ^ k)
                    pairs.append(
                        (device(xx & 1, z, xx >> 1, y, core), device(to_x & 1, z, to_x >> 1, to_y, core))
                    )
    return lax.ppermute(x, AXES, pairs)


def add(*terms):
    return sum(t.astype(F32) for t in terms)


def sum_over_z(x, rounds, dtype):
    for ks in rounds:
        sent = x.astype(dtype)
        terms = [t.astype(F32) for t in [sent] + [swap(sent, "z", k) for k in ks]]
        while len(terms) > 1:
            terms = [a + b for a, b in zip(terms[::2], terms[1::2])]
        x = terms[0]
    return x


def all_reduce(mine, theirs, keep, send):
    half = add(mine, swap(theirs, "core", 1)).astype(BF)
    quarter = add(half[0], *[plane_swap(half[k], k, 0) for k in (1, 2, 3)]).astype(BF)
    keep = add(keep, swap(send, "z", 1)).astype(BF)
    quarter, keep = lax.optimization_barrier((quarter, keep))
    part = add(quarter[0], *[plane_swap(quarter[k], k, 1) for k in (1, 2, 3)])
    user_2 = swap(keep[2], "z", 2)
    part, user_2 = lax.optimization_barrier((part, user_2))
    part = sum_over_z(part, ((1,), (2, 4, 6)), BF).astype(BF)
    part, keep = lax.optimization_barrier((part, keep))
    quarter = jnp.stack([part] + [plane_swap(part, k, 1) for k in (1, 2, 3)])
    user_6 = swap(keep[3], "z", 6)
    quarter, user_6, keep = lax.optimization_barrier((quarter, user_6, keep))
    others = [plane_swap(quarter, k, 0) for k in (1, 2, 3)]
    user_4 = swap(keep[1], "z", 4)
    others, user_4 = lax.optimization_barrier((others, user_4))
    half = jnp.stack([quarter] + others)
    return half, swap(half, "core", 1), add(keep[0], user_2, user_4, user_6)


def on_device(user_emb, pos_feat, pos_id, neg_feat, neg_id, neg_bucket, logq_table, w_in, w_out):
    mine, near = pack(user_emb, pos_id, neg_feat, neg_id, neg_bucket)
    up, down = shift(mine, 1), shift(mine, -1)
    far = swap(near, "x_lo", 1)
    users = [mine, up, down]
    hid, feat, w_in = in_vmem(
        hidden_kernel,
        "hidden",
        2 * (N + U) * E * H,
        [((N + U, H), BF), ((N + U, E), BF), ((E, H), BF)],
        neg_feat,
        pos_feat,
        w_in,
    )
    up, down = shift(after(up, hid), 1), shift(after(down, hid), -1)
    users += [up, down]
    near_emb, pemb, w_out = in_vmem(
        embed_kernel, "embed", 2 * (N + U) * E * H, [((N, E), BF), ((U, E), BF), ((H, E), BF)], hid, w_out
    )
    up, down = shift(after(up, near_emb), 1), shift(after(down, near_emb), -1)
    users += [up, down]
    far_hid, far_emb, nid, bias = in_vmem(
        far_kernel,
        "far",
        4 * N * E * H,
        [((N, H), BF), ((N, E), BF), ((NN, 128), F32), ((NN, 128), F32)],
        near,
        far,
        w_in,
        w_out,
        logq_table.reshape(8, 128),
    )
    users += [shift(after(up, far_emb), 1)]
    none = jnp.zeros((NZ, U), F32)
    ks = tuple(range(NZ))
    tloc, tot, pexp, kept_a = score(ks[:FIRST], near_emb, far_emb, nid, bias, pemb, none, none, users)
    tloc, tot, _, kept_b = score(ks[FIRST:], near_emb, far_emb, nid, bias, pemb, tloc, tot, users)
    tot = sum_over_z(tot, ((1, 6, 7), (2,)), F32)
    keep, send, g, pterm = grads(tot, tloc, pexp, near_emb, far_emb, pemb, kept_a, kept_b, users)
    args = (g, feat, far, w_out, hid, far_hid)
    theirs_g = backward(False, *args)
    half, other, user = all_reduce(backward(True, *args), theirs_g, keep, send)
    w_in_grad, w_out_grad = finish(False, other, *finish(True, half))
    return user + pterm, w_in_grad, w_out_grad


def solution(mesh):
    rows = P(AXES, None)
    ids = P(AXES)
    return jax.shard_map(
        on_device,
        mesh=Mesh(mesh.devices.reshape(SIZES), AXES),
        in_specs=(rows, rows, ids, rows, ids, ids, P(), P(), P()),
        out_specs=(rows, P(), P()),
        check_vma=False,
    )
```

```python
import functools

import jax
import jax.numpy as jnp
from jax import lax
from jax.experimental import pallas as pl
from jax.experimental.pallas import tpu as pltpu
from jax.sharding import Mesh, PartitionSpec as P

AXES = ("x_lo", "z", "x_hi", "y", "core")
SIZES = (2, 8, 2, 4, 2)
BF, F32, I32 = jnp.bfloat16, jnp.float32, jnp.int32
SCALE = 0.125
SMALL = 2.0**-64
E, H, U, N = 256, 2048, 256, 512
NN = 2 * N
ROWS = NN + U
TILE = 256
CHUNKS = H // TILE
NZ = 8
ORDER = (3, 2, 1)
OFFSETS = (0, -1, 1, -2, 2, -3, 3, 4)
FIRST = 7
VMEM_LIMIT = 24 * 1024 * 1024

WIDE = 512
NT = (((1,), (1,)), ((), ()))
TN = (((0,), (0,)), ((), ()))


def params(limit=VMEM_LIMIT):
    return pltpu.CompilerParams(vmem_limit_bytes=limit)


def cost(flops, nbytes, trans=0):
    return pl.CostEstimate(flops=int(flops), bytes_accessed=int(nbytes), transcendentals=int(trans))


def whole(shape):
    return pl.BlockSpec(shape, lambda *_: (0,) * len(shape))


def mm(a, b):
    return jnp.dot(a, b, preferred_element_type=F32)


def start(src, dst, sem):
    copy = pltpu.make_async_copy(src, dst, sem)
    copy.start()
    return copy


def pack_kernel(user_hbm, pid_hbm, feat_hbm, nid_hbm, bucket_hbm, mine_ref, near_ref, pid_ref, nid_ref, bucket_ref, sems):
    copies = [
        start(pid_hbm, pid_ref, sems.at[0]),
        start(nid_hbm, nid_ref, sems.at[1]),
        start(bucket_hbm, bucket_ref, sems.at[2]),
        start(user_hbm, mine_ref.at[0:U], sems.at[3]),
        start(feat_hbm, near_ref.at[0:N], sems.at[4]),
    ]
    row = lax.broadcasted_iota(I32, (16, E), 0)

    def tail(digits):
        out = jnp.zeros((16, E), F32)
        for i, digit in enumerate(digits):
            out = jnp.where(row == i, digit.astype(F32), out)
        return out.astype(BF)

    def digits(ids, bits):
        ids = [ids[:, i : i + 256] for i in range(0, ids.shape[1], 256)]
        return [i >> bits for i in ids] + [i & (2**bits - 1) for i in ids]

    for copy in copies[:3]:
        copy.wait()
    mine_ref[U : U + 16] = tail(digits(pid_ref[...], 6))
    near_ref[N : N + 16] = tail(digits(nid_ref[...], 6) + digits(bucket_ref[...], 5))
    for copy in copies[3:]:
        copy.wait()


def pack(user_emb, pos_id, neg_feat, neg_id, neg_bucket):
    vm = pl.BlockSpec(memory_space=pltpu.VMEM)
    return pl.pallas_call(
        pack_kernel,
        in_specs=[pl.BlockSpec(memory_space=pltpu.HBM)] * 5,
        out_specs=[vm] * 2,
        out_shape=[jax.ShapeDtypeStruct((U + 16, E), BF), jax.ShapeDtypeStruct((N + 16, E), BF)],
        scratch_shapes=[
            pltpu.VMEM((1, U), I32),
            pltpu.VMEM((1, N), I32),
            pltpu.VMEM((1, N), I32),
            pltpu.SemaphoreType.DMA((5,)),
        ],
        compiler_params=params(60 * 1024 * 1024),
        cost_estimate=cost(1e10, 1e6),
        name="pack",
    )(user_emb, pos_id.reshape(1, U), neg_feat, neg_id.reshape(1, N), neg_bucket.reshape(1, N))


def hidden(feat, w_in_ref):
    return jnp.maximum(mm(feat, w_in_ref[...]), 0.0).astype(BF)


def hidden_kernel(near_ref, pos_ref, w_in_ref, hid_ref, feat_ref, w_in_out):
    for m, feat in enumerate((near_ref[0:TILE], near_ref[TILE:N], pos_ref[...])):
        rows = slice(m * TILE, (m + 1) * TILE)
        feat_ref[rows] = feat
        hid_ref[rows] = hidden(feat, w_in_ref)
    w_in_out[...] = w_in_ref[...]


def embed_kernel(hid_ref, w_out_ref, emb_ref, pemb_ref, w_out_out):
    w_out_out[...] = w_out_ref[...]
    for m, (ref, first) in enumerate([(emb_ref, 0), (emb_ref, TILE), (pemb_ref, 0)]):
        hid = hid_ref[m * TILE : (m + 1) * TILE]
        ref[first : first + TILE] = mm(hid, w_out_ref[...]).astype(BF)


def far_kernel(near_ref, far_ref, w_in_ref, w_out_ref, table_ref, hid_ref, emb_ref, nid_ref, bias_ref):
    lane = lax.broadcasted_iota(I32, (TILE, 128), 1).astype(F32)
    for side, tail in enumerate((near_ref[N : N + 16], far_ref[N : N + 16])):
        tail = jnp.concatenate([tail.astype(F32), jnp.zeros((112, E), F32)], axis=0).T
        for block in range(2):
            rows = slice((2 * side + block) * TILE, (2 * side + block + 1) * TILE)
            nid = tail[:, block : block + 1] * 64.0 + tail[:, block + 2 : block + 3]
            nid_ref[rows] = jnp.broadcast_to(nid, (TILE, 128))
            bucket = tail[:, block + 4 : block + 5] * 32.0 + tail[:, block + 6 : block + 7]
            found = jnp.zeros((TILE, 128), F32)
            for b in range(8):
                found = found + jnp.where(bucket == lane + 128.0 * b, table_ref[b : b + 1], 0.0)
            bias_ref[rows] = jnp.broadcast_to(jnp.sum(found, axis=1, keepdims=True), (TILE, 128))
    for m in range(N // TILE):
        rows = slice(m * TILE, (m + 1) * TILE)
        hid = hidden(far_ref[rows], w_in_ref)
        hid_ref[rows] = hid
        emb_ref[rows] = mm(hid, w_out_ref[...]).astype(BF)


def in_vmem(kernel, name, flops, outs, *args):
    vm = pl.BlockSpec(memory_space=pltpu.VMEM)
    return pl.pallas_call(
        kernel,
        in_specs=[vm] * len(args),
        out_specs=[vm] * len(outs),
        out_shape=[jax.ShapeDtypeStruct(shape, dtype) for shape, dtype in outs],
        compiler_params=params(14 * 1024 * 1024),
        cost_estimate=cost(flops, 4e6),
        name=name,
    )(*args)


def twice(x):
    return jnp.concatenate([x, x], axis=1)


def home(z, k):
    return (z + OFFSETS[k] + NZ) & (NZ - 1)


def score_kernel(ks, near_emb, far_emb, nid_ref, bias_ref, pemb_ref, tloc_in, tin_in, *rest):
    users = rest[: len(ks)]
    tloc_ref, tin_ref, pexp_ref, kept_ref, kf = rest[len(ks) :]
    z = lax.axis_index("z")
    tloc_ref[...] = tloc_in[...]
    tin_ref[...] = tin_in[...]
    if ks[0] == 0:
        prod = users[0][0:U].astype(F32) * pemb_ref[...].astype(F32)
        prod = (prod[:, 0:128] + prod[:, 128:256]).T
        pexp_ref[...] = jnp.exp(SCALE * jnp.sum(prod, axis=0, keepdims=True))
    else:
        pexp_ref[...] = jnp.zeros_like(pexp_ref)
    for i, k in enumerate(ks):
        u = (users[i][0:U].astype(F32) * SCALE).astype(BF)
        tail = users[i][U : U + 16].astype(F32)
        pid = tail[0:1] * 64.0 + tail[1:2]
        total = jnp.zeros((8, U), F32)
        for m in range(NN // TILE):
            rows = slice(m * TILE, (m + 1) * TILE)
            emb = near_emb[rows] if m < 2 else far_emb[(m - 2) * TILE : (m - 1) * TILE]
            sc = lax.dot_general(emb, u, NT, preferred_element_type=F32) - twice(bias_ref[rows])
            kept = jnp.where(twice(nid_ref[rows]) != pid, jnp.exp(sc), 0.0)
            kf[rows] = kept
            total = total + jnp.sum(kept.reshape(TILE // 8, 8, U), axis=0)
        t = jnp.sum(total, axis=0, keepdims=True)
        shrink = jnp.where(t > 1.0, SMALL, 1.0)
        inv = jnp.where(t > 0.0, 1.0 / (t * shrink), 0.0)
        for m in range(NN // TILE):
            rows = slice(m * TILE, (m + 1) * TILE)
            kept_ref[rows, i * U : (i + 1) * U] = ((kf[rows] * shrink) * inv).astype(BF)
        row = pl.ds(home(z, k), 1)
        tloc_ref[row, :] = t
        tin_ref[row, :] = t + pexp_ref[...] if k == 0 else t


def score(ks, near_emb, far_emb, nid, bias, pemb, tloc, tin, users):
    vm = pl.BlockSpec(memory_space=pltpu.VMEM)
    n = len(ks)
    return pl.pallas_call(
        functools.partial(score_kernel, ks),
        in_specs=[vm] * (7 + n),
        out_specs=[vm] * 4,
        out_shape=[
            jax.ShapeDtypeStruct((NZ, U), F32),
            jax.ShapeDtypeStruct((NZ, U), F32),
            jax.ShapeDtypeStruct((1, U), F32),
            jax.ShapeDtypeStruct((NN, n * U), BF),
        ],
        scratch_shapes=[pltpu.VMEM((NN, U), F32)],
        compiler_params=params(14 * 1024 * 1024),
        cost_estimate=cost(2 * n * U * NN * E, 5e6, n * U * NN),
        name="score",
    )(near_emb, far_emb, nid, bias, pemb, tloc, tin, *[users[k] for k in ks])


def grad_kernel(tot_ref, tloc_ref, pexp_ref, near_emb, far_emb, pemb_ref, kept_a, kept_b, *rest):
    users = rest[:NZ]
    keep_ref, send_ref, g_ref, pterm_ref, wu, ratio, rel = rest[NZ:]
    z = lax.axis_index("z")
    tot = tot_ref[...]
    shrink = jnp.where(tot > 1.0, SMALL, 1.0)
    ratio[...] = (tloc_ref[...] * shrink) * (1.0 / (tot * shrink))
    own = tot_ref[pl.ds(z, 1), :]
    shrink = jnp.where(own > 1.0, SMALL, 1.0)
    pprob = (pexp_ref[...] * shrink) * (1.0 / (own * shrink))
    rel[...] = jnp.zeros_like(rel)
    for k in range(NZ):
        rel[k : k + 1] = SCALE * ratio[pl.ds(home(z, k), 1), :]
    rel[NZ : NZ + 1] = SCALE * (pprob - 1.0)
    cols = rel[...].T
    for k in range(NZ):
        wu[k * U : (k + 1) * U] = (users[k][0:U].astype(F32) * cols[:, k : k + 1]).astype(BF)
    coef = cols[:, NZ : NZ + 1]
    g_ref[N : N + U] = (users[0][0:U].astype(F32) * coef).astype(BF)
    pterm_ref[...] = pemb_ref[...].astype(F32) * coef
    for k in range(NZ):
        kept, i = (kept_a, k) if k < FIRST else (kept_b, k - FIRST)
        cols_k = slice(i * U, (i + 1) * U)
        ug = lax.dot_general(kept[0:N, cols_k], near_emb[...], TN, preferred_element_type=F32)
        ug = ug + lax.dot_general(kept[N:NN, cols_k], far_emb[...], TN, preferred_element_type=F32)
        apart = jnp.bitwise_xor(home(z, k), z)
        place = (apart & 2) + (apart >> 2)
        (send_ref if OFFSETS[k] % 2 else keep_ref)[place] = (ug * cols[:, k : k + 1]).astype(BF)
    for m in range(NN // TILE):
        rows = slice(m * TILE, (m + 1) * TILE)
        g = mm(kept_a[rows], wu[0 : FIRST * U]) + mm(kept_b[rows], wu[FIRST * U :])
        first = m * TILE if m < 2 else m * TILE + U
        g_ref[first : first + TILE] = g.astype(BF)


def grads(tot, tloc, pexp, near_emb, far_emb, pemb, kept_a, kept_b, users):
    vm = pl.BlockSpec(memory_space=pltpu.VMEM)
    return pl.pallas_call(
        grad_kernel,
        in_specs=[vm] * (8 + NZ),
        out_specs=[vm] * 4,
        out_shape=[
            jax.ShapeDtypeStruct((NZ // 2, U, E), BF),
            jax.ShapeDtypeStruct((NZ // 2, U, E), BF),
            jax.ShapeDtypeStruct((ROWS, E), BF),
            jax.ShapeDtypeStruct((U, E), F32),
        ],
        scratch_shapes=[
            pltpu.VMEM((NZ * U, E), BF),
            pltpu.VMEM((NZ, U), F32),
            pltpu.VMEM((128, U), F32),
        ],
        compiler_params=params(),
        cost_estimate=cost(4 * NZ * U * NN * E, 8e6),
        name="grads",
    )(tot, tloc, pexp, near_emb, far_emb, pemb, kept_a, kept_b, *users)


def order():
    core = lax.axis_index("core")
    xx, y = near(lax.axis_index("x_hi") * 2 + lax.axis_index("x_lo")), near(lax.axis_index("y"))
    return core, jnp.where(core == 0, xx, y), jnp.where(core == 0, y, xx)


def back_kernel(mine, g_ref, feat_ref, far_ref, w_out_ref, hid_ref, far_hid, out_ref):
    core, first, second = order()
    if not mine:
        core, first, second = 1 - core, second, first
    for c in range(2):
        cols = pl.ds(pl.multiple_of(core * (H // 2) + c * WIDE, WIDE), WIDE)
        w_in = w_out = 0.0
        for rows, feat, hid in ((slice(0, N + U), feat_ref, hid_ref), (slice(N + U, ROWS), far_ref, far_hid)):
            hid = hid[:, cols]
            g = g_ref[rows]
            back = lax.dot_general(g, w_out_ref[cols], NT, preferred_element_type=F32)
            back = jnp.where(hid > 0, back, 0.0).astype(BF)
            w_in += lax.dot_general(feat[0 : g.shape[0]], back, TN, preferred_element_type=F32)
            w_out += lax.dot_general(hid, g, TN, preferred_element_type=F32)
        w_in, w_out = w_in.astype(BF), w_out.astype(BF)
        for t in range(2):
            for half in range(2):
                inner = jnp.bitwise_xor(second, 2 * t + half)
                rows = slice(half * 128, (half + 1) * 128)
                out_ref[jnp.bitwise_xor(first, c), inner] = w_in[rows, t * TILE : (t + 1) * TILE]
                rows = slice(t * TILE + half * 128, t * TILE + (half + 1) * 128)
                out_ref[jnp.bitwise_xor(first, 2 + c), inner] = w_out[rows]


def backward(mine, *args):
    return in_vmem(
        functools.partial(back_kernel, mine), "backward", 3 * ROWS * E * H, [((4, 4, 128, TILE), BF)], *args
    )[0]


def finish_kernel(mine, x_ref, *rest):
    w_in_hbm, w_out_hbm, a, b, sems = rest[-5:]
    core, first, second = order()
    if not mine:
        core, first, second = 1 - core, second, first
    copies = []
    for c in range(2):
        for t in range(2):
            for half in range(2):
                inner = jnp.bitwise_xor(second, 2 * t + half)
                start_t = c * WIDE + t * TILE
                cols = slice(start_t, start_t + TILE)
                a[half * 128 : (half + 1) * 128, cols] = x_ref[jnp.bitwise_xor(first, c), inner].astype(F32)
                rows = slice(start_t + half * 128, start_t + (half + 1) * 128)
                b[rows] = x_ref[jnp.bitwise_xor(first, 2 + c), inner].astype(F32)
        here = pl.ds(c * WIDE, WIDE)
        there = pl.ds(pl.multiple_of(core * (H // 2) + c * WIDE, WIDE), WIDE)
        copies.append(start(a.at[:, here], w_in_hbm.at[:, there], sems.at[2 * c]))
        copies.append(start(b.at[here], w_out_hbm.at[there], sems.at[2 * c + 1]))
    for copy in copies:
        copy.wait()


def finish(mine, x, *outs):
    vm, hbm = pl.BlockSpec(memory_space=pltpu.VMEM), pl.BlockSpec(memory_space=pl.ANY)
    return pl.pallas_call(
        functools.partial(finish_kernel, mine),
        in_specs=[vm] + [hbm] * len(outs),
        out_specs=[hbm, hbm],
        out_shape=[jax.ShapeDtypeStruct((E, H), F32), jax.ShapeDtypeStruct((H, E), F32)],
        scratch_shapes=[
            pltpu.VMEM((E, H // 2), F32),
            pltpu.VMEM((H // 2, E), F32),
            pltpu.SemaphoreType.DMA((4,)),
        ],
        input_output_aliases={1: 0, 2: 1} if outs else {},
        compiler_params=params(14 * 1024 * 1024),
        cost_estimate=cost(0, 3e6),
        name="finish",
    )(x, *outs)


def swap(x, axis, k):
    return lax.ppermute(x, axis, [(i, i ^ k) for i in range(SIZES[AXES.index(axis)])])


def after(x, *needed):
    return lax.optimization_barrier((x, *needed))[0]


def shift(x, by):
    return lax.ppermute(x, "z", [(i, (i + by) % NZ) for i in range(NZ)])


def device(x_lo, z, x_hi, y, core):
    return (((x_lo * 8 + z) * 2 + x_hi) * 4 + y) * 2 + core


def near(place):
    return place ^ (place >> 1)


def plane_swap(x, k, x_core):
    pairs = []
    for z in range(8):
        for xx in range(4):
            for y in range(4):
                for core in range(2):
                    to_x, to_y = (near(near(xx) ^ k), y) if core == x_core else (xx, near(near(y) ^ k))
                    pairs.append(
                        (device(xx & 1, z, xx >> 1, y, core), device(to_x & 1, z, to_x >> 1, to_y, core))
                    )
    return lax.ppermute(x, AXES, pairs)


def add(*terms):
    return sum(t.astype(F32) for t in terms)


def sum_over_z(x, rounds, dtype):
    for ks in rounds:
        sent = x.astype(dtype)
        terms = [t.astype(F32) for t in [sent] + [swap(sent, "z", k) for k in ks]]
        while len(terms) > 1:
            terms = [a + b for a, b in zip(terms[::2], terms[1::2])]
        x = terms[0]
    return x


def gathered(x, x_core, *beside):
    got = {k: plane_swap(x, k, x_core) for k in (1, 2, 3)}
    if beside:
        got, beside = lax.optimization_barrier((got, beside))
    got = jnp.stack([x] + [got[k] for k in (1, 2, 3)])
    return (got, *beside) if beside else got


def all_reduce(mine, theirs, keep, send):
    half = add(mine, swap(theirs, "core", 1)).astype(BF)
    quarter = add(half[0], *[plane_swap(half[k], k, 0) for k in ORDER]).astype(BF)
    keep = add(keep, swap(send, "z", 1)).astype(BF)
    quarter, keep = lax.optimization_barrier((quarter, keep))
    part = add(quarter[0], *[plane_swap(quarter[k], k, 1) for k in ORDER])
    part = sum_over_z(part, ((1, 6, 7), (2,)), BF).astype(BF)
    part, keep = lax.optimization_barrier((part, keep))
    quarter = gathered(part, 1)
    user = add(keep[0], *[swap(keep[i], "z", k) for i, k in ((1, 4), (2, 2), (3, 6))])
    half, user = gathered(quarter, 0, user)
    return half, swap(half, "core", 1), user


def on_device(user_emb, pos_feat, pos_id, neg_feat, neg_id, neg_bucket, logq_table, w_in, w_out):
    mine, near = pack(user_emb, pos_id, neg_feat, neg_id, neg_bucket)
    up, down = shift(mine, 1), shift(mine, -1)
    far = swap(near, "x_lo", 1)
    users = [mine, up, down]
    hid, feat, w_in = in_vmem(
        hidden_kernel,
        "hidden",
        2 * (N + U) * E * H,
        [((N + U, H), BF), ((N + U, E), BF), ((E, H), BF)],
        neg_feat,
        pos_feat,
        w_in,
    )
    up, down = shift(after(up, hid), 1), shift(after(down, hid), -1)
    users += [up, down]
    near_emb, pemb, w_out = in_vmem(
        embed_kernel, "embed", 2 * (N + U) * E * H, [((N, E), BF), ((U, E), BF), ((H, E), BF)], hid, w_out
    )
    up, down = shift(after(up, near_emb), 1), shift(after(down, near_emb), -1)
    users += [up, down]
    far_hid, far_emb, nid, bias = in_vmem(
        far_kernel,
        "far",
        4 * N * E * H,
        [((N, H), BF), ((N, E), BF), ((NN, 128), F32), ((NN, 128), F32)],
        near,
        far,
        w_in,
        w_out,
        logq_table.reshape(8, 128),
    )
    users += [shift(after(up, far_emb), 1)]
    none = jnp.zeros((NZ, U), F32)
    ks = tuple(range(NZ))
    tloc, tot, pexp, kept_a = score(ks[:FIRST], near_emb, far_emb, nid, bias, pemb, none, none, users)
    tloc, tot, _, kept_b = score(ks[FIRST:], near_emb, far_emb, nid, bias, pemb, tloc, tot, users)
    tot = sum_over_z(tot, ((1, 6, 7), (2,)), F32)
    keep, send, g, pterm = grads(tot, tloc, pexp, near_emb, far_emb, pemb, kept_a, kept_b, users)
    args = (g, feat, far, w_out, hid, far_hid)
    theirs_g = backward(False, *args)
    half, other, user = all_reduce(backward(True, *args), theirs_g, keep, send)
    w_in_grad, w_out_grad = finish(False, other, *finish(True, half))
    return user + pterm, w_in_grad, w_out_grad


def solution(mesh):
    rows = P(AXES, None)
    ids = P(AXES)
    return jax.shard_map(
        on_device,
        mesh=Mesh(mesh.devices.reshape(SIZES), AXES),
        in_specs=(rows, rows, ids, rows, ids, ids, P(), P(), P()),
        out_specs=(rows, P(), P()),
        check_vma=False,
    )
```

```python
import functools

import jax
import jax.numpy as jnp
from jax import lax
from jax.experimental import pallas as pl
from jax.experimental.pallas import tpu as pltpu
from jax.sharding import Mesh, PartitionSpec as P

AXES = ("x_lo", "z", "x_hi", "y", "core")
SIZES = (2, 8, 2, 4, 2)
BF, F32, I32 = jnp.bfloat16, jnp.float32, jnp.int32
SCALE = 0.125
SMALL = 2.0**-64
E, H, U, N = 256, 2048, 256, 512
NN = 2 * N
ROWS = NN + U
TILE = 256
CHUNKS = H // TILE
NZ = 8
ORDER = (3, 2, 1)
OFFSETS = (0, -1, 1, -2, 2, -3, 3, 4)
FIRST = 7
VMEM_LIMIT = 24 * 1024 * 1024

WIDE = 512
NT = (((1,), (1,)), ((), ()))
TN = (((0,), (0,)), ((), ()))


def params(limit=VMEM_LIMIT):
    return pltpu.CompilerParams(vmem_limit_bytes=limit)


def cost(flops, nbytes, trans=0):
    return pl.CostEstimate(flops=int(flops), bytes_accessed=int(nbytes), transcendentals=int(trans))


def whole(shape):
    return pl.BlockSpec(shape, lambda *_: (0,) * len(shape))


def mm(a, b):
    return jnp.dot(a, b, preferred_element_type=F32)


def start(src, dst, sem):
    copy = pltpu.make_async_copy(src, dst, sem)
    copy.start()
    return copy


def pack_kernel(user_hbm, pid_hbm, feat_hbm, nid_hbm, bucket_hbm, mine_ref, near_ref, pid_ref, nid_ref, bucket_ref, sems):
    copies = [
        start(pid_hbm, pid_ref, sems.at[0]),
        start(nid_hbm, nid_ref, sems.at[1]),
        start(bucket_hbm, bucket_ref, sems.at[2]),
        start(user_hbm, mine_ref.at[0:U], sems.at[3]),
        start(feat_hbm, near_ref.at[0:N], sems.at[4]),
    ]
    row = lax.broadcasted_iota(I32, (16, E), 0)

    def tail(digits):
        out = jnp.zeros((16, E), F32)
        for i, digit in enumerate(digits):
            out = jnp.where(row == i, digit.astype(F32), out)
        return out.astype(BF)

    def digits(ids, bits):
        ids = [ids[:, i : i + 256] for i in range(0, ids.shape[1], 256)]
        return [i >> bits for i in ids] + [i & (2**bits - 1) for i in ids]

    for copy in copies[:3]:
        copy.wait()
    mine_ref[U : U + 16] = tail(digits(pid_ref[...], 6))
    near_ref[N : N + 16] = tail(digits(nid_ref[...], 6) + digits(bucket_ref[...], 5))
    for copy in copies[3:]:
        copy.wait()


def pack(user_emb, pos_id, neg_feat, neg_id, neg_bucket):
    vm = pl.BlockSpec(memory_space=pltpu.VMEM)
    return pl.pallas_call(
        pack_kernel,
        in_specs=[pl.BlockSpec(memory_space=pltpu.HBM)] * 5,
        out_specs=[vm] * 2,
        out_shape=[jax.ShapeDtypeStruct((U + 16, E), BF), jax.ShapeDtypeStruct((N + 16, E), BF)],
        scratch_shapes=[
            pltpu.VMEM((1, U), I32),
            pltpu.VMEM((1, N), I32),
            pltpu.VMEM((1, N), I32),
            pltpu.SemaphoreType.DMA((5,)),
        ],
        compiler_params=params(60 * 1024 * 1024),
        cost_estimate=cost(1e10, 1e6),
        name="pack",
    )(user_emb, pos_id.reshape(1, U), neg_feat, neg_id.reshape(1, N), neg_bucket.reshape(1, N))


def hidden(feat, w_in_ref):
    return jnp.maximum(mm(feat, w_in_ref[...]), 0.0).astype(BF)


def hidden_kernel(near_ref, pos_ref, w_in_ref, hid_ref, feat_ref, w_in_out):
    for m, feat in enumerate((near_ref[0:TILE], near_ref[TILE:N], pos_ref[...])):
        rows = slice(m * TILE, (m + 1) * TILE)
        feat_ref[rows] = feat
        hid_ref[rows] = hidden(feat, w_in_ref)
    w_in_out[...] = w_in_ref[...]


def embed_kernel(hid_ref, w_out_ref, emb_ref, pemb_ref, w_out_out):
    w_out_out[...] = w_out_ref[...]
    for m, (ref, first) in enumerate([(emb_ref, 0), (emb_ref, TILE), (pemb_ref, 0)]):
        hid = hid_ref[m * TILE : (m + 1) * TILE]
        ref[first : first + TILE] = mm(hid, w_out_ref[...]).astype(BF)


def far_kernel(near_ref, far_ref, w_in_ref, w_out_ref, table_ref, hid_ref, emb_ref, nid_ref, bias_ref):
    lane = lax.broadcasted_iota(I32, (TILE, 128), 1).astype(F32)
    for side, tail in enumerate((near_ref[N : N + 16], far_ref[N : N + 16])):
        tail = jnp.concatenate([tail.astype(F32), jnp.zeros((112, E), F32)], axis=0).T
        for block in range(2):
            rows = slice((2 * side + block) * TILE, (2 * side + block + 1) * TILE)
            nid = tail[:, block : block + 1] * 64.0 + tail[:, block + 2 : block + 3]
            nid_ref[rows] = jnp.broadcast_to(nid, (TILE, 128))
            bucket = tail[:, block + 4 : block + 5] * 32.0 + tail[:, block + 6 : block + 7]
            found = jnp.zeros((TILE, 128), F32)
            for b in range(8):
                found = found + jnp.where(bucket == lane + 128.0 * b, table_ref[b : b + 1], 0.0)
            bias_ref[rows] = jnp.broadcast_to(jnp.sum(found, axis=1, keepdims=True), (TILE, 128))
    for m in range(N // TILE):
        rows = slice(m * TILE, (m + 1) * TILE)
        hid = hidden(far_ref[rows], w_in_ref)
        hid_ref[rows] = hid
        emb_ref[rows] = mm(hid, w_out_ref[...]).astype(BF)


def in_vmem(kernel, name, flops, outs, *args, scratch=()):
    vm = pl.BlockSpec(memory_space=pltpu.VMEM)
    return pl.pallas_call(
        kernel,
        in_specs=[vm] * len(args),
        out_specs=[vm] * len(outs),
        out_shape=[jax.ShapeDtypeStruct(shape, dtype) for shape, dtype in outs],
        scratch_shapes=list(scratch),
        compiler_params=params(14 * 1024 * 1024),
        cost_estimate=cost(flops, 4e6),
        name=name,
    )(*args)


def twice(x):
    return jnp.concatenate([x, x], axis=1)


def home(z, k):
    return (z + OFFSETS[k] + NZ) & (NZ - 1)


def score_kernel(ks, near_emb, far_emb, nid_ref, bias_ref, pemb_ref, tloc_in, tin_in, *rest):
    users = rest[: len(ks)]
    tloc_ref, tin_ref, pexp_ref, kept_ref, kf = rest[len(ks) :]
    z = lax.axis_index("z")
    tloc_ref[...] = tloc_in[...]
    tin_ref[...] = tin_in[...]
    if ks[0] == 0:
        prod = users[0][0:U].astype(F32) * pemb_ref[...].astype(F32)
        prod = (prod[:, 0:128] + prod[:, 128:256]).T
        pexp_ref[...] = jnp.exp(SCALE * jnp.sum(prod, axis=0, keepdims=True))
    else:
        pexp_ref[...] = jnp.zeros_like(pexp_ref)
    for i, k in enumerate(ks):
        u = (users[i][0:U].astype(F32) * SCALE).astype(BF)
        tail = users[i][U : U + 16].astype(F32)
        pid = tail[0:1] * 64.0 + tail[1:2]
        total = jnp.zeros((8, U), F32)
        for m in range(NN // TILE):
            rows = slice(m * TILE, (m + 1) * TILE)
            emb = near_emb[rows] if m < 2 else far_emb[(m - 2) * TILE : (m - 1) * TILE]
            sc = lax.dot_general(emb, u, NT, preferred_element_type=F32) - twice(bias_ref[rows])
            kept = jnp.where(twice(nid_ref[rows]) != pid, jnp.exp(sc), 0.0)
            kf[rows] = kept
            total = total + jnp.sum(kept.reshape(TILE // 8, 8, U), axis=0)
        t = jnp.sum(total, axis=0, keepdims=True)
        shrink = jnp.where(t > 1.0, SMALL, 1.0)
        inv = jnp.where(t > 0.0, 1.0 / (t * shrink), 0.0)
        for m in range(NN // TILE):
            rows = slice(m * TILE, (m + 1) * TILE)
            kept_ref[rows, i * U : (i + 1) * U] = ((kf[rows] * shrink) * inv).astype(BF)
        row = pl.ds(home(z, k), 1)
        tloc_ref[row, :] = t
        tin_ref[row, :] = t + pexp_ref[...] if k == 0 else t


def score(ks, near_emb, far_emb, nid, bias, pemb, tloc, tin, users):
    vm = pl.BlockSpec(memory_space=pltpu.VMEM)
    n = len(ks)
    return pl.pallas_call(
        functools.partial(score_kernel, ks),
        in_specs=[vm] * (7 + n),
        out_specs=[vm] * 4,
        out_shape=[
            jax.ShapeDtypeStruct((NZ, U), F32),
            jax.ShapeDtypeStruct((NZ, U), F32),
            jax.ShapeDtypeStruct((1, U), F32),
            jax.ShapeDtypeStruct((NN, n * U), BF),
        ],
        scratch_shapes=[pltpu.VMEM((NN, U), F32)],
        compiler_params=params(14 * 1024 * 1024),
        cost_estimate=cost(2 * n * U * NN * E, 5e6, n * U * NN),
        name="score",
    )(near_emb, far_emb, nid, bias, pemb, tloc, tin, *[users[k] for k in ks])


def ratios(tot_ref, tloc_ref, pexp_ref, ratio, rel):
    z = lax.axis_index("z")
    tot = tot_ref[...]
    shrink = jnp.where(tot > 1.0, SMALL, 1.0)
    ratio[...] = (tloc_ref[...] * shrink) * (1.0 / (tot * shrink))
    own = tot_ref[pl.ds(z, 1), :]
    shrink = jnp.where(own > 1.0, SMALL, 1.0)
    pprob = (pexp_ref[...] * shrink) * (1.0 / (own * shrink))
    rel[...] = jnp.zeros_like(rel)
    for k in range(NZ):
        rel[k : k + 1] = SCALE * ratio[pl.ds(home(z, k), 1), :]
    rel[NZ : NZ + 1] = SCALE * (pprob - 1.0)
    return rel[...].T


RATIOS = [pltpu.VMEM((NZ, U), F32), pltpu.VMEM((128, U), F32)]


def item_grad_kernel(tot_ref, tloc_ref, pexp_ref, kept_a, kept_b, *rest):
    users = rest[:NZ]
    g_ref, wu, ratio, rel = rest[NZ:]
    cols = ratios(tot_ref, tloc_ref, pexp_ref, ratio, rel)
    for k in range(NZ):
        wu[k * U : (k + 1) * U] = (users[k][0:U].astype(F32) * cols[:, k : k + 1]).astype(BF)
    g_ref[N : N + U] = (users[0][0:U].astype(F32) * cols[:, NZ : NZ + 1]).astype(BF)
    for m in range(NN // TILE):
        rows = slice(m * TILE, (m + 1) * TILE)
        g = mm(kept_a[rows], wu[0 : FIRST * U]) + mm(kept_b[rows], wu[FIRST * U :])
        first = m * TILE if m < 2 else m * TILE + U
        g_ref[first : first + TILE] = g.astype(BF)


def user_grad_kernel(tot_ref, tloc_ref, pexp_ref, kept_a, kept_b, near_emb, far_emb, pemb_ref, *rest):
    keep_ref, send_ref, pterm_ref, ratio, rel = rest
    z = lax.axis_index("z")
    cols = ratios(tot_ref, tloc_ref, pexp_ref, ratio, rel)
    pterm_ref[...] = pemb_ref[...].astype(F32) * cols[:, NZ : NZ + 1]
    for k in range(NZ):
        kept, i = (kept_a, k) if k < FIRST else (kept_b, k - FIRST)
        cols_k = slice(i * U, (i + 1) * U)
        ug = lax.dot_general(kept[0:N, cols_k], near_emb[...], TN, preferred_element_type=F32)
        ug = ug + lax.dot_general(kept[N:NN, cols_k], far_emb[...], TN, preferred_element_type=F32)
        apart = jnp.bitwise_xor(home(z, k), z)
        place = (apart & 2) + (apart >> 2)
        (send_ref if OFFSETS[k] % 2 else keep_ref)[place] = (ug * cols[:, k : k + 1]).astype(BF)


def item_grads(tot, tloc, pexp, kept_a, kept_b, users):
    scratch = [pltpu.VMEM((NZ * U, E), BF)] + RATIOS
    args = (tot, tloc, pexp, kept_a, kept_b, *users)
    return in_vmem(item_grad_kernel, "items", 2 * NZ * U * NN * E, [((ROWS, E), BF)], *args, scratch=scratch)[0]


def user_grads(*args):
    outs = [((NZ // 2, U, E), BF), ((NZ // 2, U, E), BF), ((U, E), F32)]
    return in_vmem(user_grad_kernel, "users", 2 * NZ * U * NN * E, outs, *args, scratch=RATIOS)


def order():
    core = lax.axis_index("core")
    xx, y = near(lax.axis_index("x_hi") * 2 + lax.axis_index("x_lo")), near(lax.axis_index("y"))
    return core, jnp.where(core == 0, xx, y), jnp.where(core == 0, y, xx)


def back_kernel(mine, g_ref, feat_ref, far_ref, w_out_ref, hid_ref, far_hid, out_ref):
    core, first, second = order()
    if not mine:
        core, first, second = 1 - core, second, first
    for c in range(2):
        cols = pl.ds(pl.multiple_of(core * (H // 2) + c * WIDE, WIDE), WIDE)
        w_in = w_out = 0.0
        for rows, feat, hid in ((slice(0, N + U), feat_ref, hid_ref), (slice(N + U, ROWS), far_ref, far_hid)):
            hid = hid[:, cols]
            g = g_ref[rows]
            back = lax.dot_general(g, w_out_ref[cols], NT, preferred_element_type=F32)
            back = jnp.where(hid > 0, back, 0.0).astype(BF)
            w_in += lax.dot_general(feat[0 : g.shape[0]], back, TN, preferred_element_type=F32)
            w_out += lax.dot_general(hid, g, TN, preferred_element_type=F32)
        w_in, w_out = w_in.astype(BF), w_out.astype(BF)
        for t in range(2):
            for half in range(2):
                inner = jnp.bitwise_xor(second, 2 * t + half)
                rows = slice(half * 128, (half + 1) * 128)
                out_ref[jnp.bitwise_xor(first, c), inner] = w_in[rows, t * TILE : (t + 1) * TILE]
                rows = slice(t * TILE + half * 128, t * TILE + (half + 1) * 128)
                out_ref[jnp.bitwise_xor(first, 2 + c), inner] = w_out[rows]


def backward(mine, *args):
    return in_vmem(
        functools.partial(back_kernel, mine), "backward", 3 * ROWS * E * H, [((4, 4, 128, TILE), BF)], *args
    )[0]


def finish_kernel(mine, x_ref, *rest):
    w_in_hbm, w_out_hbm, a, b, sems = rest[-5:]
    core, first, second = order()
    if not mine:
        core, first, second = 1 - core, second, first
    copies = []
    for c in range(2):
        for t in range(2):
            for half in range(2):
                inner = jnp.bitwise_xor(second, 2 * t + half)
                start_t = c * WIDE + t * TILE
                cols = slice(start_t, start_t + TILE)
                a[half * 128 : (half + 1) * 128, cols] = x_ref[jnp.bitwise_xor(first, c), inner].astype(F32)
                rows = slice(start_t + half * 128, start_t + (half + 1) * 128)
                b[rows] = x_ref[jnp.bitwise_xor(first, 2 + c), inner].astype(F32)
        here = pl.ds(c * WIDE, WIDE)
        there = pl.ds(pl.multiple_of(core * (H // 2) + c * WIDE, WIDE), WIDE)
        copies.append(start(a.at[:, here], w_in_hbm.at[:, there], sems.at[2 * c]))
        copies.append(start(b.at[here], w_out_hbm.at[there], sems.at[2 * c + 1]))
    for copy in copies:
        copy.wait()


def finish(mine, x, *outs):
    vm, hbm = pl.BlockSpec(memory_space=pltpu.VMEM), pl.BlockSpec(memory_space=pl.ANY)
    return pl.pallas_call(
        functools.partial(finish_kernel, mine),
        in_specs=[vm] + [hbm] * len(outs),
        out_specs=[hbm, hbm],
        out_shape=[jax.ShapeDtypeStruct((E, H), F32), jax.ShapeDtypeStruct((H, E), F32)],
        scratch_shapes=[
            pltpu.VMEM((E, H // 2), F32),
            pltpu.VMEM((H // 2, E), F32),
            pltpu.SemaphoreType.DMA((4,)),
        ],
        input_output_aliases={1: 0, 2: 1} if outs else {},
        compiler_params=params(14 * 1024 * 1024),
        cost_estimate=cost(0, 3e6),
        name="finish",
    )(x, *outs)


def swap(x, axis, k):
    return lax.ppermute(x, axis, [(i, i ^ k) for i in range(SIZES[AXES.index(axis)])])


def after(x, *needed):
    return lax.optimization_barrier((x, *needed))[0]


def shift(x, by):
    return lax.ppermute(x, "z", [(i, (i + by) % NZ) for i in range(NZ)])


def device(x_lo, z, x_hi, y, core):
    return (((x_lo * 8 + z) * 2 + x_hi) * 4 + y) * 2 + core


def near(place):
    return place ^ (place >> 1)


def plane_swap(x, k, x_core):
    pairs = []
    for z in range(8):
        for xx in range(4):
            for y in range(4):
                for core in range(2):
                    to_x, to_y = (near(near(xx) ^ k), y) if core == x_core else (xx, near(near(y) ^ k))
                    pairs.append(
                        (device(xx & 1, z, xx >> 1, y, core), device(to_x & 1, z, to_x >> 1, to_y, core))
                    )
    return lax.ppermute(x, AXES, pairs)


def add(*terms):
    return sum(t.astype(F32) for t in terms)


def sum_over_z(x, rounds, dtype):
    for ks in rounds:
        sent = x.astype(dtype)
        terms = [t.astype(F32) for t in [sent] + [swap(sent, "z", k) for k in ks]]
        while len(terms) > 1:
            terms = [a + b for a, b in zip(terms[::2], terms[1::2])]
        x = terms[0]
    return x


def gathered(x, x_core, *beside):
    got = {k: plane_swap(x, k, x_core) for k in (1, 2, 3)}
    if beside:
        got, beside = lax.optimization_barrier((got, beside))
    got = jnp.stack([x] + [got[k] for k in (1, 2, 3)])
    return (got, *beside) if beside else got


def all_reduce(mine, theirs, keep, send):
    half = add(mine, swap(theirs, "core", 1)).astype(BF)
    quarter = add(half[0], *[plane_swap(half[k], k, 0) for k in ORDER]).astype(BF)
    keep = add(keep, swap(send, "z", 1)).astype(BF)
    got = [plane_swap(quarter[k], k, 1) for k in ORDER[::-1]]
    got, keep = lax.optimization_barrier((got, keep))
    part = add(quarter[0], *got)
    part = sum_over_z(part, ((1, 7, 6), (2,)), BF).astype(BF)
    part, keep = lax.optimization_barrier((part, keep))
    quarter = gathered(part, 1)
    user = add(keep[0], *[swap(keep[i], "z", k) for i, k in ((1, 4), (2, 2), (3, 6))])
    half, user = gathered(quarter, 0, user)
    return half, swap(half, "core", 1), user


def on_device(user_emb, pos_feat, pos_id, neg_feat, neg_id, neg_bucket, logq_table, w_in, w_out):
    mine, near = pack(user_emb, pos_id, neg_feat, neg_id, neg_bucket)
    up, down = shift(mine, 1), shift(mine, -1)
    far = swap(near, "x_lo", 1)
    users = [mine, up, down]
    hid, feat, w_in = in_vmem(
        hidden_kernel,
        "hidden",
        2 * (N + U) * E * H,
        [((N + U, H), BF), ((N + U, E), BF), ((E, H), BF)],
        neg_feat,
        pos_feat,
        w_in,
    )
    up, down = shift(after(up, hid), 1), shift(after(down, hid), -1)
    users += [up, down]
    near_emb, pemb, w_out = in_vmem(
        embed_kernel, "embed", 2 * (N + U) * E * H, [((N, E), BF), ((U, E), BF), ((H, E), BF)], hid, w_out
    )
    up, down = shift(after(up, near_emb), 1), shift(after(down, near_emb), -1)
    users += [up, down]
    far_hid, far_emb, nid, bias = in_vmem(
        far_kernel,
        "far",
        4 * N * E * H,
        [((N, H), BF), ((N, E), BF), ((NN, 128), F32), ((NN, 128), F32)],
        near,
        far,
        w_in,
        w_out,
        logq_table.reshape(8, 128),
    )
    users += [shift(after(up, far_emb), 1)]
    none = jnp.zeros((NZ, U), F32)
    ks = tuple(range(NZ))
    tloc, tot, pexp, kept_a = score(ks[:FIRST], near_emb, far_emb, nid, bias, pemb, none, none, users)
    tloc, tot, _, kept_b = score(ks[FIRST:], near_emb, far_emb, nid, bias, pemb, tloc, tot, users)
    tot = sum_over_z(tot, ((1, 7, 6), (2,)), F32)
    g = item_grads(tot, tloc, pexp, kept_a, kept_b, users)
    keep, send, pterm = user_grads(tot, tloc, pexp, kept_a, kept_b, near_emb, far_emb, pemb)
    args = (g, feat, far, w_out, hid, far_hid)
    theirs_g = backward(False, *args)
    half, other, user = all_reduce(backward(True, *args), theirs_g, keep, send)
    w_in_grad, w_out_grad = finish(False, other, *finish(True, half))
    return user + pterm, w_in_grad, w_out_grad


def solution(mesh):
    rows = P(AXES, None)
    ids = P(AXES)
    return jax.shard_map(
        on_device,
        mesh=Mesh(mesh.devices.reshape(SIZES), AXES),
        in_specs=(rows, rows, ids, rows, ids, ids, P(), P(), P()),
        out_specs=(rows, P(), P()),
        check_vma=False,
    )
```

```python
import functools

import jax
import jax.numpy as jnp
from jax import lax
from jax.experimental import pallas as pl
from jax.experimental.pallas import tpu as pltpu
from jax.sharding import Mesh, PartitionSpec as P

AXES = ("x_lo", "z", "x_hi", "y", "core")
SIZES = (2, 8, 2, 4, 2)
BF, F32, I32 = jnp.bfloat16, jnp.float32, jnp.int32
SCALE = 0.125
SMALL = 2.0**-64
E, H, U, N = 256, 2048, 256, 512
NN = 2 * N
ROWS = NN + U
TILE = 256
CHUNKS = H // TILE
NZ = 8
ORDER = (3, 2, 1)
OFFSETS = (0, -1, 1, -2, 2, -3, 3, 4)
FIRST = 7
VMEM_LIMIT = 24 * 1024 * 1024

WIDE = 512
NT = (((1,), (1,)), ((), ()))
TN = (((0,), (0,)), ((), ()))


def params(limit=VMEM_LIMIT):
    return pltpu.CompilerParams(vmem_limit_bytes=limit)


def cost(flops, nbytes, trans=0):
    return pl.CostEstimate(flops=int(flops), bytes_accessed=int(nbytes), transcendentals=int(trans))


def whole(shape):
    return pl.BlockSpec(shape, lambda *_: (0,) * len(shape))


def mm(a, b):
    return jnp.dot(a, b, preferred_element_type=F32)


def start(src, dst, sem):
    copy = pltpu.make_async_copy(src, dst, sem)
    copy.start()
    return copy


def pack_kernel(user_hbm, pid_hbm, feat_hbm, nid_hbm, bucket_hbm, mine_ref, near_ref, pid_ref, nid_ref, bucket_ref, sems):
    copies = [
        start(pid_hbm, pid_ref, sems.at[0]),
        start(nid_hbm, nid_ref, sems.at[1]),
        start(bucket_hbm, bucket_ref, sems.at[2]),
        start(user_hbm, mine_ref.at[0:U], sems.at[3]),
        start(feat_hbm, near_ref.at[0:N], sems.at[4]),
    ]
    row = lax.broadcasted_iota(I32, (16, E), 0)

    def tail(digits):
        out = jnp.zeros((16, E), F32)
        for i, digit in enumerate(digits):
            out = jnp.where(row == i, digit.astype(F32), out)
        return out.astype(BF)

    def digits(ids, bits):
        ids = [ids[:, i : i + 256] for i in range(0, ids.shape[1], 256)]
        return [i >> bits for i in ids] + [i & (2**bits - 1) for i in ids]

    for copy in copies[:3]:
        copy.wait()
    mine_ref[U : U + 16] = tail(digits(pid_ref[...], 6))
    near_ref[N : N + 16] = tail(digits(nid_ref[...], 6) + digits(bucket_ref[...], 5))
    for copy in copies[3:]:
        copy.wait()


def pack(user_emb, pos_id, neg_feat, neg_id, neg_bucket):
    vm = pl.BlockSpec(memory_space=pltpu.VMEM)
    return pl.pallas_call(
        pack_kernel,
        in_specs=[pl.BlockSpec(memory_space=pltpu.HBM)] * 5,
        out_specs=[vm] * 2,
        out_shape=[jax.ShapeDtypeStruct((U + 16, E), BF), jax.ShapeDtypeStruct((N + 16, E), BF)],
        scratch_shapes=[
            pltpu.VMEM((1, U), I32),
            pltpu.VMEM((1, N), I32),
            pltpu.VMEM((1, N), I32),
            pltpu.SemaphoreType.DMA((5,)),
        ],
        compiler_params=params(60 * 1024 * 1024),
        cost_estimate=cost(1e10, 1e6),
        name="pack",
    )(user_emb, pos_id.reshape(1, U), neg_feat, neg_id.reshape(1, N), neg_bucket.reshape(1, N))


def hidden(feat, w_in_ref):
    return jnp.maximum(mm(feat, w_in_ref[...]), 0.0).astype(BF)


def hidden_kernel(near_ref, pos_ref, w_in_ref, hid_ref, feat_ref, w_in_out):
    for m, feat in enumerate((near_ref[0:TILE], near_ref[TILE:N], pos_ref[...])):
        rows = slice(m * TILE, (m + 1) * TILE)
        feat_ref[rows] = feat
        hid_ref[rows] = hidden(feat, w_in_ref)
    w_in_out[...] = w_in_ref[...]


def embed_kernel(hid_ref, w_out_ref, emb_ref, pemb_ref, w_out_out):
    w_out_out[...] = w_out_ref[...]
    for m, (ref, first) in enumerate([(emb_ref, 0), (emb_ref, TILE), (pemb_ref, 0)]):
        hid = hid_ref[m * TILE : (m + 1) * TILE]
        ref[first : first + TILE] = mm(hid, w_out_ref[...]).astype(BF)


def far_kernel(near_ref, far_ref, w_in_ref, w_out_ref, table_ref, hid_ref, emb_ref, nid_ref, bias_ref):
    lane = lax.broadcasted_iota(I32, (TILE, 128), 1).astype(F32)
    for side, tail in enumerate((near_ref[N : N + 16], far_ref[N : N + 16])):
        tail = jnp.concatenate([tail.astype(F32), jnp.zeros((112, E), F32)], axis=0).T
        for block in range(2):
            rows = slice((2 * side + block) * TILE, (2 * side + block + 1) * TILE)
            nid = tail[:, block : block + 1] * 64.0 + tail[:, block + 2 : block + 3]
            nid_ref[rows] = jnp.broadcast_to(nid, (TILE, 128))
            bucket = tail[:, block + 4 : block + 5] * 32.0 + tail[:, block + 6 : block + 7]
            found = jnp.zeros((TILE, 128), F32)
            for b in range(8):
                found = found + jnp.where(bucket == lane + 128.0 * b, table_ref[b : b + 1], 0.0)
            bias_ref[rows] = jnp.broadcast_to(jnp.sum(found, axis=1, keepdims=True), (TILE, 128))
    for m in range(N // TILE):
        rows = slice(m * TILE, (m + 1) * TILE)
        hid = hidden(far_ref[rows], w_in_ref)
        hid_ref[rows] = hid
        emb_ref[rows] = mm(hid, w_out_ref[...]).astype(BF)


def in_vmem(kernel, name, flops, outs, *args, scratch=()):
    vm = pl.BlockSpec(memory_space=pltpu.VMEM)
    return pl.pallas_call(
        kernel,
        in_specs=[vm] * len(args),
        out_specs=[vm] * len(outs),
        out_shape=[jax.ShapeDtypeStruct(shape, dtype) for shape, dtype in outs],
        scratch_shapes=list(scratch),
        compiler_params=params(14 * 1024 * 1024),
        cost_estimate=cost(flops, 4e6),
        name=name,
    )(*args)


def twice(x):
    return jnp.concatenate([x, x], axis=1)


def home(z, k):
    return (z + OFFSETS[k] + NZ) & (NZ - 1)


def score_kernel(ks, near_emb, far_emb, nid_ref, bias_ref, pemb_ref, tloc_in, tin_in, *rest):
    users = rest[: len(ks)]
    tloc_ref, tin_ref, pexp_ref, kept_ref, kf = rest[len(ks) :]
    z = lax.axis_index("z")
    tloc_ref[...] = tloc_in[...]
    tin_ref[...] = tin_in[...]
    if ks[0] == 0:
        prod = users[0][0:U].astype(F32) * pemb_ref[...].astype(F32)
        prod = (prod[:, 0:128] + prod[:, 128:256]).T
        pexp_ref[...] = jnp.exp(SCALE * jnp.sum(prod, axis=0, keepdims=True))
    else:
        pexp_ref[...] = jnp.zeros_like(pexp_ref)
    for i, k in enumerate(ks):
        u = (users[i][0:U].astype(F32) * SCALE).astype(BF)
        tail = users[i][U : U + 16].astype(F32)
        pid = tail[0:1] * 64.0 + tail[1:2]
        total = jnp.zeros((8, U), F32)
        for m in range(NN // TILE):
            rows = slice(m * TILE, (m + 1) * TILE)
            emb = near_emb[rows] if m < 2 else far_emb[(m - 2) * TILE : (m - 1) * TILE]
            sc = lax.dot_general(emb, u, NT, preferred_element_type=F32) - twice(bias_ref[rows])
            kept = jnp.where(twice(nid_ref[rows]) != pid, jnp.exp(sc), 0.0)
            kf[rows] = kept
            total = total + jnp.sum(kept.reshape(TILE // 8, 8, U), axis=0)
        t = jnp.sum(total, axis=0, keepdims=True)
        shrink = jnp.where(t > 1.0, SMALL, 1.0)
        inv = jnp.where(t > 0.0, 1.0 / (t * shrink), 0.0)
        for m in range(NN // TILE):
            rows = slice(m * TILE, (m + 1) * TILE)
            kept_ref[rows, i * U : (i + 1) * U] = ((kf[rows] * shrink) * inv).astype(BF)
        row = pl.ds(home(z, k), 1)
        tloc_ref[row, :] = t
        tin_ref[row, :] = t + pexp_ref[...] if k == 0 else t


def score(ks, near_emb, far_emb, nid, bias, pemb, tloc, tin, users):
    vm = pl.BlockSpec(memory_space=pltpu.VMEM)
    n = len(ks)
    return pl.pallas_call(
        functools.partial(score_kernel, ks),
        in_specs=[vm] * (7 + n),
        out_specs=[vm] * 4,
        out_shape=[
            jax.ShapeDtypeStruct((NZ, U), F32),
            jax.ShapeDtypeStruct((NZ, U), F32),
            jax.ShapeDtypeStruct((1, U), F32),
            jax.ShapeDtypeStruct((NN, n * U), BF),
        ],
        scratch_shapes=[pltpu.VMEM((NN, U), F32)],
        compiler_params=params(14 * 1024 * 1024),
        cost_estimate=cost(2 * n * U * NN * E, 5e6, n * U * NN),
        name="score",
    )(near_emb, far_emb, nid, bias, pemb, tloc, tin, *[users[k] for k in ks])


def ratios(tot_ref, tloc_ref, pexp_ref, ratio, rel):
    z = lax.axis_index("z")
    tot = tot_ref[...]
    shrink = jnp.where(tot > 1.0, SMALL, 1.0)
    ratio[...] = (tloc_ref[...] * shrink) * (1.0 / (tot * shrink))
    own = tot_ref[pl.ds(z, 1), :]
    shrink = jnp.where(own > 1.0, SMALL, 1.0)
    pprob = (pexp_ref[...] * shrink) * (1.0 / (own * shrink))
    rel[...] = jnp.zeros_like(rel)
    for k in range(NZ):
        rel[k : k + 1] = SCALE * ratio[pl.ds(home(z, k), 1), :]
    rel[NZ : NZ + 1] = SCALE * (pprob - 1.0)
    return rel[...].T


RATIOS = [pltpu.VMEM((NZ, U), F32), pltpu.VMEM((128, U), F32)]


def item_grad_kernel(tot_ref, tloc_ref, pexp_ref, kept_a, kept_b, *rest):
    users = rest[:NZ]
    g_ref, wu, ratio, rel = rest[NZ:]
    cols = ratios(tot_ref, tloc_ref, pexp_ref, ratio, rel)
    for k in range(NZ):
        wu[k * U : (k + 1) * U] = (users[k][0:U].astype(F32) * cols[:, k : k + 1]).astype(BF)
    g_ref[N : N + U] = (users[0][0:U].astype(F32) * cols[:, NZ : NZ + 1]).astype(BF)
    for m in range(NN // TILE):
        rows = slice(m * TILE, (m + 1) * TILE)
        g = mm(kept_a[rows], wu[0 : FIRST * U]) + mm(kept_b[rows], wu[FIRST * U :])
        first = m * TILE if m < 2 else m * TILE + U
        g_ref[first : first + TILE] = g.astype(BF)


def user_grad_kernel(tot_ref, tloc_ref, pexp_ref, kept_a, kept_b, near_emb, far_emb, pemb_ref, *rest):
    keep_ref, send_ref, pterm_ref, ratio, rel = rest
    z = lax.axis_index("z")
    cols = ratios(tot_ref, tloc_ref, pexp_ref, ratio, rel)
    pterm_ref[...] = pemb_ref[...].astype(F32) * cols[:, NZ : NZ + 1]
    for k in range(NZ):
        kept, i = (kept_a, k) if k < FIRST else (kept_b, k - FIRST)
        cols_k = slice(i * U, (i + 1) * U)
        ug = lax.dot_general(kept[0:N, cols_k], near_emb[...], TN, preferred_element_type=F32)
        ug = ug + lax.dot_general(kept[N:NN, cols_k], far_emb[...], TN, preferred_element_type=F32)
        apart = jnp.bitwise_xor(home(z, k), z)
        place = (apart & 2) + (apart >> 2)
        (send_ref if OFFSETS[k] % 2 else keep_ref)[place] = (ug * cols[:, k : k + 1]).astype(BF)


def item_grads(tot, tloc, pexp, kept_a, kept_b, users):
    scratch = [pltpu.VMEM((NZ * U, E), BF)] + RATIOS
    args = (tot, tloc, pexp, kept_a, kept_b, *users)
    return in_vmem(item_grad_kernel, "items", 2 * NZ * U * NN * E, [((ROWS, E), BF)], *args, scratch=scratch)[0]


def user_grads(*args):
    outs = [((NZ // 2, U, E), BF), ((NZ // 2, U, E), BF), ((U, E), F32)]
    return in_vmem(user_grad_kernel, "users", 2 * NZ * U * NN * E, outs, *args, scratch=RATIOS)


def order():
    core = lax.axis_index("core")
    xx, y = near(lax.axis_index("x_hi") * 2 + lax.axis_index("x_lo")), near(lax.axis_index("y"))
    return core, jnp.where(core == 0, xx, y), jnp.where(core == 0, y, xx)


def back_kernel(mine, g_ref, feat_ref, far_ref, w_out_ref, hid_ref, far_hid, out_ref):
    core, first, second = order()
    if not mine:
        core, first, second = 1 - core, second, first
    for c in range(2):
        cols = pl.ds(pl.multiple_of(core * (H // 2) + c * WIDE, WIDE), WIDE)
        w_in = w_out = 0.0
        for rows, feat, hid in ((slice(0, N + U), feat_ref, hid_ref), (slice(N + U, ROWS), far_ref, far_hid)):
            hid = hid[:, cols]
            g = g_ref[rows]
            back = lax.dot_general(g, w_out_ref[cols], NT, preferred_element_type=F32)
            back = jnp.where(hid > 0, back, 0.0).astype(BF)
            w_in += lax.dot_general(feat[0 : g.shape[0]], back, TN, preferred_element_type=F32)
            w_out += lax.dot_general(hid, g, TN, preferred_element_type=F32)
        w_in, w_out = w_in.astype(BF), w_out.astype(BF)
        for t in range(2):
            for half in range(2):
                inner = jnp.bitwise_xor(second, 2 * t + half)
                rows = slice(half * 128, (half + 1) * 128)
                out_ref[jnp.bitwise_xor(first, c), inner] = w_in[rows, t * TILE : (t + 1) * TILE]
                rows = slice(t * TILE + half * 128, t * TILE + (half + 1) * 128)
                out_ref[jnp.bitwise_xor(first, 2 + c), inner] = w_out[rows]


def backward(mine, *args):
    return in_vmem(
        functools.partial(back_kernel, mine), "backward", 3 * ROWS * E * H, [((4, 4, 128, TILE), BF)], *args
    )[0]


def finish_kernel(mine, x_ref, *rest):
    w_in_hbm, w_out_hbm, a, b, sems = rest[-5:]
    core, first, second = order()
    if not mine:
        core, first, second = 1 - core, second, first
    copies = []
    for c in range(2):
        for t in range(2):
            for half in range(2):
                inner = jnp.bitwise_xor(second, 2 * t + half)
                start_t = c * WIDE + t * TILE
                cols = slice(start_t, start_t + TILE)
                a[half * 128 : (half + 1) * 128, cols] = x_ref[jnp.bitwise_xor(first, c), inner].astype(F32)
                rows = slice(start_t + half * 128, start_t + (half + 1) * 128)
                b[rows] = x_ref[jnp.bitwise_xor(first, 2 + c), inner].astype(F32)
        here = pl.ds(c * WIDE, WIDE)
        there = pl.ds(pl.multiple_of(core * (H // 2) + c * WIDE, WIDE), WIDE)
        copies.append(start(a.at[:, here], w_in_hbm.at[:, there], sems.at[2 * c]))
        copies.append(start(b.at[here], w_out_hbm.at[there], sems.at[2 * c + 1]))
    for copy in copies:
        copy.wait()


def finish(mine, x, *outs):
    vm, hbm = pl.BlockSpec(memory_space=pltpu.VMEM), pl.BlockSpec(memory_space=pl.ANY)
    return pl.pallas_call(
        functools.partial(finish_kernel, mine),
        in_specs=[vm] + [hbm] * len(outs),
        out_specs=[hbm, hbm],
        out_shape=[jax.ShapeDtypeStruct((E, H), F32), jax.ShapeDtypeStruct((H, E), F32)],
        scratch_shapes=[
            pltpu.VMEM((E, H // 2), F32),
            pltpu.VMEM((H // 2, E), F32),
            pltpu.SemaphoreType.DMA((4,)),
        ],
        input_output_aliases={1: 0, 2: 1} if outs else {},
        compiler_params=params(14 * 1024 * 1024),
        cost_estimate=cost(0, 3e6),
        name="finish",
    )(x, *outs)


def swap(x, axis, k):
    return lax.ppermute(x, axis, [(i, i ^ k) for i in range(SIZES[AXES.index(axis)])])


def after(x, *needed):
    return lax.optimization_barrier((x, *needed))[0]


def shift(x, by):
    return lax.ppermute(x, "z", [(i, (i + by) % NZ) for i in range(NZ)])


def device(x_lo, z, x_hi, y, core):
    return (((x_lo * 8 + z) * 2 + x_hi) * 4 + y) * 2 + core


def near(place):
    return place ^ (place >> 1)


def plane_swap(x, k, x_core):
    pairs = []
    for z in range(8):
        for xx in range(4):
            for y in range(4):
                for core in range(2):
                    to_x, to_y = (near(near(xx) ^ k), y) if core == x_core else (xx, near(near(y) ^ k))
                    pairs.append(
                        (device(xx & 1, z, xx >> 1, y, core), device(to_x & 1, z, to_x >> 1, to_y, core))
                    )
    return lax.ppermute(x, AXES, pairs)


def add(*terms):
    return sum(t.astype(F32) for t in terms)


def sum_over_z(x, rounds, dtype):
    for ks in rounds:
        sent = x.astype(dtype)
        terms = [t.astype(F32) for t in [sent] + [swap(sent, "z", k) for k in ks]]
        while len(terms) > 1:
            terms = [a + b for a, b in zip(terms[::2], terms[1::2])]
        x = terms[0]
    return x


def gathered(x, x_core, *beside):
    got = {k: plane_swap(x, k, x_core) for k in (1, 2, 3)}
    if beside:
        got, beside = lax.optimization_barrier((got, beside))
    got = jnp.stack([x] + [got[k] for k in (1, 2, 3)])
    return (got, *beside) if beside else got


def all_reduce(mine, theirs, keep, send):
    half = add(mine, swap(theirs, "core", 1)).astype(BF)
    quarter = add(half[0], *[plane_swap(half[k], k, 0) for k in ORDER]).astype(BF)
    keep = add(keep, swap(send, "z", 1)).astype(BF)
    got = [plane_swap(quarter[k], k, 1) for k in ORDER[::-1]]
    got, keep = lax.optimization_barrier((got, keep))
    part = add(quarter[0], *got)
    part = sum_over_z(part, ((1, 7, 6), (2,)), BF).astype(BF)
    part, keep = lax.optimization_barrier((part, keep))
    quarter = gathered(part, 1)
    user = add(keep[0], *[swap(keep[i], "z", k) for i, k in ((1, 4), (2, 2), (3, 6))])
    half, user = gathered(quarter, 0, user)
    return half, swap(half, "core", 1), user


def on_device(user_emb, pos_feat, pos_id, neg_feat, neg_id, neg_bucket, logq_table, w_in, w_out):
    mine, near = pack(user_emb, pos_id, neg_feat, neg_id, neg_bucket)
    up, down = shift(mine, 1), shift(mine, -1)
    far = swap(near, "x_lo", 1)
    users = [mine, up, down]
    hid, feat, w_in = in_vmem(
        hidden_kernel,
        "hidden",
        2 * (N + U) * E * H,
        [((N + U, H), BF), ((N + U, E), BF), ((E, H), BF)],
        neg_feat,
        pos_feat,
        w_in,
    )
    up, down = shift(after(up, hid), 1), shift(after(down, hid), -1)
    users += [up, down]
    near_emb, pemb, w_out = in_vmem(
        embed_kernel, "embed", 2 * (N + U) * E * H, [((N, E), BF), ((U, E), BF), ((H, E), BF)], hid, w_out
    )
    up, down = shift(after(up, near_emb), 1), shift(after(down, near_emb), -1)
    users += [up, down]
    far_hid, far_emb, nid, bias = in_vmem(
        far_kernel,
        "far",
        4 * N * E * H,
        [((N, H), BF), ((N, E), BF), ((NN, 128), F32), ((NN, 128), F32)],
        near,
        far,
        w_in,
        w_out,
        logq_table.reshape(8, 128),
    )
    users += [shift(after(up, far_emb), 1)]
    none = jnp.zeros((NZ, U), F32)
    ks = tuple(range(NZ))
    tloc, tot, pexp, kept_a = score(ks[:FIRST], near_emb, far_emb, nid, bias, pemb, none, none, users)
    tloc, tot, _, kept_b = score(ks[FIRST:], near_emb, far_emb, nid, bias, pemb, tloc, tot, users)
    tot = sum_over_z(tot, ((1, 6, 7), (2,)), F32)
    g = item_grads(tot, tloc, pexp, kept_a, kept_b, users)
    keep, send, pterm = user_grads(tot, tloc, pexp, kept_a, kept_b, near_emb, far_emb, pemb)
    args = (g, feat, far, w_out, hid, far_hid)
    theirs_g = backward(False, *args)
    half, other, user = all_reduce(backward(True, *args), theirs_g, keep, send)
    w_in_grad, w_out_grad = finish(False, other, *finish(True, half))
    return user + pterm, w_in_grad, w_out_grad


def solution(mesh):
    rows = P(AXES, None)
    ids = P(AXES)
    return jax.shard_map(
        on_device,
        mesh=Mesh(mesh.devices.reshape(SIZES), AXES),
        in_specs=(rows, rows, ids, rows, ids, ids, P(), P(), P()),
        out_specs=(rows, P(), P()),
        check_vma=False,
    )
```

```python
import functools

import jax
import jax.numpy as jnp
from jax import lax
from jax.experimental import pallas as pl
from jax.experimental.pallas import tpu as pltpu
from jax.sharding import Mesh, PartitionSpec as P

AXES = ("x_lo", "z", "x_hi", "y", "core")
SIZES = (2, 8, 2, 4, 2)
BF, F32, I32 = jnp.bfloat16, jnp.float32, jnp.int32
SCALE = 0.125
SMALL = 2.0**-64
E, H, U, N = 256, 2048, 256, 512
NN = 2 * N
ROWS = NN + U
TILE = 256
CHUNKS = H // TILE
NZ = 8
ORDER = (3, 2, 1)
OFFSETS = (0, -1, 1, -2, 2, -3, 3, 4)
FIRST = 7
VMEM_LIMIT = 24 * 1024 * 1024

WIDE = 512
NT = (((1,), (1,)), ((), ()))
TN = (((0,), (0,)), ((), ()))


def params(limit=VMEM_LIMIT):
    return pltpu.CompilerParams(vmem_limit_bytes=limit)


def cost(flops, nbytes, trans=0):
    return pl.CostEstimate(flops=int(flops), bytes_accessed=int(nbytes), transcendentals=int(trans))


def whole(shape):
    return pl.BlockSpec(shape, lambda *_: (0,) * len(shape))


def mm(a, b):
    return jnp.dot(a, b, preferred_element_type=F32)


def start(src, dst, sem):
    copy = pltpu.make_async_copy(src, dst, sem)
    copy.start()
    return copy


def pack_kernel(user_hbm, pid_hbm, feat_hbm, nid_hbm, bucket_hbm, mine_ref, near_ref, pid_ref, nid_ref, bucket_ref, sems):
    copies = [
        start(pid_hbm, pid_ref, sems.at[0]),
        start(nid_hbm, nid_ref, sems.at[1]),
        start(bucket_hbm, bucket_ref, sems.at[2]),
        start(user_hbm, mine_ref.at[0:U], sems.at[3]),
        start(feat_hbm, near_ref.at[0:N], sems.at[4]),
    ]
    row = lax.broadcasted_iota(I32, (16, E), 0)

    def tail(digits):
        out = jnp.zeros((16, E), F32)
        for i, digit in enumerate(digits):
            out = jnp.where(row == i, digit.astype(F32), out)
        return out.astype(BF)

    def digits(ids, bits):
        ids = [ids[:, i : i + 256] for i in range(0, ids.shape[1], 256)]
        return [i >> bits for i in ids] + [i & (2**bits - 1) for i in ids]

    for copy in copies[:3]:
        copy.wait()
    mine_ref[U : U + 16] = tail(digits(pid_ref[...], 6))
    near_ref[N : N + 16] = tail(digits(nid_ref[...], 6) + digits(bucket_ref[...], 5))
    for copy in copies[3:]:
        copy.wait()


def pack(user_emb, pos_id, neg_feat, neg_id, neg_bucket):
    vm = pl.BlockSpec(memory_space=pltpu.VMEM)
    return pl.pallas_call(
        pack_kernel,
        in_specs=[pl.BlockSpec(memory_space=pltpu.HBM)] * 5,
        out_specs=[vm] * 2,
        out_shape=[jax.ShapeDtypeStruct((U + 16, E), BF), jax.ShapeDtypeStruct((N + 16, E), BF)],
        scratch_shapes=[
            pltpu.VMEM((1, U), I32),
            pltpu.VMEM((1, N), I32),
            pltpu.VMEM((1, N), I32),
            pltpu.SemaphoreType.DMA((5,)),
        ],
        compiler_params=params(60 * 1024 * 1024),
        cost_estimate=cost(1e10, 1e6),
        name="pack",
    )(user_emb, pos_id.reshape(1, U), neg_feat, neg_id.reshape(1, N), neg_bucket.reshape(1, N))


def hidden(feat, w_in_ref):
    return jnp.maximum(mm(feat, w_in_ref[...]), 0.0).astype(BF)


def hidden_kernel(near_ref, pos_ref, w_in_ref, hid_ref, feat_ref, w_in_out):
    for m, feat in enumerate((near_ref[0:TILE], near_ref[TILE:N], pos_ref[...])):
        rows = slice(m * TILE, (m + 1) * TILE)
        feat_ref[rows] = feat
        hid_ref[rows] = hidden(feat, w_in_ref)
    w_in_out[...] = w_in_ref[...]


def embed_kernel(hid_ref, w_out_ref, emb_ref, pemb_ref, w_out_out):
    w_out_out[...] = w_out_ref[...]
    for m, (ref, first) in enumerate([(emb_ref, 0), (emb_ref, TILE), (pemb_ref, 0)]):
        hid = hid_ref[m * TILE : (m + 1) * TILE]
        ref[first : first + TILE] = mm(hid, w_out_ref[...]).astype(BF)


def far_kernel(near_ref, far_ref, w_in_ref, w_out_ref, table_ref, hid_ref, emb_ref, nid_ref, bias_ref):
    lane = lax.broadcasted_iota(I32, (TILE, 128), 1).astype(F32)
    for side, tail in enumerate((near_ref[N : N + 16], far_ref[N : N + 16])):
        tail = jnp.concatenate([tail.astype(F32), jnp.zeros((112, E), F32)], axis=0).T
        for block in range(2):
            rows = slice((2 * side + block) * TILE, (2 * side + block + 1) * TILE)
            nid = tail[:, block : block + 1] * 64.0 + tail[:, block + 2 : block + 3]
            nid_ref[rows] = jnp.broadcast_to(nid, (TILE, 128))
            bucket = tail[:, block + 4 : block + 5] * 32.0 + tail[:, block + 6 : block + 7]
            found = jnp.zeros((TILE, 128), F32)
            for b in range(8):
                found = found + jnp.where(bucket == lane + 128.0 * b, table_ref[b : b + 1], 0.0)
            bias_ref[rows] = jnp.broadcast_to(jnp.sum(found, axis=1, keepdims=True), (TILE, 128))
    for m in range(N // TILE):
        rows = slice(m * TILE, (m + 1) * TILE)
        hid = hidden(far_ref[rows], w_in_ref)
        hid_ref[rows] = hid
        emb_ref[rows] = mm(hid, w_out_ref[...]).astype(BF)


def in_vmem(kernel, name, flops, outs, *args, scratch=()):
    vm = pl.BlockSpec(memory_space=pltpu.VMEM)
    return pl.pallas_call(
        kernel,
        in_specs=[vm] * len(args),
        out_specs=[vm] * len(outs),
        out_shape=[jax.ShapeDtypeStruct(shape, dtype) for shape, dtype in outs],
        scratch_shapes=list(scratch),
        compiler_params=params(14 * 1024 * 1024),
        cost_estimate=cost(flops, 4e6),
        name=name,
    )(*args)


def twice(x):
    return jnp.concatenate([x, x], axis=1)


def home(z, k):
    return (z + OFFSETS[k] + NZ) & (NZ - 1)


def score_kernel(ks, near_emb, far_emb, nid_ref, bias_ref, pemb_ref, tloc_in, tin_in, *rest):
    users = rest[: len(ks)]
    tloc_ref, tin_ref, pexp_ref, kept_ref, kf = rest[len(ks) :]
    z = lax.axis_index("z")
    tloc_ref[...] = tloc_in[...]
    tin_ref[...] = tin_in[...]
    if ks[0] == 0:
        prod = users[0][0:U].astype(F32) * pemb_ref[...].astype(F32)
        prod = (prod[:, 0:128] + prod[:, 128:256]).T
        pexp_ref[...] = jnp.exp(SCALE * jnp.sum(prod, axis=0, keepdims=True))
    else:
        pexp_ref[...] = jnp.zeros_like(pexp_ref)
    for i, k in enumerate(ks):
        u = (users[i][0:U].astype(F32) * SCALE).astype(BF)
        tail = users[i][U : U + 16].astype(F32)
        pid = tail[0:1] * 64.0 + tail[1:2]
        total = jnp.zeros((8, U), F32)
        for m in range(NN // TILE):
            rows = slice(m * TILE, (m + 1) * TILE)
            emb = near_emb[rows] if m < 2 else far_emb[(m - 2) * TILE : (m - 1) * TILE]
            sc = lax.dot_general(emb, u, NT, preferred_element_type=F32) - twice(bias_ref[rows])
            kept = jnp.where(twice(nid_ref[rows]) != pid, jnp.exp(sc), 0.0)
            kf[rows] = kept
            total = total + jnp.sum(kept.reshape(TILE // 8, 8, U), axis=0)
        t = jnp.sum(total, axis=0, keepdims=True)
        shrink = jnp.where(t > 1.0, SMALL, 1.0)
        inv = jnp.where(t > 0.0, 1.0 / (t * shrink), 0.0)
        @pl.loop(0, NN // TILE)
        def _(m, i=i, shrink=shrink, inv=inv):
            rows = pl.ds(pl.multiple_of(m * TILE, TILE), TILE)
            kept_ref[rows, i * U : (i + 1) * U] = ((kf[rows, :] * shrink) * inv).astype(BF)

        row = pl.ds(home(z, k), 1)
        tloc_ref[row, :] = t
        tin_ref[row, :] = t + pexp_ref[...] if k == 0 else t


def score(ks, near_emb, far_emb, nid, bias, pemb, tloc, tin, users):
    vm = pl.BlockSpec(memory_space=pltpu.VMEM)
    n = len(ks)
    return pl.pallas_call(
        functools.partial(score_kernel, ks),
        in_specs=[vm] * (7 + n),
        out_specs=[vm] * 4,
        out_shape=[
            jax.ShapeDtypeStruct((NZ, U), F32),
            jax.ShapeDtypeStruct((NZ, U), F32),
            jax.ShapeDtypeStruct((1, U), F32),
            jax.ShapeDtypeStruct((NN, n * U), BF),
        ],
        scratch_shapes=[pltpu.VMEM((NN, U), F32)],
        compiler_params=params(14 * 1024 * 1024),
        cost_estimate=cost(2 * n * U * NN * E, 5e6, n * U * NN),
        name="score",
    )(near_emb, far_emb, nid, bias, pemb, tloc, tin, *[users[k] for k in ks])


def ratios(tot_ref, tloc_ref, pexp_ref, ratio, rel):
    z = lax.axis_index("z")
    tot = tot_ref[...]
    shrink = jnp.where(tot > 1.0, SMALL, 1.0)
    ratio[...] = (tloc_ref[...] * shrink) * (1.0 / (tot * shrink))
    own = tot_ref[pl.ds(z, 1), :]
    shrink = jnp.where(own > 1.0, SMALL, 1.0)
    pprob = (pexp_ref[...] * shrink) * (1.0 / (own * shrink))
    rel[...] = jnp.zeros_like(rel)
    for k in range(NZ):
        rel[k : k + 1] = SCALE * ratio[pl.ds(home(z, k), 1), :]
    rel[NZ : NZ + 1] = SCALE * (pprob - 1.0)
    return rel[...].T


RATIOS = [pltpu.VMEM((NZ, U), F32), pltpu.VMEM((128, U), F32)]


def item_grad_kernel(tot_ref, tloc_ref, pexp_ref, kept_a, kept_b, *rest):
    users = rest[:NZ]
    g_ref, wu, ratio, rel = rest[NZ:]
    cols = ratios(tot_ref, tloc_ref, pexp_ref, ratio, rel)
    for k in range(NZ):
        wu[k * U : (k + 1) * U] = (users[k][0:U].astype(F32) * cols[:, k : k + 1]).astype(BF)
    g_ref[N : N + U] = (users[0][0:U].astype(F32) * cols[:, NZ : NZ + 1]).astype(BF)
    for m in range(NN // TILE):
        rows = slice(m * TILE, (m + 1) * TILE)
        g = mm(kept_a[rows], wu[0 : FIRST * U]) + mm(kept_b[rows], wu[FIRST * U :])
        first = m * TILE if m < 2 else m * TILE + U
        g_ref[first : first + TILE] = g.astype(BF)


def user_grad_kernel(tot_ref, tloc_ref, pexp_ref, kept_a, kept_b, near_emb, far_emb, pemb_ref, *rest):
    keep_ref, send_ref, pterm_ref, ratio, rel = rest
    z = lax.axis_index("z")
    cols = ratios(tot_ref, tloc_ref, pexp_ref, ratio, rel)
    pterm_ref[...] = pemb_ref[...].astype(F32) * cols[:, NZ : NZ + 1]
    for k in range(NZ):
        kept, i = (kept_a, k) if k < FIRST else (kept_b, k - FIRST)
        cols_k = slice(i * U, (i + 1) * U)
        ug = lax.dot_general(kept[0:N, cols_k], near_emb[...], TN, preferred_element_type=F32)
        ug = ug + lax.dot_general(kept[N:NN, cols_k], far_emb[...], TN, preferred_element_type=F32)
        apart = jnp.bitwise_xor(home(z, k), z)
        place = (apart & 2) + (apart >> 2)
        (send_ref if OFFSETS[k] % 2 else keep_ref)[place] = (ug * cols[:, k : k + 1]).astype(BF)


def item_grads(tot, tloc, pexp, kept_a, kept_b, users):
    scratch = [pltpu.VMEM((NZ * U, E), BF)] + RATIOS
    args = (tot, tloc, pexp, kept_a, kept_b, *users)
    return in_vmem(item_grad_kernel, "items", 2 * NZ * U * NN * E, [((ROWS, E), BF)], *args, scratch=scratch)[0]


def user_grads(*args):
    outs = [((NZ // 2, U, E), BF), ((NZ // 2, U, E), BF), ((U, E), F32)]
    return in_vmem(user_grad_kernel, "users", 2 * NZ * U * NN * E, outs, *args, scratch=RATIOS)


def order():
    core = lax.axis_index("core")
    xx, y = near(lax.axis_index("x_hi") * 2 + lax.axis_index("x_lo")), near(lax.axis_index("y"))
    return core, jnp.where(core == 0, xx, y), jnp.where(core == 0, y, xx)


def back_kernel(mine, g_ref, feat_ref, far_ref, w_out_ref, hid_ref, far_hid, out_ref):
    core, first, second = order()
    if not mine:
        core, first, second = 1 - core, second, first
    for c in range(2):
        cols = pl.ds(pl.multiple_of(core * (H // 2) + c * WIDE, WIDE), WIDE)
        w_in = w_out = 0.0
        for rows, feat, hid in ((slice(0, N + U), feat_ref, hid_ref), (slice(N + U, ROWS), far_ref, far_hid)):
            hid = hid[:, cols]
            g = g_ref[rows]
            back = lax.dot_general(g, w_out_ref[cols], NT, preferred_element_type=F32)
            back = jnp.where(hid > 0, back, 0.0).astype(BF)
            w_in += lax.dot_general(feat[0 : g.shape[0]], back, TN, preferred_element_type=F32)
            w_out += lax.dot_general(hid, g, TN, preferred_element_type=F32)
        w_in, w_out = w_in.astype(BF), w_out.astype(BF)
        for t in range(2):
            for half in range(2):
                inner = jnp.bitwise_xor(second, 2 * t + half)
                rows = slice(half * 128, (half + 1) * 128)
                out_ref[jnp.bitwise_xor(first, c), inner] = w_in[rows, t * TILE : (t + 1) * TILE]
                rows = slice(t * TILE + half * 128, t * TILE + (half + 1) * 128)
                out_ref[jnp.bitwise_xor(first, 2 + c), inner] = w_out[rows]


def backward(mine, *args):
    return in_vmem(
        functools.partial(back_kernel, mine), "backward", 3 * ROWS * E * H, [((4, 4, 128, TILE), BF)], *args
    )[0]


def finish_kernel(mine, x_ref, *rest):
    w_in_hbm, w_out_hbm, a, b, sems = rest[-5:]
    core, first, second = order()
    if not mine:
        core, first, second = 1 - core, second, first
    copies = []
    for c in range(2):
        for t in range(2):
            for half in range(2):
                inner = jnp.bitwise_xor(second, 2 * t + half)
                start_t = c * WIDE + t * TILE
                cols = slice(start_t, start_t + TILE)
                a[half * 128 : (half + 1) * 128, cols] = x_ref[jnp.bitwise_xor(first, c), inner].astype(F32)
                rows = slice(start_t + half * 128, start_t + (half + 1) * 128)
                b[rows] = x_ref[jnp.bitwise_xor(first, 2 + c), inner].astype(F32)
        here = pl.ds(c * WIDE, WIDE)
        there = pl.ds(pl.multiple_of(core * (H // 2) + c * WIDE, WIDE), WIDE)
        copies.append(start(a.at[:, here], w_in_hbm.at[:, there], sems.at[2 * c]))
        copies.append(start(b.at[here], w_out_hbm.at[there], sems.at[2 * c + 1]))
    for copy in copies:
        copy.wait()


def finish(mine, x, *outs):
    vm, hbm = pl.BlockSpec(memory_space=pltpu.VMEM), pl.BlockSpec(memory_space=pl.ANY)
    return pl.pallas_call(
        functools.partial(finish_kernel, mine),
        in_specs=[vm] + [hbm] * len(outs),
        out_specs=[hbm, hbm],
        out_shape=[jax.ShapeDtypeStruct((E, H), F32), jax.ShapeDtypeStruct((H, E), F32)],
        scratch_shapes=[
            pltpu.VMEM((E, H // 2), F32),
            pltpu.VMEM((H // 2, E), F32),
            pltpu.SemaphoreType.DMA((4,)),
        ],
        input_output_aliases={1: 0, 2: 1} if outs else {},
        compiler_params=params(14 * 1024 * 1024),
        cost_estimate=cost(0, 3e6),
        name="finish",
    )(x, *outs)


def swap(x, axis, k):
    return lax.ppermute(x, axis, [(i, i ^ k) for i in range(SIZES[AXES.index(axis)])])


def after(x, *needed):
    return lax.optimization_barrier((x, *needed))[0]


def shift(x, by):
    return lax.ppermute(x, "z", [(i, (i + by) % NZ) for i in range(NZ)])


def device(x_lo, z, x_hi, y, core):
    return (((x_lo * 8 + z) * 2 + x_hi) * 4 + y) * 2 + core


def near(place):
    return place ^ (place >> 1)


def plane_swap(x, k, x_core):
    pairs = []
    for z in range(8):
        for xx in range(4):
            for y in range(4):
                for core in range(2):
                    to_x, to_y = (near(near(xx) ^ k), y) if core == x_core else (xx, near(near(y) ^ k))
                    pairs.append(
                        (device(xx & 1, z, xx >> 1, y, core), device(to_x & 1, z, to_x >> 1, to_y, core))
                    )
    return lax.ppermute(x, AXES, pairs)


def add(*terms):
    return sum(t.astype(F32) for t in terms)


def sum_over_z(x, rounds, dtype):
    for ks in rounds:
        sent = x.astype(dtype)
        terms = [t.astype(F32) for t in [sent] + [swap(sent, "z", k) for k in ks]]
        while len(terms) > 1:
            terms = [a + b for a, b in zip(terms[::2], terms[1::2])]
        x = terms[0]
    return x


def gathered(x, x_core, *beside):
    got = {k: plane_swap(x, k, x_core) for k in (1, 2, 3)}
    if beside:
        got, beside = lax.optimization_barrier((got, beside))
    got = jnp.stack([x] + [got[k] for k in (1, 2, 3)])
    return (got, *beside) if beside else got


def all_reduce(mine, theirs, keep, send):
    half = add(mine, swap(theirs, "core", 1)).astype(BF)
    quarter = add(half[0], *[plane_swap(half[k], k, 0) for k in ORDER]).astype(BF)
    keep = add(keep, swap(send, "z", 1)).astype(BF)
    got = [plane_swap(quarter[k], k, 1) for k in ORDER[::-1]]
    got, keep = lax.optimization_barrier((got, keep))
    part = add(quarter[0], *got)
    part = sum_over_z(part, ((1, 7, 6), (2,)), BF).astype(BF)
    part, keep = lax.optimization_barrier((part, keep))
    quarter = gathered(part, 1)
    user = add(keep[0], *[swap(keep[i], "z", k) for i, k in ((1, 4), (2, 2), (3, 6))])
    half, user = gathered(quarter, 0, user)
    return half, swap(half, "core", 1), user


def on_device(user_emb, pos_feat, pos_id, neg_feat, neg_id, neg_bucket, logq_table, w_in, w_out):
    mine, near = pack(user_emb, pos_id, neg_feat, neg_id, neg_bucket)
    up, down = shift(mine, 1), shift(mine, -1)
    far = swap(near, "x_lo", 1)
    users = [mine, up, down]
    hid, feat, w_in = in_vmem(
        hidden_kernel,
        "hidden",
        2 * (N + U) * E * H,
        [((N + U, H), BF), ((N + U, E), BF), ((E, H), BF)],
        neg_feat,
        pos_feat,
        w_in,
    )
    up, down = shift(after(up, hid), 1), shift(after(down, hid), -1)
    users += [up, down]
    near_emb, pemb, w_out = in_vmem(
        embed_kernel, "embed", 2 * (N + U) * E * H, [((N, E), BF), ((U, E), BF), ((H, E), BF)], hid, w_out
    )
    up, down = shift(after(up, near_emb), 1), shift(after(down, near_emb), -1)
    users += [up, down]
    far_hid, far_emb, nid, bias = in_vmem(
        far_kernel,
        "far",
        4 * N * E * H,
        [((N, H), BF), ((N, E), BF), ((NN, 128), F32), ((NN, 128), F32)],
        near,
        far,
        w_in,
        w_out,
        logq_table.reshape(8, 128),
    )
    users += [shift(after(up, far_emb), 1)]
    none = jnp.zeros((NZ, U), F32)
    ks = tuple(range(NZ))
    tloc, tot, pexp, kept_a = score(ks[:FIRST], near_emb, far_emb, nid, bias, pemb, none, none, users)
    tloc, tot, _, kept_b = score(ks[FIRST:], near_emb, far_emb, nid, bias, pemb, tloc, tot, users)
    tot = sum_over_z(tot, ((1, 6, 7), (2,)), F32)
    g = item_grads(tot, tloc, pexp, kept_a, kept_b, users)
    keep, send, pterm = user_grads(tot, tloc, pexp, kept_a, kept_b, near_emb, far_emb, pemb)
    args = (g, feat, far, w_out, hid, far_hid)
    theirs_g = backward(False, *args)
    half, other, user = all_reduce(backward(True, *args), theirs_g, keep, send)
    w_in_grad, w_out_grad = finish(False, other, *finish(True, half))
    return user + pterm, w_in_grad, w_out_grad


def solution(mesh):
    rows = P(AXES, None)
    ids = P(AXES)
    return jax.shard_map(
        on_device,
        mesh=Mesh(mesh.devices.reshape(SIZES), AXES),
        in_specs=(rows, rows, ids, rows, ids, ids, P(), P(), P()),
        out_specs=(rows, P(), P()),
        check_vma=False,
    )
```

```python
import functools

import jax
import jax.numpy as jnp
from jax import lax
from jax.experimental import pallas as pl
from jax.experimental.pallas import tpu as pltpu
from jax.sharding import Mesh, PartitionSpec as P

AXES = ("x_lo", "z", "x_hi", "y", "core")
SIZES = (2, 8, 2, 4, 2)
BF, F32, I32 = jnp.bfloat16, jnp.float32, jnp.int32
SCALE = 0.125
SMALL = 2.0**-64
E, H, U, N = 256, 2048, 256, 512
NN = 2 * N
ROWS = NN + U
TILE = 256
CHUNKS = H // TILE
NZ = 8
ORDER = (3, 2, 1)
OFFSETS = (0, -1, 1, -2, 2, -3, 3, 4)
FIRST = 7
VMEM_LIMIT = 24 * 1024 * 1024

WIDE = 512
NT = (((1,), (1,)), ((), ()))
TN = (((0,), (0,)), ((), ()))


def params(limit=VMEM_LIMIT):
    return pltpu.CompilerParams(vmem_limit_bytes=limit)


def cost(flops, nbytes, trans=0):
    return pl.CostEstimate(flops=int(flops), bytes_accessed=int(nbytes), transcendentals=int(trans))


def whole(shape):
    return pl.BlockSpec(shape, lambda *_: (0,) * len(shape))


def mm(a, b):
    return jnp.dot(a, b, preferred_element_type=F32)


def start(src, dst, sem):
    copy = pltpu.make_async_copy(src, dst, sem)
    copy.start()
    return copy


def pack_kernel(user_hbm, pid_hbm, feat_hbm, nid_hbm, bucket_hbm, mine_ref, near_ref, pid_ref, nid_ref, bucket_ref, sems):
    copies = [
        start(pid_hbm, pid_ref, sems.at[0]),
        start(nid_hbm, nid_ref, sems.at[1]),
        start(bucket_hbm, bucket_ref, sems.at[2]),
        start(user_hbm, mine_ref.at[0:U], sems.at[3]),
        start(feat_hbm, near_ref.at[0:N], sems.at[4]),
    ]
    row = lax.broadcasted_iota(I32, (16, E), 0)

    def tail(digits):
        out = jnp.zeros((16, E), F32)
        for i, digit in enumerate(digits):
            out = jnp.where(row == i, digit.astype(F32), out)
        return out.astype(BF)

    def digits(ids, bits):
        ids = [ids[:, i : i + 256] for i in range(0, ids.shape[1], 256)]
        return [i >> bits for i in ids] + [i & (2**bits - 1) for i in ids]

    for copy in copies[:3]:
        copy.wait()
    mine_ref[U : U + 16] = tail(digits(pid_ref[...], 6))
    near_ref[N : N + 16] = tail(digits(nid_ref[...], 6) + digits(bucket_ref[...], 5))
    for copy in copies[3:]:
        copy.wait()


def pack(user_emb, pos_id, neg_feat, neg_id, neg_bucket):
    vm = pl.BlockSpec(memory_space=pltpu.VMEM)
    return pl.pallas_call(
        pack_kernel,
        in_specs=[pl.BlockSpec(memory_space=pltpu.HBM)] * 5,
        out_specs=[vm] * 2,
        out_shape=[jax.ShapeDtypeStruct((U + 16, E), BF), jax.ShapeDtypeStruct((N + 16, E), BF)],
        scratch_shapes=[
            pltpu.VMEM((1, U), I32),
            pltpu.VMEM((1, N), I32),
            pltpu.VMEM((1, N), I32),
            pltpu.SemaphoreType.DMA((5,)),
        ],
        compiler_params=params(60 * 1024 * 1024),
        cost_estimate=cost(1e10, 1e6),
        name="pack",
    )(user_emb, pos_id.reshape(1, U), neg_feat, neg_id.reshape(1, N), neg_bucket.reshape(1, N))


def hidden(feat, w_in_ref):
    return jnp.maximum(mm(feat, w_in_ref[...]), 0.0).astype(BF)


def hidden_kernel(near_ref, pos_ref, w_in_ref, hid_ref, feat_ref, w_in_out):
    for m, feat in enumerate((near_ref[0:TILE], near_ref[TILE:N], pos_ref[...])):
        rows = slice(m * TILE, (m + 1) * TILE)
        feat_ref[rows] = feat
        hid_ref[rows] = hidden(feat, w_in_ref)
    w_in_out[...] = w_in_ref[...]


def embed_kernel(hid_ref, w_out_ref, emb_ref, pemb_ref, w_out_out):
    w_out_out[...] = w_out_ref[...]
    pemb_ref[...] = mm(hid_ref[N : N + U], w_out_ref[...]).astype(BF)

    @pl.loop(0, N // TILE)
    def _(m):
        rows = pl.ds(pl.multiple_of(m * TILE, TILE), TILE)
        emb_ref[rows, :] = mm(hid_ref[rows, :], w_out_ref[...]).astype(BF)


def far_kernel(near_ref, far_ref, w_in_ref, w_out_ref, table_ref, hid_ref, emb_ref, nid_ref, bias_ref):
    lane = lax.broadcasted_iota(I32, (TILE, 128), 1).astype(F32)
    for side, tail in enumerate((near_ref[N : N + 16], far_ref[N : N + 16])):
        tail = jnp.concatenate([tail.astype(F32), jnp.zeros((112, E), F32)], axis=0).T
        for block in range(2):
            rows = slice((2 * side + block) * TILE, (2 * side + block + 1) * TILE)
            nid = tail[:, block : block + 1] * 64.0 + tail[:, block + 2 : block + 3]
            nid_ref[rows] = jnp.broadcast_to(nid, (TILE, 128))
            bucket = tail[:, block + 4 : block + 5] * 32.0 + tail[:, block + 6 : block + 7]
            found = jnp.zeros((TILE, 128), F32)
            for b in range(8):
                found = found + jnp.where(bucket == lane + 128.0 * b, table_ref[b : b + 1], 0.0)
            bias_ref[rows] = jnp.broadcast_to(jnp.sum(found, axis=1, keepdims=True), (TILE, 128))

    @pl.loop(0, N // TILE)
    def _(m):
        rows = pl.ds(pl.multiple_of(m * TILE, TILE), TILE)
        hid = hidden(far_ref[rows, :], w_in_ref)
        hid_ref[rows, :] = hid
        emb_ref[rows, :] = mm(hid, w_out_ref[...]).astype(BF)


def in_vmem(kernel, name, flops, outs, *args, scratch=()):
    vm = pl.BlockSpec(memory_space=pltpu.VMEM)
    return pl.pallas_call(
        kernel,
        in_specs=[vm] * len(args),
        out_specs=[vm] * len(outs),
        out_shape=[jax.ShapeDtypeStruct(shape, dtype) for shape, dtype in outs],
        scratch_shapes=list(scratch),
        compiler_params=params(14 * 1024 * 1024),
        cost_estimate=cost(flops, 4e6),
        name=name,
    )(*args)


def twice(x):
    return jnp.concatenate([x, x], axis=1)


def home(z, k):
    return (z + OFFSETS[k] + NZ) & (NZ - 1)


def score_kernel(ks, near_emb, far_emb, nid_ref, bias_ref, pemb_ref, tloc_in, tin_in, *rest):
    users = rest[: len(ks)]
    tloc_ref, tin_ref, pexp_ref, kept_ref, kf = rest[len(ks) :]
    z = lax.axis_index("z")
    tloc_ref[...] = tloc_in[...]
    tin_ref[...] = tin_in[...]
    if ks[0] == 0:
        prod = users[0][0:U].astype(F32) * pemb_ref[...].astype(F32)
        prod = (prod[:, 0:128] + prod[:, 128:256]).T
        pexp_ref[...] = jnp.exp(SCALE * jnp.sum(prod, axis=0, keepdims=True))
    else:
        pexp_ref[...] = jnp.zeros_like(pexp_ref)
    for i, k in enumerate(ks):
        u = (users[i][0:U].astype(F32) * SCALE).astype(BF)
        tail = users[i][U : U + 16].astype(F32)
        pid = tail[0:1] * 64.0 + tail[1:2]
        total = jnp.zeros((8, U), F32)
        for m in range(NN // TILE):
            rows = slice(m * TILE, (m + 1) * TILE)
            emb = near_emb[rows] if m < 2 else far_emb[(m - 2) * TILE : (m - 1) * TILE]
            sc = lax.dot_general(emb, u, NT, preferred_element_type=F32) - twice(bias_ref[rows])
            kept = jnp.where(twice(nid_ref[rows]) != pid, jnp.exp(sc), 0.0)
            kf[rows] = kept
            total = total + jnp.sum(kept.reshape(TILE // 8, 8, U), axis=0)
        t = jnp.sum(total, axis=0, keepdims=True)
        shrink = jnp.where(t > 1.0, SMALL, 1.0)
        inv = jnp.where(t > 0.0, 1.0 / (t * shrink), 0.0)
        @pl.loop(0, NN // TILE)
        def _(m, i=i, shrink=shrink, inv=inv):
            rows = pl.ds(pl.multiple_of(m * TILE, TILE), TILE)
            kept_ref[rows, i * U : (i + 1) * U] = ((kf[rows, :] * shrink) * inv).astype(BF)

        row = pl.ds(home(z, k), 1)
        tloc_ref[row, :] = t
        tin_ref[row, :] = t + pexp_ref[...] if k == 0 else t


def score(ks, near_emb, far_emb, nid, bias, pemb, tloc, tin, users):
    vm = pl.BlockSpec(memory_space=pltpu.VMEM)
    n = len(ks)
    return pl.pallas_call(
        functools.partial(score_kernel, ks),
        in_specs=[vm] * (7 + n),
        out_specs=[vm] * 4,
        out_shape=[
            jax.ShapeDtypeStruct((NZ, U), F32),
            jax.ShapeDtypeStruct((NZ, U), F32),
            jax.ShapeDtypeStruct((1, U), F32),
            jax.ShapeDtypeStruct((NN, n * U), BF),
        ],
        scratch_shapes=[pltpu.VMEM((NN, U), F32)],
        compiler_params=params(14 * 1024 * 1024),
        cost_estimate=cost(2 * n * U * NN * E, 5e6, n * U * NN),
        name="score",
    )(near_emb, far_emb, nid, bias, pemb, tloc, tin, *[users[k] for k in ks])


def ratios(tot_ref, tloc_ref, pexp_ref, ratio, rel):
    z = lax.axis_index("z")
    tot = tot_ref[...]
    shrink = jnp.where(tot > 1.0, SMALL, 1.0)
    ratio[...] = (tloc_ref[...] * shrink) * (1.0 / (tot * shrink))
    own = tot_ref[pl.ds(z, 1), :]
    shrink = jnp.where(own > 1.0, SMALL, 1.0)
    pprob = (pexp_ref[...] * shrink) * (1.0 / (own * shrink))
    rel[...] = jnp.zeros_like(rel)
    for k in range(NZ):
        rel[k : k + 1] = SCALE * ratio[pl.ds(home(z, k), 1), :]
    rel[NZ : NZ + 1] = SCALE * (pprob - 1.0)
    return rel[...].T


RATIOS = [pltpu.VMEM((NZ, U), F32), pltpu.VMEM((128, U), F32)]


def item_grad_kernel(tot_ref, tloc_ref, pexp_ref, kept_a, kept_b, *rest):
    users = rest[:NZ]
    g_ref, wu, ratio, rel = rest[NZ:]
    cols = ratios(tot_ref, tloc_ref, pexp_ref, ratio, rel)
    for k in range(NZ):
        wu[k * U : (k + 1) * U] = (users[k][0:U].astype(F32) * cols[:, k : k + 1]).astype(BF)
    g_ref[N : N + U] = (users[0][0:U].astype(F32) * cols[:, NZ : NZ + 1]).astype(BF)
    for m in range(NN // TILE):
        rows = slice(m * TILE, (m + 1) * TILE)
        g = mm(kept_a[rows], wu[0 : FIRST * U]) + mm(kept_b[rows], wu[FIRST * U :])
        first = m * TILE if m < 2 else m * TILE + U
        g_ref[first : first + TILE] = g.astype(BF)


def user_grad_kernel(odd, tot_ref, tloc_ref, pexp_ref, kept_a, kept_b, near_emb, far_emb, pemb_ref, out_ref, *rest):
    z = lax.axis_index("z")
    cols = ratios(tot_ref, tloc_ref, pexp_ref, *rest[-2:])
    if not odd:
        rest[0][...] = pemb_ref[...].astype(F32) * cols[:, NZ : NZ + 1]
    for k in range(NZ):
        if OFFSETS[k] % 2 != odd:
            continue
        kept, i = (kept_a, k) if k < FIRST else (kept_b, k - FIRST)
        cols_k = slice(i * U, (i + 1) * U)
        ug = lax.dot_general(kept[0:N, cols_k], near_emb[...], TN, preferred_element_type=F32)
        ug = ug + lax.dot_general(kept[N:NN, cols_k], far_emb[...], TN, preferred_element_type=F32)
        apart = jnp.bitwise_xor(home(z, k), z)
        place = (apart & 2) + (apart >> 2)
        out_ref[place] = (ug * cols[:, k : k + 1]).astype(BF)


def item_grads(tot, tloc, pexp, kept_a, kept_b, users):
    scratch = [pltpu.VMEM((NZ * U, E), BF)] + RATIOS
    args = (tot, tloc, pexp, kept_a, kept_b, *users)
    return in_vmem(item_grad_kernel, "items", 2 * NZ * U * NN * E, [((ROWS, E), BF)], *args, scratch=scratch)[0]


def user_grads(odd, *args):
    outs = [((NZ // 2, U, E), BF)] + ([] if odd else [((U, E), F32)])
    kernel = functools.partial(user_grad_kernel, odd)
    return in_vmem(kernel, "users", NZ * U * NN * E, outs, *args, scratch=RATIOS)


def order():
    core = lax.axis_index("core")
    xx, y = near(lax.axis_index("x_hi") * 2 + lax.axis_index("x_lo")), near(lax.axis_index("y"))
    return core, jnp.where(core == 0, xx, y), jnp.where(core == 0, y, xx)


def back_kernel(mine, g_ref, feat_ref, far_ref, w_out_ref, hid_ref, far_hid, out_ref):
    core, first, second = order()
    if not mine:
        core, first, second = 1 - core, second, first
    for c in range(2):
        cols = pl.ds(pl.multiple_of(core * (H // 2) + c * WIDE, WIDE), WIDE)
        w_in = w_out = 0.0
        for rows, feat, hid in ((slice(0, N + U), feat_ref, hid_ref), (slice(N + U, ROWS), far_ref, far_hid)):
            hid = hid[:, cols]
            g = g_ref[rows]
            back = lax.dot_general(g, w_out_ref[cols], NT, preferred_element_type=F32)
            back = jnp.where(hid > 0, back, 0.0).astype(BF)
            w_in += lax.dot_general(feat[0 : g.shape[0]], back, TN, preferred_element_type=F32)
            w_out += lax.dot_general(hid, g, TN, preferred_element_type=F32)
        w_in, w_out = w_in.astype(BF), w_out.astype(BF)
        for t in range(2):
            for half in range(2):
                inner = jnp.bitwise_xor(second, 2 * t + half)
                rows = slice(half * 128, (half + 1) * 128)
                out_ref[jnp.bitwise_xor(first, c), inner] = w_in[rows, t * TILE : (t + 1) * TILE]
                rows = slice(t * TILE + half * 128, t * TILE + (half + 1) * 128)
                out_ref[jnp.bitwise_xor(first, 2 + c), inner] = w_out[rows]


def backward(mine, *args):
    return in_vmem(
        functools.partial(back_kernel, mine), "backward", 3 * ROWS * E * H, [((4, 4, 128, TILE), BF)], *args
    )[0]


def finish_kernel(mine, x_ref, *rest):
    w_in_hbm, w_out_hbm, a, b, sems = rest[-5:]
    core, first, second = order()
    if not mine:
        core, first, second = 1 - core, second, first
    copies = []
    for c in range(2):
        for t in range(2):
            for half in range(2):
                inner = jnp.bitwise_xor(second, 2 * t + half)
                start_t = c * WIDE + t * TILE
                cols = slice(start_t, start_t + TILE)
                a[half * 128 : (half + 1) * 128, cols] = x_ref[jnp.bitwise_xor(first, c), inner].astype(F32)
                rows = slice(start_t + half * 128, start_t + (half + 1) * 128)
                b[rows] = x_ref[jnp.bitwise_xor(first, 2 + c), inner].astype(F32)
        here = pl.ds(c * WIDE, WIDE)
        there = pl.ds(pl.multiple_of(core * (H // 2) + c * WIDE, WIDE), WIDE)
        copies.append(start(a.at[:, here], w_in_hbm.at[:, there], sems.at[2 * c]))
        copies.append(start(b.at[here], w_out_hbm.at[there], sems.at[2 * c + 1]))
    for copy in copies:
        copy.wait()


def finish(mine, x, *outs):
    vm, hbm = pl.BlockSpec(memory_space=pltpu.VMEM), pl.BlockSpec(memory_space=pl.ANY)
    return pl.pallas_call(
        functools.partial(finish_kernel, mine),
        in_specs=[vm] + [hbm] * len(outs),
        out_specs=[hbm, hbm],
        out_shape=[jax.ShapeDtypeStruct((E, H), F32), jax.ShapeDtypeStruct((H, E), F32)],
        scratch_shapes=[
            pltpu.VMEM((E, H // 2), F32),
            pltpu.VMEM((H // 2, E), F32),
            pltpu.SemaphoreType.DMA((4,)),
        ],
        input_output_aliases={1: 0, 2: 1} if outs else {},
        compiler_params=params(14 * 1024 * 1024),
        cost_estimate=cost(0, 3e6),
        name="finish",
    )(x, *outs)


def swap(x, axis, k):
    return lax.ppermute(x, axis, [(i, i ^ k) for i in range(SIZES[AXES.index(axis)])])


def after(x, *needed):
    return lax.optimization_barrier((x, *needed))[0]


def shift(x, by):
    return lax.ppermute(x, "z", [(i, (i + by) % NZ) for i in range(NZ)])


def device(x_lo, z, x_hi, y, core):
    return (((x_lo * 8 + z) * 2 + x_hi) * 4 + y) * 2 + core


def near(place):
    return place ^ (place >> 1)


def plane_swap(x, k, x_core):
    pairs = []
    for z in range(8):
        for xx in range(4):
            for y in range(4):
                for core in range(2):
                    to_x, to_y = (near(near(xx) ^ k), y) if core == x_core else (xx, near(near(y) ^ k))
                    pairs.append(
                        (device(xx & 1, z, xx >> 1, y, core), device(to_x & 1, z, to_x >> 1, to_y, core))
                    )
    return lax.ppermute(x, AXES, pairs)


def add(*terms):
    return sum(t.astype(F32) for t in terms)


def sum_over_z(x, rounds, dtype):
    for ks in rounds:
        sent = x.astype(dtype)
        terms = [t.astype(F32) for t in [sent] + [swap(sent, "z", k) for k in ks]]
        while len(terms) > 1:
            terms = [a + b for a, b in zip(terms[::2], terms[1::2])]
        x = terms[0]
    return x


def gathered(x, x_core, *beside):
    got = {k: plane_swap(x, k, x_core) for k in (1, 2, 3)}
    if beside:
        got, beside = lax.optimization_barrier((got, beside))
    got = jnp.stack([x] + [got[k] for k in (1, 2, 3)])
    return (got, *beside) if beside else got


def all_reduce(mine, theirs, keep, send):
    half = add(mine, swap(theirs, "core", 1)).astype(BF)
    quarter = add(half[0], *[plane_swap(half[k], k, 0) for k in ORDER]).astype(BF)
    keep = add(keep, swap(send, "z", 1)).astype(BF)
    got = [plane_swap(quarter[k], k, 1) for k in ORDER[::-1]]
    got, keep = lax.optimization_barrier((got, keep))
    part = add(quarter[0], *got)
    part = sum_over_z(part, ((1, 7, 6), (2,)), BF).astype(BF)
    part, keep = lax.optimization_barrier((part, keep))
    quarter = gathered(part, 1)
    user = add(keep[0], *[swap(keep[i], "z", k) for i, k in ((1, 4), (2, 2), (3, 6))])
    half, user = gathered(quarter, 0, user)
    return half, swap(half, "core", 1), user


def on_device(user_emb, pos_feat, pos_id, neg_feat, neg_id, neg_bucket, logq_table, w_in, w_out):
    mine, near = pack(user_emb, pos_id, neg_feat, neg_id, neg_bucket)
    up, down = shift(mine, 1), shift(mine, -1)
    far = swap(near, "x_lo", 1)
    users = [mine, up, down]
    hid, feat, w_in = in_vmem(
        hidden_kernel,
        "hidden",
        2 * (N + U) * E * H,
        [((N + U, H), BF), ((N + U, E), BF), ((E, H), BF)],
        neg_feat,
        pos_feat,
        w_in,
    )
    up, down = shift(after(up, hid), 1), shift(after(down, hid), -1)
    users += [up, down]
    near_emb, pemb, w_out = in_vmem(
        embed_kernel, "embed", 2 * (N + U) * E * H, [((N, E), BF), ((U, E), BF), ((H, E), BF)], hid, w_out
    )
    up, down = shift(after(up, near_emb), 1), shift(after(down, near_emb), -1)
    users += [up, down]
    far_hid, far_emb, nid, bias = in_vmem(
        far_kernel,
        "far",
        4 * N * E * H,
        [((N, H), BF), ((N, E), BF), ((NN, 128), F32), ((NN, 128), F32)],
        near,
        far,
        w_in,
        w_out,
        logq_table.reshape(8, 128),
    )
    users += [shift(after(up, far_emb), 1)]
    none = jnp.zeros((NZ, U), F32)
    ks = tuple(range(NZ))
    tloc, tot, pexp, kept_a = score(ks[:FIRST], near_emb, far_emb, nid, bias, pemb, none, none, users)
    tloc, tot, _, kept_b = score(ks[FIRST:], near_emb, far_emb, nid, bias, pemb, tloc, tot, users)
    tot = sum_over_z(tot, ((1, 6, 7), (2,)), F32)
    g = item_grads(tot, tloc, pexp, kept_a, kept_b, users)
    args = (tot, tloc, pexp, kept_a, kept_b, near_emb, far_emb, pemb)
    (send,), (keep, pterm) = user_grads(1, *args), user_grads(0, *args)
    args = (g, feat, far, w_out, hid, far_hid)
    theirs_g = backward(False, *args)
    half, other, user = all_reduce(backward(True, *args), theirs_g, keep, send)
    w_in_grad, w_out_grad = finish(False, other, *finish(True, half))
    return user + pterm, w_in_grad, w_out_grad


def solution(mesh):
    rows = P(AXES, None)
    ids = P(AXES)
    return jax.shard_map(
        on_device,
        mesh=Mesh(mesh.devices.reshape(SIZES), AXES),
        in_specs=(rows, rows, ids, rows, ids, ids, P(), P(), P()),
        out_specs=(rows, P(), P()),
        check_vma=False,
    )
```
